32 devices in a mesh: wide: 8 (over z, y), narrow: 4 (over x, core).
Axes of the slice: x: 2, y: 2, z: 4, core: 2. Of those that a mesh axis runs over, the one named last changes fastest.
Arguments:
- block_input: bfloat16 [16, 1024, 768], P('wide', 'narrow'), may hold values from -6 to 6
- norm1_gain: bfloat16 [768], replicated, may hold values from 0.5 to 1.5
- query_weight: bfloat16 [768, 768], replicated, may hold values from -0.21875 to 0.21875
- key_weight: bfloat16 [768, 768], replicated, may hold values from -0.21875 to 0.21875
- value_weight: bfloat16 [768, 768], replicated, may hold values from -0.21875 to 0.21875
- out_weight: bfloat16 [768, 768], replicated, may hold values from -3 to 3
- relative_bucket_bias: bfloat16 [32, 12], replicated, may hold values from -6 to 6
- norm2_gain: bfloat16 [768], replicated, may hold values from 0.5 to 1.5
- router_weight: bfloat16 [768, 16], replicated, may hold values from -0.109375 to 0.109375
- expert_in: bfloat16 [16, 768, 3072], P('wide', None, 'narrow'), may hold values from -0.21875 to 0.21875
- expert_out: bfloat16 [16, 3072, 768], P('wide', 'narrow'), may hold values from -2.5 to 2.5
- expert_index: int32 [16, 1024], P('wide', 'narrow'), may hold values from 0 to 15, as said below
- slot_index: int32 [16, 1024], P('wide', 'narrow'), may hold values from 0 to 40, as said below
- bucket_table: int32 [2048], replicated, may hold values from 0 to 31
- out_grad: bfloat16 [16, 1024, 768], P('wide', 'narrow'), may hold values from -6 to 6
Outputs:
- block_out: bfloat16 [16, 1024, 768], P('wide', 'narrow')
- input_grad: float32 [16, 1024, 768], P('wide', 'narrow')
- norm1_gain_grad: float32 [768], replicated
- query_grad: float32 [768, 768], replicated
- key_grad: float32 [768, 768], replicated
- value_grad: float32 [768, 768], replicated
- out_weight_grad: float32 [768, 768], replicated
- rel_bias_grad: float32 [32, 12], replicated
- norm2_gain_grad: float32 [768], replicated
- router_grad: float32 [768, 16], replicated
- expert_in_grad: float32 [16, 768, 3072], P('wide', None, 'narrow')
- expert_out_grad: float32 [16, 3072, 768], P('wide', 'narrow')
The draws below stay inside these ranges and needn't reach their ends.
Inputs may be any that keep to these rules, and one draw needn't show every extreme that they name: `expert_index`: every expert is the choice of some token. `slot_index`: the number of earlier tokens of the same group, in the group's order, whose expert is the same, or 40 where that number is 40 or more.
All inputs are finite; a program needn't handle non-finite values.
Results may differ from the reference program's by a relative error of at most 0.017.
Values may be sent and summed in bfloat16 or wider, within the bound.
No kernel may reach another device: no remote copies, remote signals or barrier semaphores. Data moves between devices by JAX's collectives and lax.ppermute only.
A program may use at most 256 MiB of HBM per device.

```python
from functools import partial
import jax
import jax.numpy as jnp
from jax import lax

D = 768
HEADS = 12
HD = 64
FF = 3072
NB = 32
SEQ = 1024
SEQ_GRP = 2
EXPERTS = 16
QLOC = 256
SEQS = 16
CAP = 40
N_WIDE = 8
N_NARROW = 4


def route_table(key):
    first_key, second_key, third_key, fourth_key, fifth_key = jax.random.split(key, 5)
    grid_shape = (SEQS, SEQ)
    uniform_pick = jax.random.randint(first_key, grid_shape, 0, EXPERTS)
    left_pick = jax.random.randint(second_key, grid_shape, 0, EXPERTS)
    right_pick = jax.random.randint(third_key, grid_shape, 0, EXPERTS)
    coin_flip = jax.random.randint(fourth_key, grid_shape, 0, 2)
    skewed = left_pick * right_pick // EXPERTS
    permuted = jax.random.permutation(fifth_key, EXPERTS).astype(jnp.int32)
    return jnp.take(permuted, jnp.where(coin_flip == 1, skewed, uniform_pick)).astype(jnp.int32)


def draw_expert_index(key, part):
    return route_table(key)


def draw_slot_index(key, part):
    chosen = route_table(key)
    per_device = SEQ // N_NARROW
    grouped = chosen.reshape(N_WIDE, SEQ_GRP, N_NARROW, per_device).transpose(0, 2, 1, 3).reshape(N_WIDE * N_NARROW, SEQ_GRP * per_device)
    matches = (grouped[:, :, None] == jnp.arange(EXPERTS, dtype=jnp.int32)[None, None, :]).astype(jnp.int32)
    earlier = jnp.cumsum(matches, axis=1) - matches
    slot_rows = jnp.minimum(jnp.sum(earlier * matches, axis=2), CAP)
    return slot_rows.reshape(N_WIDE, N_NARROW, SEQ_GRP, per_device).transpose(0, 2, 1, 3).reshape(SEQS, SEQ).astype(jnp.int32)


def set_ends(drawn, stream_key, low, largest):
    shape = drawn.shape
    place = [jax.random.randint(jax.random.fold_in(stream_key, axis), (), 0, shape[axis]) for axis in range(len(shape))]
    drawn = drawn.at[tuple(place)].set(low)
    longest = shape.index(max(shape))
    place[longest] = (place[longest] + 1) % shape[longest]
    return drawn.at[tuple(place)].set(largest)


def block_scale(key, dims, shards, low, high):
    def one(position, parts):
        heights = jax.random.uniform(jax.random.fold_in(jax.random.fold_in(key, 6), position), (parts,), jnp.float32, low / len(shards), high / len(shards))
        return jnp.repeat(jnp.exp(heights), dims[position] // parts).reshape((-1,) + (1,) * (len(dims) - position - 1))

    factor_of = one(*shards[0])
    for cut in shards[1:]:
        factor_of = factor_of * one(*cut)
    return factor_of


def gaussian(rng, dims, scale, most, shards=(), kind=jnp.bfloat16):
    loudness = block_scale(rng, dims, shards, -0.22, 0.18) if shards else 1.0
    values = jax.random.normal(rng, dims, jnp.float32) * scale * loudness
    return jnp.minimum(jnp.maximum(values, -most), most).astype(kind)


def setup_inputs(seed: int = 0) -> dict:
    key_of = jax.random.split(jax.random.key(seed), 16)
    block_input = gaussian(key_of[0], (SEQS, SEQ, D), 1.0, 6.0, ((0, 8), (1, 4)))
    norm1_gain = jnp.clip(1.0 + 0.1 * jax.random.normal(key_of[1], (D,), jnp.float32), 0.5, 1.5).astype(jnp.bfloat16)
    query_weight = gaussian(key_of[2], (D, D), D ** -0.5, 0.21875)
    key_weight = gaussian(key_of[3], (D, D), D ** -0.5, 0.21875)
    value_weight = gaussian(key_of[4], (D, D), D ** -0.5, 0.21875)
    out_weight = gaussian(key_of[5], (D, D), 4 ** -0.5, 3.0)
    relative_bucket_bias = gaussian(key_of[6], (NB, HEADS), 1.0, 6.0)
    norm2_gain = jnp.clip(1.0 + 0.1 * jax.random.normal(key_of[7], (D,), jnp.float32), 0.5, 1.5).astype(jnp.bfloat16)
    router_weight = gaussian(key_of[8], (D, EXPERTS), (4 * D) ** -0.5, 0.109375)
    expert_in = gaussian(key_of[9], (EXPERTS, D, FF), D ** -0.5, 0.21875, ((0, 8), (2, 4)))
    expert_out = gaussian(key_of[10], (EXPERTS, FF, D), (EXPERTS * 0.025), 2.5, ((0, 8), (1, 4)))
    expert_index = draw_expert_index(jax.random.fold_in(key_of[15], 71), 0)
    slot_index = draw_slot_index(jax.random.fold_in(key_of[15], 71), 0)
    bucket_table = set_ends(jax.random.randint(key_of[13], (2 * SEQ,), 0, NB), jax.random.fold_in(key_of[13], 1), 0, NB - 1).astype(jnp.int32)
    out_grad = gaussian(key_of[14], (SEQS, SEQ, D), 1.0, 6.0, ((0, 8), (1, 4)))
    return dict(block_input=block_input, norm1_gain=norm1_gain, query_weight=query_weight, key_weight=key_weight, value_weight=value_weight, out_weight=out_weight, relative_bucket_bias=relative_bucket_bias, norm2_gain=norm2_gain, router_weight=router_weight, expert_in=expert_in, expert_out=expert_out, expert_index=expert_index, slot_index=slot_index, bucket_table=bucket_table, out_grad=out_grad)


exact_mode = lax.Precision.HIGHEST
epsilon = 1e-06

@jax.custom_vjp
def low(v):
    return lax.optimization_barrier(v.astype(jnp.bfloat16)).astype(jnp.float32)

@jax.custom_vjp
def low_back(v):
    return v

def low_keep(v):
    return (low(v), None)

def low_pass(kept, grad):
    return (grad,)

def back_keep(v):
    return (v, None)

def back_low(kept, grad):
    return (low(grad),)
low.defvjp(low_keep, low_pass)
low_back.defvjp(back_keep, back_low)

def unit_rows(values, gain_values):
    return values * lax.rsqrt(lax.optimization_barrier(jnp.mean(values * values, axis=-1, keepdims=True)) + epsilon) * gain_values

def matmul(left_side, right_side):
    return jnp.dot(left_side, right_side, precision=exact_mode)

def attend_one(position_score_bias, packed):
    queries, keys_in, values_in = packed
    query_heads = queries.reshape(SEQ, HEADS, HD)
    key_heads = keys_in.reshape(SEQ, HEADS, HD)
    value_heads = values_in.reshape(SEQ, HEADS, HD)
    scores = jnp.einsum('ihd,jhd->hij', query_heads, key_heads, precision=exact_mode) * HD ** (-0.5) + position_score_bias
    scores = low_back(scores)
    weights = low(jax.nn.softmax(scores, axis=-1))
    return jnp.einsum('hij,jhd->ihd', weights, value_heads, precision=exact_mode).reshape(SEQ, D)

def expert_apply(packed):
    rows_in, first_matrix, second_matrix = packed
    pre_act = low_back(matmul(rows_in, first_matrix))
    return matmul(low(jax.nn.gelu(pre_act)), second_matrix)

def forward(block_input, norm1_gain, query_weight, key_weight, value_weight, out_weight, relative_bucket_bias, norm2_gain, router_weight, expert_in, expert_out, chosen, placed, block_ids, bucket_index):
    inputs = block_input.reshape(SEQS * SEQ, D)
    normed_one = low(unit_rows(inputs, norm1_gain))
    queries = low_back(low(matmul(normed_one, query_weight)))
    keys_all = low_back(low(matmul(normed_one, key_weight)))
    values_all = low_back(low(matmul(normed_one, value_weight)))
    position_score_bias = jnp.transpose(relative_bucket_bias[bucket_index], (2, 0, 1))
    attended = lax.map(jax.checkpoint(partial(attend_one, position_score_bias)), (queries.reshape(SEQS, SEQ, D), keys_all.reshape(SEQS, SEQ, D), values_all.reshape(SEQS, SEQ, D)))
    attended = low_back(low(attended.reshape(SEQS * SEQ, D)))
    residual = inputs + low_back(matmul(attended, out_weight))
    normed_two = low(unit_rows(residual, norm2_gain))
    logits = low_back(matmul(normed_two, router_weight))
    router_probs = jax.nn.softmax(logits, axis=-1)
    gate_prob = jnp.take_along_axis(router_probs, chosen[:, None], axis=-1)[:, 0]
    kept_mask = placed < CAP
    slot_place = jnp.where(kept_mask, placed, CAP)
    bucket_table_input = jnp.zeros((EXPERTS, N_WIDE * N_NARROW, CAP + 1, D), jnp.float32).at[chosen, block_ids, slot_place].add(normed_two)
    routed = low_back(bucket_table_input[:, :, :CAP].reshape(EXPERTS, N_WIDE * N_NARROW * CAP, D))
    produced = lax.map(jax.checkpoint(expert_apply), (routed, expert_in, expert_out))
    produced = low_back(low(produced)).reshape(EXPERTS, N_WIDE * N_NARROW, CAP, D)
    fetched = produced[chosen, block_ids, jnp.minimum(placed, CAP - 1)]
    gate_kept = jnp.where(kept_mask, gate_prob, jnp.zeros_like(gate_prob))
    return residual + gate_kept[:, None] * fetched

def reference(block_input, norm1_gain, query_weight, key_weight, value_weight, out_weight, relative_bucket_bias, norm2_gain, router_weight, expert_in, expert_out, expert_index, slot_index, bucket_table, out_grad):
    chosen = expert_index.reshape(SEQS * SEQ).astype(jnp.int32)
    placed = slot_index.reshape(SEQS * SEQ).astype(jnp.int32)
    token_ids = jnp.arange(SEQS * SEQ, dtype=jnp.int32)
    block_ids = token_ids // SEQ // SEQ_GRP * N_NARROW + token_ids % SEQ // QLOC
    positions = jnp.arange(SEQ, dtype=jnp.int32)
    bucket_index = bucket_table[positions[:, None] - positions[None, :] + SEQ]
    weights_in = (block_input, norm1_gain, query_weight, key_weight, value_weight, out_weight, relative_bucket_bias, norm2_gain, router_weight, expert_in, expert_out)
    floats_in = tuple((array_in.astype(jnp.float32) for array_in in weights_in))

    def forward_fn(*params):
        return forward(*params, chosen, placed, block_ids, bucket_index)
    result, pullback = jax.vjp(forward_fn, *floats_in)
    gradients = pullback(out_grad.astype(jnp.float32).reshape(SEQS * SEQ, D))
    return (result.astype(jnp.bfloat16).reshape(SEQS, SEQ, D), gradients[0].reshape(SEQS, SEQ, D), gradients[1], gradients[2], gradients[3], gradients[4], gradients[5], gradients[6], gradients[7], gradients[8], gradients[9], gradients[10])
```

```python
import functools

import jax
import jax.numpy as jnp
from jax import lax
from jax.experimental import pallas as pl
from jax.experimental.pallas import tpu as pltpu
from jax.sharding import PartitionSpec as P

epsilon = 1e-06
bf16 = jnp.bfloat16
f32 = jnp.float32
vmem_bytes = 60 * 1024 * 1024


def swap(values, axis, bits):
    count = lax.axis_size(axis)
    return lax.ppermute(values, axis, [(j, j ^ bits) for j in range(count)])


def gather_narrow(values):
    near = swap(values, "narrow", 1)
    far = swap(values, "narrow", 2)
    return [values, near, far, swap(far, "narrow", 1)]


def scatter_narrow(pieces):
    near_one = swap(pieces[1], "narrow", 1)
    near_three = swap(pieces[3], "narrow", 1)
    crossing = (pieces[2].astype(f32) + near_three.astype(f32)).astype(bf16)
    far = swap(crossing, "narrow", 2)
    return pieces[0].astype(f32) + near_one.astype(f32) + far.astype(f32)


def exchange_narrow(pieces):
    return [pieces[0]] + [swap(pieces[i], "narrow", i) for i in (1, 2, 3)]


def to_owners(values):
    return lax.all_to_all(values, "wide", split_axis=0, concat_axis=0, tiled=True)


def sum_over_wide(block):
    rows, width = block.shape
    count = lax.axis_size("wide")
    unit = count * 8 if count <= 8 else count
    padded = -(-rows // unit) * unit
    if padded != rows:
        block = jnp.pad(block, ((0, padded - rows), (0, 0)))
    parts = to_owners(block.reshape(count, padded // count, width))
    mine = jnp.sum(parts.astype(f32), axis=0).astype(bf16)
    whole = to_owners(jnp.broadcast_to(mine[None], (count,) + mine.shape))
    return whole.reshape(padded, width)


def wide_bits():
    bits = [1]
    while bits[-1] * 2 < lax.axis_size("wide"):
        bits.append(bits[-1] * 2)
    return bits[:1] + bits[:0:-1]


def sum_by_halves(block, small=None):
    mine = lax.axis_index("wide")
    bits = wide_bits()
    for bit in bits:
        upper = (mine & bit) > 0
        low, high = jnp.split(block, 2, axis=0)
        got = swap(jnp.where(upper, low, high), "wide", bit)
        if small is not None:
            small = small + swap(small, "wide", bit)
        block = (jnp.where(upper, high, low).astype(f32) + got.astype(f32)).astype(bf16)
    for bit in bits[::-1]:
        upper = (mine & bit) > 0
        got = swap(block, "wide", bit)
        block = jnp.concatenate([jnp.where(upper, got, block), jnp.where(upper, block, got)], axis=0)
    return block, small


def by_difference(values):
    count = values.shape[0]
    mine = lax.axis_index("wide")
    bit = 1
    while bit < count:
        shaped = values.reshape((count // (2 * bit), 2, bit) + values.shape[1:])
        values = jnp.where((mine & bit) > 0, shaped[:, ::-1], shaped).reshape(values.shape)
        bit *= 2
    return values


def exchange_wide(chunks):
    count = len(chunks)
    if count > 8:
        stacked = by_difference(to_owners(by_difference(jnp.stack(chunks, axis=0))))
        return [stacked[i] for i in range(count)]
    got = {0: chunks[0]}
    for i in list(range(count // 2, count)) + list(range(1, count // 2)):
        got[i] = swap(chunks[i], "wide", i)
    return [got[i] for i in range(count)]


def partner_groups(count):
    return [
        list(range(0, count // 2)),
        list(range(count // 2, 3 * count // 4)),
        list(range(3 * count // 4, count)),
    ]


def dot(left, right, dims=((1,), (0,))):
    return lax.dot_general(left, right, (dims, ((), ())), preferred_element_type=f32)


def forward_kernel(
    rank_ref, x0, x1, x2, x3, gain_ref, weight_ref, bias_ref, *rest, rows, first
):
    if not first:
        rest = rest[5:]
    normed_ref, qkv_ref, raised_ref, inverse_ref, out_ref, p0, p1, p2, p3, q_ref, v_ref, base_ref = rest
    rank = rank_ref[0]
    length = 4 * rows
    span = bias_ref.shape[-1]

    @pl.when(pl.program_id(0) == 0)
    def _():
        for i, x_ref in enumerate((x0, x1, x2, x3)):
            x = x_ref[...].astype(f32)
            scale = lax.rsqrt(jnp.mean(x * x, axis=-1, keepdims=True) + epsilon)
            place = pl.multiple_of((rank ^ i) * rows, rows)
            normed_ref[0, pl.ds(place, rows), :] = (x * scale * gain_ref[...]).astype(bf16)

    head = qkv_ref.shape[3]
    qkv = dot(weight_ref[0], normed_ref[0], ((1,), (1,)))
    queries = qkv[:head] * (head ** -0.5)
    q_ref[...] = queries.T.astype(bf16)
    v_ref[...] = qkv[2 * head :].T.astype(bf16)
    qkv_ref[0, 0, 0] = queries.astype(bf16)
    qkv_ref[0, 0, 1] = qkv[head : 2 * head].astype(bf16)
    qkv_ref[0, 0, 2] = qkv[2 * head :].astype(bf16)
    base_ref[...] = pltpu.roll(
        jnp.broadcast_to(bias_ref[0], (128, span)), 0, axis=1, stride=1, stride_axis=0
    )
    keys = qkv_ref[0, 0, 1]
    values = v_ref[...]
    top = length - 128
    step = 256
    for b in range(length // step):
        scores = dot(q_ref[b * step : (b + 1) * step, :], keys)
        bias = jnp.concatenate(
            [
                base_ref[:, top - b * step - k * 128 : top - b * step - k * 128 + length]
                for k in range(step // 128)
            ],
            axis=0,
        )
        scores = scores + bias
        raised = jnp.exp(scores - jnp.max(scores, axis=1, keepdims=True))
        inverse = 1.0 / jnp.sum(raised, axis=1, keepdims=True)
        raised = raised.astype(bf16)
        raised_ref[0, 0, b * step : (b + 1) * step, :] = raised
        attended = dot(raised, values) * inverse
        out_ref[0, 0, :, b * step : (b + 1) * step] = attended.T.astype(bf16)
        inverse_ref[0, 0, :, b * step : (b + 1) * step] = jnp.broadcast_to(inverse, (step, 128)).T[:8]
    for i, p_ref in enumerate((p0, p1, p2, p3)):
        p_ref[...] = out_ref[0, 0, :, pl.ds(pl.multiple_of((rank ^ i) * rows, rows), rows)]


def attend(rank, blocks, gain, weights, bias_rows, previous, seq, groups):
    rows, width = blocks[0].shape
    heads, three, _ = weights.shape
    head = three // 3
    length = 4 * rows
    span = bias_rows.shape[-1]
    first = previous is None
    whole = lambda h, r: (0, 0)
    in_specs = [pl.BlockSpec((rows, width), whole)] * 4 + [
        pl.BlockSpec((1, width), whole),
        pl.BlockSpec((1, three, width), lambda h, r: (h, 0, 0)),
        pl.BlockSpec((1, 1, span), lambda h, r: (h, 0, 0)),
    ]
    args = list(blocks) + [gain, weights, bias_rows]
    aliases = {}
    if not first:
        aliases = {1 + len(args) + k: k for k in range(5)}
        in_specs = in_specs + [pl.BlockSpec(memory_space=pl.ANY)] * 5
        args = args + list(previous)
    out_shape = [
        jax.ShapeDtypeStruct((groups, length, width), bf16),
        jax.ShapeDtypeStruct((groups, heads, 3, head, length), bf16),
        jax.ShapeDtypeStruct((groups, heads, length, length), bf16),
        jax.ShapeDtypeStruct((groups, heads, 8, length), f32),
        jax.ShapeDtypeStruct((groups, heads, head, length), bf16),
    ] + [jax.ShapeDtypeStruct((heads * head, rows), bf16)] * 4
    out_specs = [
        pl.BlockSpec((1, length, width), lambda h, r: (seq, 0, 0)),
        pl.BlockSpec((1, 1, 3, head, length), lambda h, r: (seq, h, 0, 0, 0)),
        pl.BlockSpec((1, 1, length, length), lambda h, r: (seq, h, 0, 0)),
        pl.BlockSpec((1, 1, 8, length), lambda h, r: (seq, h, 0, 0)),
        pl.BlockSpec((1, 1, head, length), lambda h, r: (seq, h, 0, 0)),
    ] + [pl.BlockSpec((head, rows), lambda h, r: (h, 0))] * 4
    outs = pl.pallas_call(
        functools.partial(forward_kernel, rows=rows, first=first),
        grid_spec=pltpu.PrefetchScalarGridSpec(
            num_scalar_prefetch=1,
            grid=(heads,),
            in_specs=in_specs,
            out_specs=out_specs,
            scratch_shapes=[
                pltpu.VMEM((length, head), bf16),
                pltpu.VMEM((length, head), bf16),
                pltpu.VMEM((128, span), f32),
            ],
        ),
        out_shape=out_shape,
        input_output_aliases=aliases,
        compiler_params=pltpu.CompilerParams(vmem_limit_bytes=vmem_bytes),
        cost_estimate=pl.CostEstimate(
            flops=8 * heads * length * length * 256, bytes_accessed=20_000_000, transcendentals=0
        ),
        name="attention_forward",
    )(rank, *args)
    return outs[:5], outs[5:]


def backward_kernel(
    rank_ref, g0, g1, g2, g3, qkv_ref, raised_ref, inverse_ref, out_ref, normed_ref,
    d0, d1, d2, d3, weight_grad_ref, bias_ref,
    grad_ref, left_ref, right_ref, key_ref, scores_ref, packed_ref, total_ref, offsets_ref, *, rows
):
    rank = rank_ref[0]
    length = 4 * rows
    head = grad_ref.shape[0]
    step_id = pl.program_id(0)
    for i, g_ref in enumerate((g0, g1, g2, g3)):
        grad_ref[:, pl.ds(pl.multiple_of((rank ^ i) * rows, rows), rows)] = g_ref[...].astype(f32)
    scaled = grad_ref[...] * inverse_ref[0, 0, 0:1, :]
    shift = jnp.sum(scaled * out_ref[0, 0].astype(f32), axis=0, keepdims=True)
    high = shift.astype(bf16).astype(f32)
    scaled_low = scaled.astype(bf16)
    tail = jnp.concatenate(
        [high, shift - high, jnp.zeros((128 - head - 2, length), f32)], axis=0
    )
    left_ref[...] = jnp.concatenate([scaled_low.astype(f32), tail], axis=0).T.astype(bf16)
    right_ref[0:head, :] = qkv_ref[0, 0, 2]
    right_ref[head:, :] = jnp.where(
        lax.broadcasted_iota(jnp.int32, (128 - head, length), 0) < 2, -1.0, 0.0
    ).astype(bf16)
    key_ref[...] = qkv_ref[0, 0, 1].astype(f32).T.astype(bf16)

    @pl.when(step_id == 0)
    def _():
        offsets_ref[...] = jnp.zeros_like(offsets_ref)
        total_ref[...] = jnp.zeros_like(total_ref)

    top = length - 128
    step = 256
    for b in range(length // step):
        inner = dot(left_ref[b * step : (b + 1) * step, :], right_ref[...])
        grads = raised_ref[0, 0, b * step : (b + 1) * step, :].astype(f32) * inner
        for k in range(step // 128):
            place = top - b * step - k * 128
            offsets_ref[:, place : place + length] += grads[k * 128 : (k + 1) * 128]
        scores_ref[b * step : (b + 1) * step, :] = grads.astype(bf16)
    packed_ref[0:head, :] = (dot(scores_ref[...], key_ref[...]) * (head ** -0.5)).T.astype(bf16)
    packed_ref[head : 2 * head, :] = dot(qkv_ref[0, 0, 0], scores_ref[...]).astype(bf16)
    packed_ref[2 * head :, :] = dot(scaled_low, raised_ref[0, 0]).astype(bf16)
    for i, d_ref in enumerate((d0, d1, d2, d3)):
        d_ref[...] = packed_ref[:, pl.ds(pl.multiple_of((rank ^ i) * rows, rows), rows)]
    total_ref[...] += dot(packed_ref[...], normed_ref[0])

    @pl.when(step_id == pl.num_programs(0) - 1)
    def _():
        weight_grad_ref[...] = total_ref[...].astype(bf16)
        span = offsets_ref.shape[1]
        folded = offsets_ref[...]
        half = 64
        while half >= 1:
            folded = folded[:half] + pltpu.roll(folded[half : 2 * half], span - half, axis=1)
            half //= 2
        bias_ref[...] = jnp.broadcast_to(folded, bias_ref.shape)


def attend_back(rank, grads, saved, head_index):
    normed, qkv, raised, inverse, out = saved
    groups, length, width = normed.shape
    _, heads, _, head, _ = qkv.shape
    rows = length // 4
    span = 2 * length
    h = head_index
    in_specs = [pl.BlockSpec((head, rows), lambda s, r: (h, s))] * 4 + [
        pl.BlockSpec((1, 1, 3, head, length), lambda s, r: (s, h, 0, 0, 0)),
        pl.BlockSpec((1, 1, length, length), lambda s, r: (s, h, 0, 0)),
        pl.BlockSpec((1, 1, 8, length), lambda s, r: (s, h, 0, 0)),
        pl.BlockSpec((1, 1, head, length), lambda s, r: (s, h, 0, 0)),
        pl.BlockSpec((1, length, width), lambda s, r: (s, 0, 0)),
    ]
    out_shape = [jax.ShapeDtypeStruct((3 * head, groups * rows), bf16)] * 4 + [
        jax.ShapeDtypeStruct((3 * head, width), bf16),
        jax.ShapeDtypeStruct((8, span), f32),
    ]
    out_specs = [pl.BlockSpec((3 * head, rows), lambda s, r: (0, s))] * 4 + [
        pl.BlockSpec((3 * head, width), lambda s, r: (0, 0)),
        pl.BlockSpec((8, span), lambda s, r: (0, 0)),
    ]
    outs = pl.pallas_call(
        functools.partial(backward_kernel, rows=rows),
        grid_spec=pltpu.PrefetchScalarGridSpec(
            num_scalar_prefetch=1,
            grid=(groups,),
            in_specs=in_specs,
            out_specs=out_specs,
            scratch_shapes=[
                pltpu.VMEM((head, length), f32),
                pltpu.VMEM((length, 128), bf16),
                pltpu.VMEM((128, length), bf16),
                pltpu.VMEM((length, head), bf16),
                pltpu.VMEM((length, length), bf16),
                pltpu.VMEM((3 * head, length), bf16),
                pltpu.VMEM((3 * head, width), f32),
                pltpu.VMEM((128, span), f32),
            ],
        ),
        out_shape=out_shape,
        compiler_params=pltpu.CompilerParams(vmem_limit_bytes=vmem_bytes),
        cost_estimate=pl.CostEstimate(
            flops=8 * groups * length * length * 256, bytes_accessed=10_000_000, transcendentals=0
        ),
        name="attention_backward",
    )(rank, *grads, qkv, raised, inverse, out, normed)
    return outs[:4], outs[4], outs[5][:1]


def turn_kernel(rank_ref, *refs, heads):
    blocks = refs[: 4 * heads]
    weight_refs = refs[4 * heads : 4 * heads + 3]
    gain_ref, q_ref, k_ref, v_ref, norm_ref, gathered_ref, total_ref = refs[4 * heads + 3 :]
    rank = rank_ref[0]
    step = pl.program_id(0)
    head = blocks[0].shape[0] // 3

    @pl.when(step == 0)
    def _():
        total_ref[...] = jnp.zeros_like(total_ref)
        for h in range(heads):
            for i in range(4):
                place = pl.multiple_of((rank ^ i) * (heads * head) + h * head, head)
                for c in range(3):
                    gathered_ref[c, pl.ds(place, head), :] = blocks[h * 4 + i][
                        c * head : (c + 1) * head, :
                    ].astype(f32)

    place = pl.multiple_of(step * 128, 128)
    for c, out_ref in enumerate((q_ref, k_ref, v_ref)):
        grads = gathered_ref[c, pl.ds(place, 128), :].T
        out_ref[...] = grads
        total_ref[...] += dot(
            jnp.ones((8, 128), f32), grads * weight_refs[c][...].astype(f32), ((1,), (1,))
        )

    @pl.when(step == pl.num_programs(0) - 1)
    def _():
        norm_ref[...] = total_ref[...] / gain_ref[...]


def turn(rank, blocks, weights, gain, heads):
    rows, width = blocks[0].shape
    column = pl.BlockSpec((width, 128), lambda s, r: (0, s))
    row = pl.BlockSpec((8, width), lambda s, r: (0, 0))
    return pl.pallas_call(
        functools.partial(turn_kernel, heads=heads),
        grid_spec=pltpu.PrefetchScalarGridSpec(
            num_scalar_prefetch=1,
            grid=(width // 128,),
            in_specs=[pl.BlockSpec((rows, width), lambda s, r: (0, 0))] * len(blocks)
            + [column] * 3
            + [pl.BlockSpec((1, width), lambda s, r: (0, 0))],
            out_specs=[column] * 3 + [row],
            scratch_shapes=[pltpu.VMEM((3, width, width), f32), pltpu.VMEM((8, width), f32)],
        ),
        out_shape=[jax.ShapeDtypeStruct((width, width), f32)] * 3
        + [jax.ShapeDtypeStruct((8, width), f32)],
        compiler_params=pltpu.CompilerParams(vmem_limit_bytes=vmem_bytes),
        name="weight_gradient_turn",
    )(rank, *blocks, *weights, gain)


def input_kernel(rank_ref, *refs, heads):
    pieces = refs[: 4 * heads]
    weight_refs = refs[4 * heads : 4 * heads + 3]
    x_ref, grad_ref, gain_ref, out_ref, gathered_ref = refs[4 * heads + 3 :]
    rank = rank_ref[0]
    head = pieces[0].shape[0] // 3
    for h in range(heads):
        for i in range(4):
            place = pl.multiple_of((rank ^ i) * (heads * head) + h * head, head)
            for c in range(3):
                gathered_ref[c, pl.ds(place, head), :] = pieces[h * 4 + i][
                    c * head : (c + 1) * head, :
                ]
    total = dot(gathered_ref[0], weight_refs[0][...], ((0,), (1,)))
    total += dot(gathered_ref[1], weight_refs[1][...], ((0,), (1,)))
    total += dot(gathered_ref[2], weight_refs[2][...], ((0,), (1,)))
    x = x_ref[...].astype(f32)
    scale = lax.rsqrt(jnp.mean(x * x, axis=-1, keepdims=True) + epsilon)
    unit = x * scale
    scaled = total * gain_ref[...]
    inner_mean = jnp.mean(scaled * unit, axis=-1, keepdims=True)
    out_ref[...] = grad_ref[...] + scale * (scaled - unit * inner_mean)


def input_gradient(rank, pieces, weights, inputs, residual_grad, gain, heads):
    tokens, width = inputs.shape
    half = tokens // 2
    rows = pieces[0].shape[0]
    whole = lambda s, r: (0, 0)
    part = pl.BlockSpec((half, width), lambda s, r: (s, 0))
    return pl.pallas_call(
        functools.partial(input_kernel, heads=heads),
        grid_spec=pltpu.PrefetchScalarGridSpec(
            num_scalar_prefetch=1,
            grid=(2,),
            in_specs=[pl.BlockSpec((rows, half), lambda s, r: (0, s))] * len(pieces)
            + [pl.BlockSpec((width, width), whole)] * 3
            + [part, part, pl.BlockSpec((1, width), whole)],
            out_specs=part,
            scratch_shapes=[pltpu.VMEM((3, width, half), bf16)],
        ),
        out_shape=jax.ShapeDtypeStruct((tokens, width), f32),
        compiler_params=pltpu.CompilerParams(vmem_limit_bytes=vmem_bytes),
        name="input_gradient",
    )(rank, *pieces, *weights, inputs, residual_grad, gain)


def expert_kernel(
    first_ref, xa, xb, ga, gb, into_ref, out_of_ref, router_ref,
    da, db, ya, yb, aa, ab, ba, bb, *, experts
):
    expert = first_ref[0] + pl.program_id(0)
    half = xa.shape[0]
    width = xa.shape[1]
    rows = jnp.concatenate([xa[...], xb[...]], axis=0)
    grads = jnp.concatenate([ga[...], gb[...]], axis=0)
    logits = dot(rows, router_ref[...])
    lanes = lax.broadcasted_iota(jnp.int32, logits.shape, 1)
    logits = jnp.where(lanes < experts, logits, -1e30)
    raised = jnp.exp(logits - jnp.max(logits, axis=1, keepdims=True))
    picked = jnp.sum(jnp.where(lanes == expert, raised, 0.0), axis=1, keepdims=True)
    gate = picked / jnp.sum(raised, axis=1, keepdims=True)

    before = dot(rows, into_ref[0])
    hidden = dot(grads, out_of_ref[0], ((1,), (1,)))
    square = before * before
    bend = 0.5 + 0.5 * jnp.tanh(before * (0.7978845608 + (0.7978845608 * 0.044715) * square))
    active = before * bend
    slope = 2.0 * 0.7978845608 + (6.0 * 0.7978845608 * 0.044715) * square
    back = hidden * (bend + active * (1.0 - bend) * slope)
    gate_part = jnp.sum(active * hidden, axis=1, keepdims=True)
    row_part = dot(back.astype(bf16), into_ref[0], ((1,), (1,)))
    extra = jnp.where(
        lax.broadcasted_iota(jnp.int32, (2 * half, 128), 1) == 0, gate_part, 0.0
    ).astype(bf16)
    row_part = row_part.astype(bf16)
    gated = (gate * active).astype(bf16)
    produced = dot(gated, out_of_ref[0]).astype(bf16)
    gated_back = (gate * back).astype(bf16)
    for k, (d, y, a, b) in enumerate(((da, ya, aa, ba), (db, yb, ab, bb))):
        part = slice(k * half, (k + 1) * half)
        d[:, :width] = row_part[part]
        d[:, width:] = extra[part]
        y[...] = produced[part]
        a[...] = gated[part]
        b[...] = gated_back[part]


def run_experts(first, rows, grads, into, out_of, router, experts):
    count, width = rows[0].shape
    owned, _, hidden = into.shape
    half = count // owned
    block = lambda lanes: pl.BlockSpec((half, lanes), lambda e, f: (e, 0))
    matrix = lambda e, f: (e, 0, 0)
    shape = lambda lanes: jax.ShapeDtypeStruct((count, lanes), bf16)
    outs = pl.pallas_call(
        functools.partial(expert_kernel, experts=experts),
        grid_spec=pltpu.PrefetchScalarGridSpec(
            num_scalar_prefetch=1,
            grid=(owned,),
            in_specs=[block(width)] * 4
            + [
                pl.BlockSpec((1, width, hidden), matrix),
                pl.BlockSpec((1, hidden, width), matrix),
                pl.BlockSpec(router.shape, lambda e, f: (0, 0)),
            ],
            out_specs=[block(width + 128)] * 2 + [block(width)] * 2 + [block(hidden)] * 4,
        ),
        out_shape=[shape(width + 128)] * 2 + [shape(width)] * 2 + [shape(hidden)] * 4,
        compiler_params=pltpu.CompilerParams(vmem_limit_bytes=vmem_bytes),
        cost_estimate=pl.CostEstimate(
            flops=8 * 2 * count * width * hidden, bytes_accessed=9_000_000, transcendentals=0
        ),
        name="experts",
    )(first, *rows, *grads, into, out_of, router)
    return outs[0:2], outs[2:4], outs[4:6], outs[6:8]


def expert_weight_kernel(*refs, count):
    rows, actives, backs = refs[:count], refs[count : 2 * count], refs[2 * count : 3 * count]
    grads = refs[3 * count : 4 * count]
    into_ref, out_of_ref = refs[4 * count :]
    whole = lambda parts: jnp.concatenate([p[...] for p in parts], axis=0)
    into_ref[0] = dot(whole(rows), whole(backs), ((0,), (0,)))
    out_of_ref[0] = dot(whole(actives), whole(grads), ((0,), (0,)))


def expert_weight_grads(rows, actives, backs, grads, owned, starts):
    flat = lambda nested: [nested[g][j] for j in range(4) for g in range(len(starts))]
    rows, actives, backs = flat(rows), flat(actives), flat(backs)
    width, hidden = rows[0].shape[1], actives[0].shape[1]
    sizes = [r.shape[0] // owned for r in rows]
    own = lambda size, lanes: pl.BlockSpec((size, lanes), lambda e: (e, 0))

    def shifted(size, start):
        return pl.BlockSpec((size, width), lambda e: (start // size + e, 0))

    spread = [(grads[j], starts[g]) for j in range(4) for g in range(len(starts))]
    return pl.pallas_call(
        functools.partial(expert_weight_kernel, count=len(rows)),
        grid=(owned,),
        in_specs=[own(n, width) for n in sizes]
        + [own(n, hidden) for n in sizes] * 2
        + [shifted(n, start) for n, (_, start) in zip(sizes, spread)],
        out_specs=[
            pl.BlockSpec((1, width, hidden), lambda e: (e, 0, 0)),
            pl.BlockSpec((1, hidden, width), lambda e: (e, 0, 0)),
        ],
        out_shape=[
            jax.ShapeDtypeStruct((owned, width, hidden), f32),
            jax.ShapeDtypeStruct((owned, hidden, width), f32),
        ],
        compiler_params=pltpu.CompilerParams(vmem_limit_bytes=vmem_bytes),
        cost_estimate=pl.CostEstimate(
            flops=8 * 1280 * 768 * 768, bytes_accessed=25_000_000, transcendentals=0
        ),
        name="expert_weight_gradients",
    )(*rows, *actives, *backs, *[g for g, _ in spread])


def on_device(
    block_input, norm1_gain, query_weight, key_weight, value_weight, out_weight,
    relative_bucket_bias, norm2_gain, router_weight, expert_in, expert_out,
    expert_index, slot_index, bucket_table, out_grad,
):
    groups, rows, width = block_input.shape
    tokens = groups * rows
    wide_count = lax.axis_size("wide")
    narrow_count = lax.axis_size("narrow")
    experts = router_weight.shape[1]
    owned = expert_in.shape[0]
    capacity = max(2, (5 * tokens + 4 * experts - 1) // (4 * experts))
    buckets, head_count = relative_bucket_bias.shape
    head = width // head_count
    heads = head_count // narrow_count
    columns = heads * head
    score_scale = head ** (-0.5)
    span = bucket_table.shape[0]
    rank = lax.axis_index("narrow")
    wide_rank = lax.axis_index("wide")
    rank_arg = rank.astype(jnp.int32).reshape(1)
    gain_one = norm1_gain.astype(f32).reshape(1, width)
    gain_two = norm2_gain.astype(f32)

    gathered = [gather_narrow(block_input[s]) for s in range(groups)]

    upstream_low = out_grad.reshape(tokens, width)
    chosen = expert_index.reshape(tokens)
    placed = slot_index.reshape(tokens)
    chunk = owned * capacity
    slots = wide_count * chunk
    slot_ids = jnp.arange(slots, dtype=jnp.int32)
    within = (chosen % owned) * capacity + placed
    kept = placed < capacity

    def slot_hot(owner):
        target = jnp.where(kept, owner * chunk + within, -1)
        return (target[None, :] == slot_ids[:, None]).astype(bf16)

    owner = chosen // owned
    dispatch = slot_hot(owner ^ wide_rank)
    dispatch_plain = slot_hot(owner)
    split = partner_groups(wide_count)

    def grouped(chunks, members):
        stacked = jnp.stack([chunks[i].reshape(owned, capacity, -1) for i in members], axis=1)
        return stacked.reshape(len(members) * chunk, -1)

    def ungrouped(values, members):
        shaped = values.reshape(owned, len(members), capacity, -1)
        return [shaped[:, m].reshape(chunk, -1) for m in range(len(members))]

    sent = dot(dispatch_plain, upstream_low).astype(bf16)
    arrived = by_difference(to_owners(sent.reshape(wide_count, chunk, width)))
    arrived = jnp.concatenate([grouped(arrived, members) for members in split], axis=0)
    grad_rows = gather_narrow(arrived)
    starts = [members[0] * chunk for members in split]

    def own_columns(matrix):
        part = lax.dynamic_slice_in_dim(matrix, rank * columns, columns, axis=1)
        return part.T.reshape(heads, head, width)

    own_weights = jnp.concatenate(
        [own_columns(m) for m in (query_weight, key_weight, value_weight)], axis=1
    )
    out_weight_own = [
        lax.dynamic_slice_in_dim(out_weight, (rank ^ i) * columns, columns, axis=0)
        for i in range(4)
    ]

    table_turned = jnp.roll(bucket_table[::-1], -127)
    bucket_hot = (
        table_turned[None, :] == jnp.arange(buckets, dtype=jnp.int32)[:, None]
    ).astype(bf16)
    own_bias = lax.dynamic_slice_in_dim(relative_bucket_bias.T, rank * heads, heads, axis=0)
    bias_rows = dot(own_bias, bucket_hot).reshape(heads, 1, span)

    saved = None
    pieces = []
    for s in range(groups):
        saved, piece = attend(
            rank_arg, gathered[s], gain_one, own_weights, bias_rows, saved, s, groups
        )
        pieces.append(exchange_narrow(piece))
    attended = [
        jnp.concatenate([pieces[s][i] for s in range(groups)], axis=1) for i in range(4)
    ]

    inputs = block_input.reshape(tokens, width)
    residual = inputs.astype(f32)
    for i in range(4):
        residual = residual + dot(attended[i], out_weight_own[i], ((0,), (0,)))
    scale_two = lax.rsqrt(jnp.mean(residual * residual, axis=-1, keepdims=True) + epsilon)
    unit_two = residual * scale_two
    normed_two = (unit_two * gain_two).astype(bf16)

    sent = dot(dispatch, normed_two).astype(bf16)
    chunks = exchange_wide([sent[i * chunk : (i + 1) * chunk] for i in range(wide_count)])
    lanes = -(-experts // 128) * 128
    router_wide = jnp.pad(router_weight, ((0, 0), (0, lanes - experts)))
    first_expert = (wide_rank * owned).astype(jnp.int32).reshape(1)
    expert_rows, expert_outs, actives, backs = [], [], [], []
    returned = [None] * wide_count
    for g, members in enumerate(split):
        rows_in = gather_narrow(grouped(chunks, members))
        count = rows_in[0].shape[0]
        grads_in = [v[starts[g] : starts[g] + count] for v in grad_rows]
        near = run_experts(
            first_expert, rows_in[:2], grads_in[:2], expert_in, expert_out, router_wide, experts
        )
        far = run_experts(
            first_expert, rows_in[2:], grads_in[2:], expert_in, expert_out, router_wide, experts
        )
        back, forth, active, bent = [list(n) + list(f) for n, f in zip(near, far)]
        expert_rows.append(rows_in)
        expert_outs.append(forth)
        actives.append(active)
        backs.append(bent)
        whole = scatter_narrow(back).astype(bf16)
        for i, part in zip(members, ungrouped(whole, members)):
            returned[i] = part
    returned = jnp.concatenate(exchange_wide(returned), axis=0)

    logits = dot(normed_two, router_weight)
    probs = jax.nn.softmax(logits, axis=-1)
    picked = (chosen[:, None] == jnp.arange(experts, dtype=jnp.int32)[None, :]).astype(f32)
    gate = jnp.sum(probs * picked, axis=-1)

    upstream = upstream_low.astype(f32)
    back_rows = dot(dispatch, returned, ((0,), (0,)))
    row_grad, gate_grad = back_rows[:, :width], back_rows[:, width]
    logit_grad = (probs * gate_grad[:, None] * (picked - gate[:, None])).astype(bf16)
    normed_two_grad = dot(logit_grad, router_weight, ((1,), (1,))) + gate[:, None] * row_grad
    router_part = dot(logit_grad, normed_two, ((0,), (0,)))
    norm2_part = jnp.sum(normed_two_grad * unit_two, axis=0)
    scaled = normed_two_grad * gain_two
    inner_mean = jnp.mean(scaled * unit_two, axis=-1, keepdims=True)
    residual_grad = upstream + scale_two * (scaled - unit_two * inner_mean)
    branch_grad = residual_grad.astype(bf16)

    grads = exchange_narrow(
        [dot(w, branch_grad, ((1,), (1,))).astype(bf16) for w in out_weight_own]
    )
    extra = jnp.concatenate([router_part, norm2_part[None]], axis=0).astype(bf16)
    out_sum = scatter_narrow(
        [
            jnp.concatenate([dot(attended[i], branch_grad).astype(bf16), extra], axis=0)
            for i in range(4)
        ]
    ).astype(bf16)
    out_total = sum_over_wide(out_sum)
    out_blocks = gather_narrow(out_total[:columns])

    bias_parts = []
    weight_parts = []
    mine = []
    for h in range(heads):
        packed, weight_part, bias_part = attend_back(rank_arg, grads, saved, h)
        bias_parts.append(bias_part)
        weight_parts.append(weight_part)
        mine += exchange_narrow(packed)
    bias_sum = jnp.einsum(
        "hm,nm->hn",
        jnp.concatenate(bias_parts, axis=0),
        bucket_hot.astype(f32),
        precision=lax.Precision.HIGHEST,
    )
    bias_sum = jnp.pad(bias_sum, ((0, 8 - heads), (0, 128 - buckets)))
    early, _ = sum_by_halves(jnp.concatenate(weight_parts[: heads - 1], axis=0))
    late, bias_sum = sum_by_halves(weight_parts[-1], bias_sum)
    early = gather_narrow(early)
    late = gather_narrow(late)
    bias_all = jnp.stack(gather_narrow(bias_sum), axis=0)
    turned_blocks = [
        early[i][h * 3 * head : (h + 1) * 3 * head] for h in range(heads - 1) for i in range(4)
    ] + late

    def by_rank(stacked):
        return jnp.stack(
            [lax.dynamic_index_in_dim(stacked, rank ^ j, axis=0, keepdims=False) for j in range(4)],
            axis=0,
        )

    rel_bias_grad = by_rank(bias_all)[:, :heads, :buckets].reshape(head_count, buckets).T

    weights = (query_weight, key_weight, value_weight)
    input_grad = input_gradient(rank_arg, mine, weights, inputs, residual_grad, gain_one, heads)

    in_grads, out_grads = expert_weight_grads(
        expert_rows, actives, backs, grad_rows, owned, starts
    )
    whole = scatter_narrow(
        [jnp.concatenate([expert_outs[g][j] for g in range(len(split))], axis=0) for j in range(4)]
    ).astype(bf16)
    parts = []
    for g, members in enumerate(split):
        size = len(members) * chunk
        parts += ungrouped(whole[starts[g] : starts[g] + size], members)
    fetched = to_owners(by_difference(jnp.stack(parts, axis=0))).reshape(slots, width)
    block_out = (residual + dot(dispatch_plain, fetched, ((0,), (0,)))).astype(bf16)

    query_grad, key_grad, value_grad, norm1_grad = turn(
        rank_arg, turned_blocks, weights, gain_one, heads
    )
    out_weight_grad = by_rank(jnp.stack(out_blocks, axis=0)).reshape(width, width).astype(f32)
    router_grad = out_total[columns : columns + experts].astype(f32).T
    norm2_grad = out_total[columns + experts].astype(f32)

    return (
        block_out.reshape(groups, rows, width),
        input_grad.reshape(groups, rows, width),
        norm1_grad[0],
        query_grad,
        key_grad,
        value_grad,
        out_weight_grad,
        rel_bias_grad,
        norm2_grad,
        router_grad,
        in_grads,
        out_grads,
    )


def solution(mesh):
    rows = P("wide", "narrow", None)
    into, out_of = P("wide", None, "narrow"), P("wide", "narrow", None)
    return jax.shard_map(
        on_device,
        mesh=mesh,
        in_specs=(rows,) + (P(),) * 8 + (into, out_of, P("wide", "narrow"), P("wide", "narrow"), P(), rows),
        out_specs=(rows, rows) + (P(),) * 8 + (into, out_of),
        check_vma=False,
    )
```

```python
import functools

import jax
import jax.numpy as jnp
from jax import lax
from jax.experimental import pallas as pl
from jax.experimental.pallas import tpu as pltpu
from jax.sharding import PartitionSpec as P

epsilon = 1e-06
bf16 = jnp.bfloat16
f32 = jnp.float32
vmem_bytes = 60 * 1024 * 1024


def swap(values, axis, bits):
    count = lax.axis_size(axis)
    return lax.ppermute(values, axis, [(j, j ^ bits) for j in range(count)])


def tie(values, *others):
    return list(lax.optimization_barrier((tuple(values), tuple(others)))[0])


def gather_narrow(values, *holds):
    near = swap(values, "narrow", 1)
    far = swap(values, "narrow", 2)
    held = tie([far], *holds)[0] if holds else far
    return [values, near, far, swap(held, "narrow", 1)]


def scatter_begin(pieces):
    near_one = swap(pieces[1], "narrow", 1)
    near_three = swap(pieces[3], "narrow", 1)
    crossing = (pieces[2].astype(f32) + near_three.astype(f32)).astype(bf16)
    return pieces[0], near_one, crossing


def scatter_end(own, near_one, crossing):
    far = swap(crossing, "narrow", 2)
    return (own.astype(f32) + near_one.astype(f32) + far.astype(f32)).astype(bf16)


def exchange_narrow(pieces):
    return [pieces[0]] + [swap(pieces[i], "narrow", i) for i in (1, 2, 3)]


def to_owners(values):
    return lax.all_to_all(values, "wide", split_axis=0, concat_axis=0, tiled=True)


def wide_bits():
    bits = [1]
    while bits[-1] * 2 < lax.axis_size("wide"):
        bits.append(bits[-1] * 2)
    return bits[:1] + bits[:0:-1]


def halve(block, bit):
    upper = (lax.axis_index("wide") & bit) > 0
    low, high = jnp.split(block, 2, axis=0)
    got = swap(jnp.where(upper, low, high), "wide", bit)
    return (jnp.where(upper, high, low).astype(f32) + got.astype(f32)).astype(bf16)


def double(block, bit):
    upper = (lax.axis_index("wide") & bit) > 0
    got = swap(block, "wide", bit)
    return jnp.concatenate([jnp.where(upper, got, block), jnp.where(upper, block, got)], axis=0)


class Sum:
    def __init__(self, block):
        self.block = block
        bits = wide_bits()
        self.rounds = [(halve, b) for b in bits] + [(double, b) for b in bits[::-1]]

    def step(self, *others):
        if others:
            self.block = tie([self.block], *others)[0]
        if self.rounds:
            move, bit = self.rounds.pop(0)
            self.block = move(self.block, bit)
        return self.block

    def rest(self):
        while self.rounds:
            self.step()
        return self.block


def wide_parts(block):
    count = lax.axis_size("wide")
    rows, width = block.shape
    parts = to_owners(block.reshape(count, rows // count, width))
    return jnp.sum(parts.astype(f32), axis=0).astype(bf16)


def wide_whole(mine):
    count = lax.axis_size("wide")
    whole = to_owners(jnp.broadcast_to(mine[None], (count,) + mine.shape))
    return whole.reshape((count * mine.shape[0],) + mine.shape[1:])


def dot(left, right, dims=((1,), (0,))):
    return lax.dot_general(left, right, (dims, ((), ())), preferred_element_type=f32)


def forward_kernel(
    rank_ref, x0, x1, x2, x3, gain_ref, wq0, wk0, wv0, wq1, wk1, wv1, bias_ref, *rest, rows, heads, first
):
    if not first:
        rest = rest[5:]
    normed_ref, qkv_ref, raised_ref, inverse_ref, out_ref, p0, p1, p2, p3 = rest[:9]
    q_ref, v_ref, base_ref, wide_ref = rest[9:]
    rank = rank_ref[0]
    length = 4 * rows
    span = bias_ref.shape[-1]

    @pl.when(pl.program_id(0) == 0)
    def _():
        for i, x_ref in enumerate((x0, x1, x2, x3)):
            x = x_ref[...].astype(f32)
            scale = lax.rsqrt(jnp.mean(x * x, axis=-1, keepdims=True) + epsilon)
            place = pl.multiple_of((rank ^ i) * rows, rows)
            normed_ref[0, pl.ds(place, rows), :] = (x * scale * gain_ref[...]).astype(bf16)
        whole = jnp.concatenate([w[...] for w in (wq0, wq1, wk0, wk1, wv0, wv1)], axis=1)
        wide_ref[...] = dot(whole, normed_ref[0], ((0,), (1,)))

    head = qkv_ref.shape[3]
    h = pl.program_id(0)
    lanes = wq0.shape[1]
    place = jnp.where(h < heads - 1, h * head, lanes + lax.rem(rank, 2) * head)
    part = lambda c: pl.ds(pl.multiple_of(c * (lanes + 128) + place, head), head)
    queries = wide_ref[part(0), :] * (head ** -0.5)
    values = wide_ref[part(2), :]
    q_ref[...] = queries.T.astype(bf16)
    v_ref[...] = values.T.astype(bf16)
    qkv_ref[0, 0, 0] = queries.astype(bf16)
    qkv_ref[0, 0, 1] = wide_ref[part(1), :].astype(bf16)
    qkv_ref[0, 0, 2] = values.astype(bf16)
    base_ref[...] = pltpu.roll(
        jnp.broadcast_to(bias_ref[0], (128, span)), 0, axis=1, stride=1, stride_axis=0
    )
    keys = qkv_ref[0, 0, 1]
    values = v_ref[...]
    top = length - 128
    step = 256
    for b in range(length // step):
        scores = dot(q_ref[b * step : (b + 1) * step, :], keys)
        bias = jnp.concatenate(
            [
                base_ref[:, top - b * step - k * 128 : top - b * step - k * 128 + length]
                for k in range(step // 128)
            ],
            axis=0,
        )
        scores = scores + bias
        raised = jnp.exp(scores - jnp.max(scores, axis=1, keepdims=True))
        inverse = 1.0 / jnp.sum(raised, axis=1, keepdims=True)
        raised = raised.astype(bf16)
        raised_ref[0, 0, b * step : (b + 1) * step, :] = raised
        attended = dot(raised, values) * inverse
        out_ref[0, 0, :, b * step : (b + 1) * step] = attended.T.astype(bf16)
        inverse_ref[0, 0, :, b * step : (b + 1) * step] = jnp.broadcast_to(inverse, (step, 128)).T[:8]
    for i, p_ref in enumerate((p0, p1, p2, p3)):
        p_ref[...] = out_ref[0, 0, :, pl.ds(pl.multiple_of((rank ^ i) * rows, rows), rows)]


def attend(rank, blocks, gain, weights, bias_rows, previous, seq, groups):
    rows, width = blocks[0].shape
    heads, _, span = bias_rows.shape
    head = width // (4 * heads)
    length = 4 * rows
    first = previous is None
    whole = lambda h, r: (0, 0)
    low = 4 * (heads - 1) * head // 128
    lanes = (heads - 1) * head
    in_specs = [pl.BlockSpec((rows, width), whole)] * 4 + [
        pl.BlockSpec((1, width), whole),
        *[pl.BlockSpec((width, lanes), lambda h, r: (0, r[0]))] * 3,
        *[pl.BlockSpec((width, 128), lambda h, r: (0, low + lax.div(r[0], 2)))] * 3,
        pl.BlockSpec((1, 1, span), lambda h, r: (h, 0, 0)),
    ]
    args = list(blocks) + [gain] + list(weights) * 2 + [bias_rows]
    aliases = {}
    if not first:
        aliases = {1 + len(args) + k: k for k in range(5)}
        in_specs = in_specs + [pl.BlockSpec(memory_space=pl.ANY)] * 5
        args = args + list(previous)
    out_shape = [
        jax.ShapeDtypeStruct((groups, length, width), bf16),
        jax.ShapeDtypeStruct((groups, heads, 3, head, length), bf16),
        jax.ShapeDtypeStruct((groups, heads, length, length), bf16),
        jax.ShapeDtypeStruct((groups, heads, 8, length), f32),
        jax.ShapeDtypeStruct((groups, heads, head, length), bf16),
    ] + [jax.ShapeDtypeStruct((heads * head, rows), bf16)] * 4
    out_specs = [
        pl.BlockSpec((1, length, width), lambda h, r: (seq, 0, 0)),
        pl.BlockSpec((1, 1, 3, head, length), lambda h, r: (seq, h, 0, 0, 0)),
        pl.BlockSpec((1, 1, length, length), lambda h, r: (seq, h, 0, 0)),
        pl.BlockSpec((1, 1, 8, length), lambda h, r: (seq, h, 0, 0)),
        pl.BlockSpec((1, 1, head, length), lambda h, r: (seq, h, 0, 0)),
    ] + [pl.BlockSpec((head, rows), lambda h, r: (h, 0))] * 4
    outs = pl.pallas_call(
        functools.partial(forward_kernel, rows=rows, heads=heads, first=first),
        grid_spec=pltpu.PrefetchScalarGridSpec(
            num_scalar_prefetch=1,
            grid=(heads,),
            in_specs=in_specs,
            out_specs=out_specs,
            scratch_shapes=[
                pltpu.VMEM((length, head), bf16),
                pltpu.VMEM((length, head), bf16),
                pltpu.VMEM((128, span), f32),
                pltpu.VMEM((3 * (lanes + 128), length), f32),
            ],
        ),
        out_shape=out_shape,
        input_output_aliases=aliases,
        compiler_params=pltpu.CompilerParams(vmem_limit_bytes=vmem_bytes),
        cost_estimate=pl.CostEstimate(
            flops=20 * heads * length * length * 256, bytes_accessed=20_000_000, transcendentals=0
        ),
        name="attention_forward",
    )(rank, *args)
    return outs[:5], outs[5:]


def backward_kernel(
    rank_ref, g0, g1, g2, g3, qkv_ref, raised_ref, inverse_ref, out_ref, normed_ref, bucket_ref,
    d0, d1, d2, d3, weight_grad_ref,
    grad_ref, left_ref, right_ref, key_ref, scores_ref, packed_ref, total_ref, offsets_ref, *, rows
):
    rank = rank_ref[0]
    length = 4 * rows
    head = grad_ref.shape[0]
    step_id = pl.program_id(0)
    for i, g_ref in enumerate((g0, g1, g2, g3)):
        grad_ref[:, pl.ds(pl.multiple_of((rank ^ i) * rows, rows), rows)] = g_ref[...].astype(f32)
    scaled = grad_ref[...] * inverse_ref[0, 0, 0:1, :]
    shift = jnp.sum(scaled * out_ref[0, 0].astype(f32), axis=0, keepdims=True)
    high = shift.astype(bf16).astype(f32)
    scaled_low = scaled.astype(bf16)
    tail = jnp.concatenate(
        [high, shift - high, jnp.zeros((128 - head - 2, length), f32)], axis=0
    )
    left_ref[...] = jnp.concatenate([scaled_low.astype(f32), tail], axis=0).T.astype(bf16)
    right_ref[0:head, :] = qkv_ref[0, 0, 2]
    right_ref[head:, :] = jnp.where(
        lax.broadcasted_iota(jnp.int32, (128 - head, length), 0) < 2, -1.0, 0.0
    ).astype(bf16)
    key_ref[...] = qkv_ref[0, 0, 1].astype(f32).T.astype(bf16)

    @pl.when(step_id == 0)
    def _():
        offsets_ref[...] = jnp.zeros_like(offsets_ref)
        total_ref[...] = jnp.zeros_like(total_ref)

    top = length - 128
    step = 256
    for b in range(length // step):
        inner = dot(left_ref[b * step : (b + 1) * step, :], right_ref[...])
        grads = raised_ref[0, 0, b * step : (b + 1) * step, :].astype(f32) * inner
        for k in range(step // 128):
            place = top - b * step - k * 128
            offsets_ref[:, place : place + length] += grads[k * 128 : (k + 1) * 128]
        scores_ref[b * step : (b + 1) * step, :] = grads.astype(bf16)
    packed_ref[0:head, :] = (dot(scores_ref[...], key_ref[...]) * (head ** -0.5)).T.astype(bf16)
    packed_ref[head : 2 * head, :] = dot(qkv_ref[0, 0, 0], scores_ref[...]).astype(bf16)
    packed_ref[2 * head :, :] = dot(scaled_low, raised_ref[0, 0]).astype(bf16)
    for i, d_ref in enumerate((d0, d1, d2, d3)):
        d_ref[...] = packed_ref[:, pl.ds(pl.multiple_of((rank ^ i) * rows, rows), rows)]
    total_ref[...] += dot(packed_ref[...], normed_ref[0])

    @pl.when(step_id == pl.num_programs(0) - 1)
    def _():
        width = total_ref.shape[1]
        weight_grad_ref[:, :width] = total_ref[...].astype(bf16)
        span = offsets_ref.shape[1]
        folded = offsets_ref[...]
        half = 64
        while half >= 1:
            folded = folded[:half] + pltpu.roll(folded[half : 2 * half], span - half, axis=1)
            half //= 2
        folded = jnp.broadcast_to(folded, (16, span))
        high_part = folded.astype(bf16)
        low_part = (folded - high_part.astype(f32)).astype(bf16)
        buckets = dot(high_part, bucket_ref[...], ((1,), (1,))) + dot(
            low_part, bucket_ref[...], ((1,), (1,))
        )
        weight_grad_ref[:, width:] = jnp.zeros((weight_grad_ref.shape[0], 128), bf16)
        weight_grad_ref[0:16, width:] = buckets.astype(bf16)


def attend_back(rank, grads, saved, bucket_hot, head_index):
    normed, qkv, raised, inverse, out = saved
    groups, length, width = normed.shape
    _, heads, _, head, _ = qkv.shape
    rows = length // 4
    span = 2 * length
    h = head_index
    in_specs = [pl.BlockSpec((head, rows), lambda s, r: (h, s))] * 4 + [
        pl.BlockSpec((1, 1, 3, head, length), lambda s, r: (s, h, 0, 0, 0)),
        pl.BlockSpec((1, 1, length, length), lambda s, r: (s, h, 0, 0)),
        pl.BlockSpec((1, 1, 8, length), lambda s, r: (s, h, 0, 0)),
        pl.BlockSpec((1, 1, head, length), lambda s, r: (s, h, 0, 0)),
        pl.BlockSpec((1, length, width), lambda s, r: (s, 0, 0)),
        pl.BlockSpec((128, span), lambda s, r: (0, 0)),
    ]
    out_shape = [jax.ShapeDtypeStruct((3 * head, groups * rows), bf16)] * 4 + [
        jax.ShapeDtypeStruct((3 * head, width + 128), bf16),
    ]
    out_specs = [pl.BlockSpec((3 * head, rows), lambda s, r: (0, s))] * 4 + [
        pl.BlockSpec((3 * head, width + 128), lambda s, r: (0, 0)),
    ]
    outs = pl.pallas_call(
        functools.partial(backward_kernel, rows=rows),
        grid_spec=pltpu.PrefetchScalarGridSpec(
            num_scalar_prefetch=1,
            grid=(groups,),
            in_specs=in_specs,
            out_specs=out_specs,
            scratch_shapes=[
                pltpu.VMEM((head, length), f32),
                pltpu.VMEM((length, 128), bf16),
                pltpu.VMEM((128, length), bf16),
                pltpu.VMEM((length, head), bf16),
                pltpu.VMEM((length, length), bf16),
                pltpu.VMEM((3 * head, length), bf16),
                pltpu.VMEM((3 * head, width), f32),
                pltpu.VMEM((128, span), f32),
            ],
        ),
        out_shape=out_shape,
        compiler_params=pltpu.CompilerParams(vmem_limit_bytes=vmem_bytes),
        cost_estimate=pl.CostEstimate(
            flops=20 * groups * length * length * 256, bytes_accessed=10_000_000, transcendentals=0
        ),
        name="attention_backward",
    )(rank, *grads, qkv, raised, inverse, out, normed, bucket_hot)
    return outs[:4], outs[4]


def out_weight_kernel(rank_ref, b0, b1, b2, b3, out_ref, extra_ref, grad_ref, whole_ref, total_ref):
    rank = rank_ref[0]
    rows, width = b0.shape
    for i, b_ref in enumerate((b0, b1, b2, b3)):
        whole_ref[pl.ds(pl.multiple_of((rank ^ i) * rows, rows), rows), :] = b_ref[...]
    part = dot(out_ref[0].reshape(grad_ref.shape[0], 4 * rows), whole_ref[...])

    @pl.when(pl.program_id(0) == 0)
    def _():
        total_ref[...] = part

    @pl.when(pl.program_id(0) > 0)
    def _():
        total_ref[...] += part

    @pl.when(pl.program_id(0) == pl.num_programs(0) - 1)
    def _():
        grad_ref[:, :width] = total_ref[...].astype(bf16)
        grad_ref[:, width:] = extra_ref[...]


def out_weight_rows(rank, blocks, out, extra):
    groups, heads, head, length = out.shape
    count, width = heads * head, blocks[0].shape[1]
    rows = length // 4
    lanes = width + extra.shape[1]
    return pl.pallas_call(
        out_weight_kernel,
        grid_spec=pltpu.PrefetchScalarGridSpec(
            num_scalar_prefetch=1,
            grid=(groups,),
            in_specs=[pl.BlockSpec((rows, width), lambda s, r: (s, 0))] * 4
            + [
                pl.BlockSpec((1, heads, head, length), lambda s, r: (s, 0, 0, 0)),
                pl.BlockSpec(extra.shape, lambda s, r: (0, 0)),
            ],
            out_specs=pl.BlockSpec((count, lanes), lambda s, r: (0, 0)),
            scratch_shapes=[pltpu.VMEM((length, width), bf16), pltpu.VMEM((count, width), f32)],
        ),
        out_shape=jax.ShapeDtypeStruct((count, lanes), bf16),
        compiler_params=pltpu.CompilerParams(vmem_limit_bytes=vmem_bytes),
        cost_estimate=pl.CostEstimate(
            flops=3_000_000_000, bytes_accessed=5_000_000, transcendentals=0
        ),
        name="out_weight_rows",
    )(rank, *blocks, out, extra)


def head_place(rank, h, heads):
    return rank * (heads - 1) + h if h < heads - 1 else 4 * (heads - 1) + rank


def turn_kernel(rank_ref, *refs, heads, part):
    blocks, weight_refs, before_ref, rest = refs[0:4], refs[4:7], refs[7], refs[8:]
    if part:
        rest = rest[3:]
    q_ref, k_ref, v_ref, norm_ref, gathered_ref, total_ref = rest
    rank = rank_ref[0]
    count = heads - 1 if part == 0 else 1
    head = blocks[0].shape[0] // (3 * count)

    @pl.when(pl.program_id(0) == 0)
    def _():
        total_ref[...] = jnp.zeros_like(total_ref)
        for i in range(4):
            for h in range(count):
                place = pl.multiple_of(((rank ^ i) * count + h) * head, head)
                for c in range(3):
                    gathered_ref[c, pl.ds(place, head), :] = blocks[i][
                        (3 * h + c) * head : (3 * h + c + 1) * head, :
                    ].astype(f32)

    place = pl.multiple_of(pl.program_id(0) * 128, 128)
    for c, grad_ref in enumerate((q_ref, k_ref, v_ref)):
        grads = gathered_ref[c, pl.ds(place, 128), :].T
        grad_ref[...] = grads
        total_ref[...] += grads * weight_refs[c][...].astype(f32)

    @pl.when(pl.program_id(0) == pl.num_programs(0) - 1)
    def _():
        norm_ref[...] = before_ref[...] + jnp.sum(total_ref[...].T, axis=0, keepdims=True)


def turn(rank, blocks, weights, previous, heads, part):
    width = weights[0].shape[0]
    head = width // (4 * heads)
    count = heads - 1 if part == 0 else 1
    first = 0 if part == 0 else 4 * (heads - 1) * head // 128
    column = pl.BlockSpec((width, 128), lambda s, r: (0, first + s))
    row = pl.BlockSpec((8, width), lambda s, r: (0, 0))
    in_specs = [pl.BlockSpec((3 * count * head, width), lambda s, r: (0, 0))] * 4
    in_specs += [column] * 3 + [row]
    before = jnp.zeros((8, width), f32) if part == 0 else previous[3]
    args = list(blocks) + list(weights) + [before]
    aliases = {}
    if part:
        aliases = {1 + len(args) + k: k for k in range(3)}
        in_specs += [pl.BlockSpec(memory_space=pl.ANY)] * 3
        args += list(previous[:3])
    return pl.pallas_call(
        functools.partial(turn_kernel, heads=heads, part=part),
        grid_spec=pltpu.PrefetchScalarGridSpec(
            num_scalar_prefetch=1,
            grid=(4 * count * head // 128,),
            in_specs=in_specs,
            out_specs=[column] * 3 + [row],
            scratch_shapes=[
                pltpu.VMEM((3, 4 * count * head, width), f32),
                pltpu.VMEM((width, 128), f32),
            ],
        ),
        out_shape=[jax.ShapeDtypeStruct((width, width), f32)] * 3
        + [jax.ShapeDtypeStruct((8, width), f32)],
        input_output_aliases=aliases,
        compiler_params=pltpu.CompilerParams(vmem_limit_bytes=vmem_bytes),
        cost_estimate=pl.CostEstimate(
            flops=3_000_000_000 * count, bytes_accessed=3_000_000 * count, transcendentals=0
        ),
        name="weight_gradient_turn",
    )(rank, *args)


def input_kernel(rank_ref, *refs, heads):
    pieces = refs[: 4 * heads]
    weight_refs = refs[4 * heads : 4 * heads + 3]
    x_ref, grad_ref, gain_ref, out_ref, gathered_ref = refs[4 * heads + 3 :]
    rank = rank_ref[0]
    head = pieces[0].shape[0] // 3
    for h in range(heads):
        for i in range(4):
            place = pl.multiple_of(head_place(rank ^ i, h, heads) * head, head)
            for c in range(3):
                gathered_ref[c, pl.ds(place, head), :] = pieces[h * 4 + i][
                    c * head : (c + 1) * head, :
                ]
    total = dot(gathered_ref[0], weight_refs[0][...], ((0,), (1,)))
    total += dot(gathered_ref[1], weight_refs[1][...], ((0,), (1,)))
    total += dot(gathered_ref[2], weight_refs[2][...], ((0,), (1,)))
    x = x_ref[...].astype(f32)
    scale = lax.rsqrt(jnp.mean(x * x, axis=-1, keepdims=True) + epsilon)
    unit = x * scale
    scaled = total * gain_ref[...]
    inner_mean = jnp.mean(scaled * unit, axis=-1, keepdims=True)
    out_ref[...] = grad_ref[...] + scale * (scaled - unit * inner_mean)


def input_gradient(rank, pieces, weights, inputs, residual_grad, gain, heads):
    tokens, width = inputs.shape
    half = tokens // 2
    whole = lambda s, r: (0, 0)
    part = pl.BlockSpec((half, width), lambda s, r: (s, 0))
    return pl.pallas_call(
        functools.partial(input_kernel, heads=heads),
        grid_spec=pltpu.PrefetchScalarGridSpec(
            num_scalar_prefetch=1,
            grid=(2,),
            in_specs=[pl.BlockSpec((p.shape[0], half), lambda s, r: (0, s)) for p in pieces]
            + [pl.BlockSpec((width, width), whole)] * 3
            + [part, part, pl.BlockSpec((1, width), whole)],
            out_specs=part,
            scratch_shapes=[pltpu.VMEM((3, width, half), bf16)],
        ),
        out_shape=jax.ShapeDtypeStruct((tokens, width), f32),
        compiler_params=pltpu.CompilerParams(vmem_limit_bytes=vmem_bytes),
        cost_estimate=pl.CostEstimate(
            flops=6_000_000_000, bytes_accessed=9_000_000, transcendentals=0
        ),
        name="input_gradient",
    )(rank, *pieces, *weights, inputs, residual_grad, gain)


def expert_part(expert, rows, grads, into, out_of, router, experts):
    logits = dot(rows, router)
    lanes = lax.broadcasted_iota(jnp.int32, logits.shape, 1)
    logits = jnp.where(lanes < experts, logits, -1e30)
    raised = jnp.exp(logits - jnp.max(logits, axis=1, keepdims=True))
    picked = jnp.sum(jnp.where(lanes == expert, raised, 0.0), axis=1, keepdims=True)
    gate = picked / jnp.sum(raised, axis=1, keepdims=True)

    before = dot(rows, into)
    hidden = dot(grads, out_of, ((1,), (1,)))
    square = before * before
    bend = 0.5 + 0.5 * jnp.tanh(before * (0.7978845608 + (0.7978845608 * 0.044715) * square))
    active = before * bend
    slope = 2.0 * 0.7978845608 + (6.0 * 0.7978845608 * 0.044715) * square
    back = hidden * (bend + active * (1.0 - bend) * slope)
    gate_part = jnp.sum(active * hidden, axis=1, keepdims=True)
    row_part = dot(back.astype(bf16), into, ((1,), (1,))).astype(bf16)
    extra = jnp.where(
        lax.broadcasted_iota(jnp.int32, (rows.shape[0], 128), 1) == 0, gate_part, 0.0
    ).astype(bf16)
    gated = (gate * active).astype(bf16)
    produced = dot(gated, out_of).astype(bf16)
    return row_part, extra, produced, gated, (gate * back).astype(bf16)


def expert_kernel(first_ref, *refs, members, experts):
    count = len(members)
    ins, outs = refs[: 6 * count + 1], refs[6 * count + 1 :]
    router_ref = ins[-1]
    for k, e in enumerate(members):
        xa, xb, ga, gb, into_ref, out_of_ref = ins[6 * k : 6 * k + 6]
        rows = jnp.concatenate([xa[...], xb[...]], axis=0)
        grads = jnp.concatenate([ga[...], gb[...]], axis=0)
        row_part, extra, produced, gated, gated_back = expert_part(
            first_ref[0] + e, rows, grads, into_ref[0], out_of_ref[0], router_ref[...], experts
        )
        half, width = xa.shape
        for p in range(2):
            part = slice(p * half, (p + 1) * half)
            d, y, a, b = outs[8 * k + p : 8 * k + 8 : 2]
            d[:, :width] = row_part[part]
            d[:, width:] = extra[part]
            y[...] = produced[part]
            a[...] = gated[part]
            b[...] = gated_back[part]


def run_experts(members, first, rows, grads, into, out_of, router, experts):
    count, width = rows[0][0].shape
    hidden = into.shape[2]
    steps = 2
    half = count // steps
    block = lambda lanes: pl.BlockSpec((half, lanes), lambda s, f: (s, 0))
    shape = lambda lanes: jax.ShapeDtypeStruct((count, lanes), bf16)
    in_specs, args, out_specs, out_shape = [], [], [], []
    for k, e in enumerate(members):
        in_specs += [block(width)] * 2
        in_specs += [
            pl.BlockSpec((half, width), functools.partial(lambda e, s, f: (steps * e + s, 0), e))
        ] * 2
        in_specs += [
            pl.BlockSpec((1, width, hidden), functools.partial(lambda e, s, f: (e, 0, 0), e)),
            pl.BlockSpec((1, hidden, width), functools.partial(lambda e, s, f: (e, 0, 0), e)),
        ]
        args += list(rows[k]) + list(grads) + [into, out_of]
        out_specs += [block(width + 128)] * 2 + [block(width)] * 2 + [block(hidden)] * 4
        out_shape += [shape(width + 128)] * 2 + [shape(width)] * 2 + [shape(hidden)] * 4
    outs = pl.pallas_call(
        functools.partial(expert_kernel, members=members, experts=experts),
        grid_spec=pltpu.PrefetchScalarGridSpec(
            num_scalar_prefetch=1,
            grid=(steps,),
            in_specs=in_specs + [pl.BlockSpec(router.shape, lambda s, f: (0, 0))],
            out_specs=out_specs,
        ),
        out_shape=out_shape,
        compiler_params=pltpu.CompilerParams(vmem_limit_bytes=vmem_bytes),
        cost_estimate=pl.CostEstimate(
            flops=8_500_000_000 * len(members), bytes_accessed=9_000_000, transcendentals=0
        ),
        name="experts",
    )(first, *args, router)
    return [[outs[8 * k + 2 * t : 8 * k + 2 * t + 2] for t in range(4)] for k in range(len(members))]


def expert_weight_kernel(*refs, count):
    rows, actives, backs = refs[:count], refs[count : 2 * count], refs[2 * count : 3 * count]
    grads = refs[3 * count : 4 * count]
    into_ref, out_of_ref = refs[-2:]
    whole = lambda parts: jnp.concatenate([p[...] for p in parts], axis=0)
    into_ref[0] = dot(whole(rows), whole(backs), ((0,), (0,)))
    out_of_ref[0] = dot(whole(actives), whole(grads), ((0,), (0,)))


def expert_weight_grads(expert, owned, rows, actives, backs, grads, previous):
    count, width = rows[0].shape
    hidden = actives[0].shape[1]
    own = lambda v: pl.BlockSpec(v.shape, lambda s: (0, 0))
    args = list(rows) + list(actives) + list(backs) + list(grads)
    in_specs = [own(v) for v in args[:-4]] + [
        pl.BlockSpec((count, width), lambda s: (expert, 0))
    ] * 4
    aliases = {}
    if previous is not None:
        aliases = {len(args) + k: k for k in range(2)}
        in_specs += [pl.BlockSpec(memory_space=pl.ANY)] * 2
        args += list(previous)
    return pl.pallas_call(
        functools.partial(expert_weight_kernel, count=4),
        grid=(1,),
        in_specs=in_specs,
        out_specs=[
            pl.BlockSpec((1, width, hidden), lambda s: (expert, 0, 0)),
            pl.BlockSpec((1, hidden, width), lambda s: (expert, 0, 0)),
        ],
        out_shape=[
            jax.ShapeDtypeStruct((owned, width, hidden), f32),
            jax.ShapeDtypeStruct((owned, hidden, width), f32),
        ],
        input_output_aliases=aliases,
        compiler_params=pltpu.CompilerParams(vmem_limit_bytes=vmem_bytes),
        cost_estimate=pl.CostEstimate(
            flops=7_000_000_000, bytes_accessed=12_000_000, transcendentals=0
        ),
        name="expert_weight_gradients",
    )(*args)


def combine_kernel(
    target_ref, chosen_ref, *refs, owned, experts
):
    returned = refs[:owned]
    normed_ref, residual_ref, up_ref, router_ref, gain_ref, weight_ref = refs[owned : owned + 6]
    grad_ref, branch_ref, g0, g1, g2, g3, extra_ref = refs[owned + 6 :]
    tokens, width = normed_ref.shape
    count = returned[0].shape[0]
    back = jnp.zeros((tokens, width + 128), f32)
    for e in range(owned):
        hot = target_ref[e : e + 1, :] == lax.broadcasted_iota(jnp.int32, (count, tokens), 0)
        back += dot(hot.astype(f32).astype(bf16), returned[e][...], ((0,), (0,)))
    residual = residual_ref[...]
    scale = lax.rsqrt(jnp.mean(residual * residual, axis=-1, keepdims=True) + epsilon)
    unit = residual * scale

    logits = dot(normed_ref[...], router_ref[...])
    lanes = lax.broadcasted_iota(jnp.int32, logits.shape, 1)
    logits = jnp.where(lanes < experts, logits, -1e30)
    raised = jnp.exp(logits - jnp.max(logits, axis=1, keepdims=True))
    probs = raised / jnp.sum(raised, axis=1, keepdims=True)
    hot = (lanes == chosen_ref[...]).astype(f32)
    gate = jnp.sum(probs * hot, axis=1, keepdims=True)
    gate_grad = back[:, width : width + 1]
    logit_grad = (probs * gate_grad * (hot - gate)).astype(bf16)
    normed_grad = dot(logit_grad, router_ref[...], ((1,), (1,))) + gate * back[:, :width]
    scaled = normed_grad * gain_ref[...]
    inner_mean = jnp.mean(scaled * unit, axis=-1, keepdims=True)
    grads = up_ref[...].astype(f32) + scale * (scaled - unit * inner_mean)
    grad_ref[...] = grads
    branch = grads.astype(bf16)
    branch_ref[...] = branch
    rows = weight_ref.shape[0] // 4
    for i, g_ref in enumerate((g0, g1, g2, g3)):
        g_ref[...] = dot(weight_ref[i * rows : (i + 1) * rows, :], branch, ((1,), (1,))).astype(bf16)
    router_part = dot(logit_grad, normed_ref[...], ((0,), (0,)))
    norm_part = jnp.broadcast_to(jnp.sum(normed_grad * unit, axis=0, keepdims=True), (8, width))

    @pl.when(pl.program_id(0) == 0)
    def _():
        extra_ref[: router_part.shape[0], :] = router_part
        extra_ref[router_part.shape[0] :, :] = norm_part

    @pl.when(pl.program_id(0) > 0)
    def _():
        extra_ref[: router_part.shape[0], :] += router_part
        extra_ref[router_part.shape[0] :, :] += norm_part


def combine(targets, chosen, returned, normed, residual, upstream, router, gain, weights, experts):
    tokens, width = residual.shape
    half = tokens // 2
    owned = len(returned)
    whole = lambda v: pl.BlockSpec(v.shape, lambda s: (0, 0))
    part = pl.BlockSpec((half, width), lambda s: (s, 0))
    lanes = router.shape[1]
    columns = weights.shape[0] // 4
    outs = pl.pallas_call(
        functools.partial(combine_kernel, owned=owned, experts=experts),
        grid=(2,),
        in_specs=[
            pl.BlockSpec((targets.shape[0], half), lambda s: (0, s)),
            pl.BlockSpec((half, 1), lambda s: (s, 0)),
        ]
        + [whole(v) for v in returned]
        + [part] * 3
        + [whole(router), whole(gain), whole(weights)],
        out_specs=[part, part]
        + [pl.BlockSpec((columns, half), lambda s: (0, s))] * 4
        + [pl.BlockSpec((lanes + 8, width), lambda s: (0, 0))],
        out_shape=[
            jax.ShapeDtypeStruct((tokens, width), f32),
            jax.ShapeDtypeStruct((tokens, width), bf16),
        ]
        + [jax.ShapeDtypeStruct((columns, tokens), bf16)] * 4
        + [jax.ShapeDtypeStruct((lanes + 8, width), f32)],
        compiler_params=pltpu.CompilerParams(vmem_limit_bytes=vmem_bytes),
        cost_estimate=pl.CostEstimate(
            flops=6_000_000_000, bytes_accessed=12_000_000, transcendentals=0
        ),
        name="combine",
    )(targets, chosen, *returned, normed, residual, upstream, router, gain, weights)
    return outs[0], outs[1], outs[2:6], outs[6]


def on_device(
    block_input, norm1_gain, query_weight, key_weight, value_weight, out_weight,
    relative_bucket_bias, norm2_gain, router_weight, expert_in, expert_out,
    expert_index, slot_index, bucket_table, out_grad,
):
    groups, rows, width = block_input.shape
    tokens = groups * rows
    wide_count = lax.axis_size("wide")
    narrow_count = lax.axis_size("narrow")
    experts = router_weight.shape[1]
    owned = expert_in.shape[0]
    capacity = max(2, (5 * tokens + 4 * experts - 1) // (4 * experts))
    buckets, head_count = relative_bucket_bias.shape
    head = width // head_count
    heads = head_count // narrow_count
    columns = heads * head
    score_scale = head ** (-0.5)
    span = bucket_table.shape[0]
    rank = lax.axis_index("narrow")
    wide_rank = lax.axis_index("wide")
    rank_arg = rank.astype(jnp.int32).reshape(1)
    gain_one = norm1_gain.astype(f32).reshape(1, width)
    gain_two = norm2_gain.astype(f32)

    first_blocks = gather_narrow(block_input[0])

    upstream_low = out_grad.reshape(tokens, width)
    chosen = expert_index.reshape(tokens)
    placed = slot_index.reshape(tokens)
    half = wide_count * capacity
    slots = owned * half
    target = jnp.where(placed < capacity, chosen * capacity + placed, -1)
    dispatch = (target[None, :] == jnp.arange(slots, dtype=jnp.int32)[:, None]).astype(bf16)

    def to_experts(values):
        sent = dot(dispatch, values).astype(bf16)
        return to_owners(sent.reshape(wide_count, owned, capacity, width))

    grad_rows = to_experts(upstream_low)

    table_turned = jnp.roll(bucket_table[::-1], -127)
    bucket_hot = (
        table_turned[None, :] == jnp.arange(128, dtype=jnp.int32)[:, None]
    ).astype(bf16)
    bias_turned = relative_bucket_bias.T
    own_bias = jnp.concatenate(
        [
            lax.dynamic_slice_in_dim(bias_turned, rank * (heads - 1), heads - 1, axis=0),
            lax.dynamic_slice_in_dim(bias_turned, narrow_count * (heads - 1) + rank, 1, axis=0),
        ],
        axis=0,
    )
    bias_rows = dot(own_bias, bucket_hot[:buckets]).reshape(heads, 1, span)

    weights = (query_weight, key_weight, value_weight)
    saved = None
    pieces = []
    blocks = first_blocks
    for s in range(groups):
        if s:
            (block,) = tie([block_input[s]], blocks[2])
            blocks = tie(gather_narrow(block, piece[0]), grad_rows)
        saved, piece = attend(rank_arg, blocks, gain_one, weights, bias_rows, saved, s, groups)
        pieces.append(exchange_narrow(piece))

    (out_weight_late,) = tie([out_weight], pieces[0][0])
    out_weight_own = []
    for i in range(4):
        low = lax.dynamic_slice_in_dim(
            out_weight_late, (rank ^ i) * (columns - head), columns - head, axis=0
        )
        last = lax.dynamic_slice_in_dim(
            out_weight_late, narrow_count * (columns - head) + (rank ^ i) * head, head, axis=0
        )
        out_weight_own.append(jnp.concatenate([low, last], axis=0))
    attended = [
        jnp.concatenate([pieces[s][i] for s in range(groups)], axis=1) for i in range(4)
    ]

    inputs = block_input.reshape(tokens, width)
    residual = inputs.astype(f32)
    for i in range(4):
        residual = residual + dot(attended[i], out_weight_own[i], ((0,), (0,)))
    scale_two = lax.rsqrt(jnp.mean(residual * residual, axis=-1, keepdims=True) + epsilon)
    unit_two = residual * scale_two
    normed_two = (unit_two * gain_two).astype(bf16)

    arrived = to_experts(normed_two)
    (grad_rows,) = tie([grad_rows], normed_two)
    grad_rows = gather_narrow(grad_rows.transpose(1, 0, 2, 3).reshape(slots, width))
    lanes = -(-experts // 128) * 128
    router_wide = jnp.pad(router_weight, ((0, 0), (0, lanes - experts)))
    first_expert = (wide_rank * owned).astype(jnp.int32).reshape(1)

    def experts_on(members, rows_in, grads_in):
        return run_experts(
            members, first_expert, rows_in, grads_in, expert_in, expert_out, router_wide, experts
        )

    own = [arrived[:, e].reshape(half, width) for e in range(owned)]
    beside = [swap(v, "narrow", 1) for v in own]
    across = [swap(v, "narrow", 2) for v in own]
    everyone = list(range(owned))
    near = experts_on(everyone, [(own[e], beside[e]) for e in everyone], grad_rows[:2])
    far, returned, expert_rows = [], [], []
    holds = near[-1][0][0]
    for e in everyone:
        (there,) = tie([across[e]], holds)
        expert_rows.append([own[e], beside[e], there, swap(there, "narrow", 1)])
        far += experts_on([e], [expert_rows[e][2:]], grad_rows[2:])
        begun = scatter_begin(list(near[e][0]) + list(far[e][0]))
        holds = begun[2]
        whole = scatter_end(*begun)
        returned.append(to_owners(whole.reshape(wide_count, capacity, -1)).reshape(half, -1))
    last = holds

    both = lambda k: [tie(list(near[e][k]) + list(far[e][k]), last) for e in range(owned)]
    outs_sum = [scatter_end(*scatter_begin(o)) for o in both(1)]
    actives, backs = both(2), both(3)
    expert_grads = None
    for e in range(owned):
        expert_grads = expert_weight_grads(
            e, owned, expert_rows[e], actives[e], backs[e], grad_rows, expert_grads
        )
    in_grads, out_grads = expert_grads
    returned = tie(returned, *expert_grads)
    targets = jnp.stack(
        [
            jnp.where(chosen % owned == e, target - (chosen // owned) * ((owned - 1) * capacity) - e * capacity, -1)
            for e in everyone
        ]
    )
    targets = jnp.where(placed < capacity, targets, -1)
    targets = jnp.pad(targets, ((0, -owned % 8), (0, 0)), constant_values=-1)
    residual_grad, branch_grad, own_grads, extra = combine(
        targets,
        chosen[:, None],
        returned,
        normed_two,
        residual,
        upstream_low,
        router_wide,
        gain_two.reshape(1, width),
        jnp.concatenate(out_weight_own, axis=0),
        experts,
    )
    grads = exchange_narrow(own_grads)
    outs_sum = tie(outs_sum, *own_grads)
    fetched = to_owners(
        jnp.stack([o.reshape(wide_count, capacity, width) for o in outs_sum], axis=1)
    ).reshape(slots, width)
    extra = jnp.concatenate([extra[:experts], extra[-1:]], axis=0).astype(bf16).reshape(-1)
    lanes = 128 * -(-extra.shape[0] // (columns * 128))
    extra = jnp.pad(extra, (0, columns * lanes - extra.shape[0])).reshape(columns, lanes)

    held = grads
    pieces, weight_parts = [], []
    for h in range(heads):
        packed, weight_part = attend_back(rank_arg, held, saved, bucket_hot, h)
        weight_parts.append(weight_part)
        pieces.append(exchange_narrow(packed))
        if h == 0:
            branch_later = tie([branch_grad], weight_part)[0]
            branch_near, branch_far = [swap(branch_later, "narrow", i) for i in (1, 2)]
        if h == heads - 2:
            branch_far = tie([branch_far], weight_part)[0]
            blocks = [branch_later, branch_near, branch_far, swap(branch_far, "narrow", 1)]
            out_rows = out_weight_rows(rank_arg, blocks, saved[4], extra)
            held = tie(grads, *pieces[0], out_rows)
    early = tie([jnp.concatenate(weight_parts[: heads - 1], axis=0)], fetched)[0]
    early = wide_parts(early)
    late_chain = Sum(weight_parts[-1])
    late_chain.step(*pieces[heads - 2], early)
    out_sum = wide_parts(tie([out_rows], early)[0])
    late_chain.step(*pieces[heads - 1], out_sum)
    early = wide_whole(tie([early], out_sum)[0])
    early = gather_narrow(early)
    late_chain.step()
    late_chain.step()
    late_chain.step(early[0])
    out_sum = wide_whole(tie([out_sum], early[0])[0])
    late = late_chain.rest()
    late = gather_narrow(tie([late], out_sum)[0])

    input_grad = input_gradient(
        rank_arg, sum(pieces, []), weights, inputs, residual_grad, gain_one, heads
    )
    turned = turn(rank_arg, early, weights, None, heads, 0)
    out_sum = gather_narrow(out_sum, turned[3])
    query_grad, key_grad, value_grad, norm1_grad = turn(rank_arg, late, weights, turned, heads, 1)

    def by_rank(parts):
        stacked = jnp.stack(parts, axis=0)
        return jnp.stack(
            [lax.dynamic_index_in_dim(stacked, rank ^ j, axis=0, keepdims=False) for j in range(4)],
            axis=0,
        )

    bias_lanes = slice(width, width + buckets)
    low_bias = by_rank(
        [jnp.stack([v[h * 3 * head, bias_lanes] for h in range(heads - 1)]) for v in early]
    ).reshape(-1, buckets)
    last_bias = by_rank([v[0, bias_lanes] for v in late])
    rel_bias_grad = jnp.concatenate([low_bias, last_bias], axis=0).astype(f32).T
    extra = sum(v[:, width:].astype(f32) for v in out_sum).reshape(-1)
    extra = extra[: (experts + 1) * width].reshape(experts + 1, width)
    out_rows = by_rank([v[:, :width] for v in out_sum])
    out_weight_grad = jnp.concatenate(
        [
            out_rows[:, : columns - head].reshape(-1, width),
            out_rows[:, columns - head :].reshape(-1, width),
        ],
        axis=0,
    ).astype(f32)

    block_out = (residual + dot(dispatch, fetched, ((0,), (0,)))).astype(bf16)

    return (
        block_out.reshape(groups, rows, width),
        input_grad.reshape(groups, rows, width),
        norm1_grad[0] / gain_one[0],
        query_grad,
        key_grad,
        value_grad,
        out_weight_grad,
        rel_bias_grad,
        extra[experts],
        extra[:experts].T,
        in_grads,
        out_grads,
    )


def solution(mesh):
    rows = P("wide", "narrow", None)
    into, out_of = P("wide", None, "narrow"), P("wide", "narrow", None)
    return jax.shard_map(
        on_device,
        mesh=mesh,
        in_specs=(rows,) + (P(),) * 8 + (into, out_of, P("wide", "narrow"), P("wide", "narrow"), P(), rows),
        out_specs=(rows, rows) + (P(),) * 8 + (into, out_of),
        check_vma=False,
    )
```

```python
import functools

import jax
import jax.numpy as jnp
from jax import lax
from jax.experimental import pallas as pl
from jax.experimental.pallas import tpu as pltpu
from jax.sharding import PartitionSpec as P

epsilon = 1e-06
bf16 = jnp.bfloat16
f32 = jnp.float32
vmem_bytes = 60 * 1024 * 1024
strip = 16


def swap(values, axis, bits):
    count = lax.axis_size(axis)
    return lax.ppermute(values, axis, [(j, j ^ bits) for j in range(count)])


def tie(values, *others):
    return list(lax.optimization_barrier((tuple(values), tuple(others)))[0])


def doubled(block):
    mine = lax.axis_index("wide")
    bit = 1
    while bit < lax.axis_size("wide"):
        upper = (mine & bit) > 0
        got = swap(block, "wide", bit)
        block = jnp.concatenate(
            [jnp.where(upper, got, block), jnp.where(upper, block, got)], axis=0
        )
        bit *= 2
    return block


def gather_narrow(values, *holds):
    near = swap(values, "narrow", 1)
    far = swap(values, "narrow", 2)
    held = tie([far], *holds)[0] if holds else far
    return [values, near, far, swap(held, "narrow", 1)]


def scatter_begin(pieces):
    near_one = swap(pieces[1], "narrow", 1)
    near_three = swap(pieces[3], "narrow", 1)
    crossing = (pieces[2].astype(f32) + near_three.astype(f32)).astype(bf16)
    return pieces[0], near_one, crossing


def scatter_end(own, near_one, crossing):
    far = swap(crossing, "narrow", 2)
    return add_three(own, near_one, far)


def add_three(own, near_one, far):
    return (own.astype(f32) + near_one.astype(f32) + far.astype(f32)).astype(bf16)


def exchange_narrow(pieces):
    return [pieces[0]] + [swap(pieces[i], "narrow", i) for i in (1, 2, 3)]


def to_owners(values):
    return lax.all_to_all(values, "wide", split_axis=0, concat_axis=0, tiled=True)


def wide_parts(block):
    count = lax.axis_size("wide")
    rows, width = block.shape
    parts = to_owners(block.reshape(count, rows // count, width))
    return jnp.sum(parts.astype(f32), axis=0).astype(bf16)


def wide_whole(mine):
    count = lax.axis_size("wide")
    whole = to_owners(jnp.broadcast_to(mine[None], (count,) + mine.shape))
    return whole.reshape((count * mine.shape[0],) + mine.shape[1:])


def dot(left, right, dims=((1,), (0,))):
    return lax.dot_general(left, right, (dims, ((), ())), preferred_element_type=f32)


def forward_kernel(
    rank_ref, x0, x1, x2, x3, gain_ref, wq0, wk0, wv0, wq1, wk1, wv1, bias_ref, *rest, rows, heads, first
):
    if not first:
        rest = rest[5:]
    normed_ref, qkv_ref, raised_ref, inverse_ref, out_ref, p0, p1, p2, p3 = rest[:9]
    q_ref, v_ref, base_ref, wide_ref, scores_ref, sums_ref = rest[9:]
    rank = rank_ref[0]
    length = 4 * rows
    span = bias_ref.shape[-1]

    @pl.when(pl.program_id(0) == 0)
    def _():
        for i, x_ref in enumerate((x0, x1, x2, x3)):
            x = x_ref[...].astype(f32)
            scale = lax.rsqrt(jnp.mean(x * x, axis=-1, keepdims=True) + epsilon)
            place = pl.multiple_of((rank ^ i) * rows, rows)
            normed_ref[0, pl.ds(place, rows), :] = (x * scale * gain_ref[...]).astype(bf16)
        whole = jnp.concatenate([w[...] for w in (wq0, wq1, wk0, wk1, wv0, wv1)], axis=1)
        wide_ref[...] = dot(whole, normed_ref[0], ((0,), (1,)))

    head = qkv_ref.shape[3]
    h = pl.program_id(0)
    lanes = wq0.shape[1]
    place = jnp.where(h < heads - 1, h * head, lanes + lax.rem(rank, 2) * head)
    part = lambda c: pl.ds(pl.multiple_of(c * (lanes + 128) + place, head), head)
    queries = wide_ref[part(0), :] * (head ** -0.5)
    values = wide_ref[part(2), :]
    q_ref[...] = queries.T.astype(bf16)
    v_ref[...] = values.T.astype(bf16)
    qkv_ref[0, 0, 0] = queries.astype(bf16)
    qkv_ref[0, 0, 1] = wide_ref[part(1), :].astype(bf16)
    qkv_ref[0, 0, 2] = values.astype(bf16)
    base_ref[...] = pltpu.roll(
        jnp.broadcast_to(bias_ref[0], (128, span)), 0, axis=1, stride=1, stride_axis=0
    )
    keys = qkv_ref[0, 0, 1]
    values = v_ref[...]
    top = length - 128
    step = 256
    blocks = length // step
    scores_ref[0] = dot(q_ref[0:step, :], keys)
    for b in range(blocks):
        if b + 1 < blocks:
            scores_ref[(b + 1) % 2] = dot(q_ref[(b + 1) * step : (b + 2) * step, :], keys)
        for k in range(0, step, strip):
            row = b * step + k
            place = top - row // 128 * 128
            line = row % 128
            scores = (
                scores_ref[b % 2, k : k + strip, :]
                + base_ref[line : line + strip, place : place + length]
            )
            raised = jnp.exp(scores - jnp.max(scores, axis=1, keepdims=True))
            total = jnp.sum(raised, axis=1, keepdims=True)
            sums_ref[k : k + strip, :] = jnp.broadcast_to(1.0 / total, (strip, 128))
            raised_ref[0, 0, row : row + strip, :] = raised.astype(bf16)
        inverse = sums_ref[...]
        attended = dot(raised_ref[0, 0, b * step : (b + 1) * step, :], values) * inverse[:, :head]
        out_ref[0, 0, :, b * step : (b + 1) * step] = attended.T.astype(bf16)
        inverse_ref[0, 0, :, b * step : (b + 1) * step] = inverse.T[:8]
    for i, p_ref in enumerate((p0, p1, p2, p3)):
        p_ref[...] = out_ref[0, 0, :, pl.ds(pl.multiple_of((rank ^ i) * rows, rows), rows)]


def attend(rank, blocks, gain, weights, bias_rows, previous, seq, groups):
    rows, width = blocks[0].shape
    heads, _, span = bias_rows.shape
    head = width // (4 * heads)
    length = 4 * rows
    first = previous is None
    whole = lambda h, r: (0, 0)
    low = 4 * (heads - 1) * head // 128
    lanes = (heads - 1) * head
    in_specs = [pl.BlockSpec((rows, width), whole)] * 4 + [
        pl.BlockSpec((1, width), whole),
        *[pl.BlockSpec((width, lanes), lambda h, r: (0, r[0]))] * 3,
        *[pl.BlockSpec((width, 128), lambda h, r: (0, low + lax.div(r[0], 2)))] * 3,
        pl.BlockSpec((1, 1, span), lambda h, r: (h, 0, 0)),
    ]
    args = list(blocks) + [gain] + list(weights) * 2 + [bias_rows]
    aliases = {}
    if not first:
        aliases = {1 + len(args) + k: k for k in range(5)}
        in_specs = in_specs + [pl.BlockSpec(memory_space=pl.ANY)] * 5
        args = args + list(previous)
    out_shape = [
        jax.ShapeDtypeStruct((groups, length, width), bf16),
        jax.ShapeDtypeStruct((groups, heads, 3, head, length), bf16),
        jax.ShapeDtypeStruct((groups, heads, length, length), bf16),
        jax.ShapeDtypeStruct((groups, heads, 8, length), f32),
        jax.ShapeDtypeStruct((groups, heads, head, length), bf16),
    ] + [jax.ShapeDtypeStruct((heads * head, rows), bf16)] * 4
    out_specs = [
        pl.BlockSpec((1, length, width), lambda h, r: (seq, 0, 0)),
        pl.BlockSpec((1, 1, 3, head, length), lambda h, r: (seq, h, 0, 0, 0)),
        pl.BlockSpec((1, 1, length, length), lambda h, r: (seq, h, 0, 0)),
        pl.BlockSpec((1, 1, 8, length), lambda h, r: (seq, h, 0, 0)),
        pl.BlockSpec((1, 1, head, length), lambda h, r: (seq, h, 0, 0)),
    ] + [pl.BlockSpec((head, rows), lambda h, r: (h, 0))] * 4
    outs = pl.pallas_call(
        functools.partial(forward_kernel, rows=rows, heads=heads, first=first),
        grid_spec=pltpu.PrefetchScalarGridSpec(
            num_scalar_prefetch=1,
            grid=(heads,),
            in_specs=in_specs,
            out_specs=out_specs,
            scratch_shapes=[
                pltpu.VMEM((length, head), bf16),
                pltpu.VMEM((length, head), bf16),
                pltpu.VMEM((128, span), f32),
                pltpu.VMEM((3 * (lanes + 128), length), f32),
                pltpu.VMEM((2, 256, length), f32),
                pltpu.VMEM((256, 128), f32),
            ],
        ),
        out_shape=out_shape,
        input_output_aliases=aliases,
        compiler_params=pltpu.CompilerParams(vmem_limit_bytes=vmem_bytes),
        cost_estimate=pl.CostEstimate(
            flops=20 * heads * length * length * 256, bytes_accessed=20_000_000, transcendentals=0
        ),
        name="attention_forward",
    )(rank, *args)
    return outs[:5], outs[5:]


def backward_kernel(
    rank_ref, g0, g1, g2, g3, qkv_ref, raised_ref, inverse_ref, out_ref, normed_ref,
    d0, d1, d2, d3, weight_grad_ref, bias_ref,
    grad_ref, left_ref, right_ref, key_ref, scores_ref, packed_ref, total_ref, offsets_ref, inner_ref, *, rows
):
    rank = rank_ref[0]
    length = 4 * rows
    head = grad_ref.shape[0]
    step_id = pl.program_id(0)
    h = pl.program_id(1)
    for i, g_ref in enumerate((g0, g1, g2, g3)):
        grad_ref[:, pl.ds(pl.multiple_of((rank ^ i) * rows, rows), rows)] = g_ref[...].astype(f32)
    scaled = grad_ref[...] * inverse_ref[0, 0, 0:1, :]
    shift = jnp.sum(scaled * out_ref[0, 0].astype(f32), axis=0, keepdims=True)
    high = shift.astype(bf16).astype(f32)
    scaled_low = scaled.astype(bf16)
    tail = jnp.concatenate(
        [high, shift - high, jnp.zeros((128 - head - 2, length), f32)], axis=0
    )
    left_ref[...] = jnp.concatenate([scaled_low.astype(f32), tail], axis=0).T.astype(bf16)
    right_ref[0:head, :] = qkv_ref[0, 0, 2]
    right_ref[head:, :] = jnp.where(
        lax.broadcasted_iota(jnp.int32, (128 - head, length), 0) < 2, -1.0, 0.0
    ).astype(bf16)
    key_ref[...] = qkv_ref[0, 0, 1].astype(f32).T.astype(bf16)

    @pl.when(step_id == 0)
    def _():
        offsets_ref[h] = jnp.zeros(offsets_ref.shape[1:], f32)
        total_ref[h] = jnp.zeros(total_ref.shape[1:], f32)

    top = length - 128
    step = 256
    blocks = length // step
    inner_ref[0] = dot(left_ref[0:step, :], right_ref[...])
    for b in range(blocks):
        if b + 1 < blocks:
            inner_ref[(b + 1) % 2] = dot(left_ref[(b + 1) * step : (b + 2) * step, :], right_ref[...])
        for k in range(0, step, strip):
            row = b * step + k
            place = top - row // 128 * 128
            line = row % 128
            grads = raised_ref[0, 0, row : row + strip, :].astype(f32) * inner_ref[b % 2, k : k + strip, :]
            offsets_ref[h, line : line + strip, place : place + length] += grads
            scores_ref[row : row + strip, :] = grads.astype(bf16)
    packed_ref[0:head, :] = (dot(scores_ref[...], key_ref[...]) * (head ** -0.5)).T.astype(bf16)
    packed_ref[head : 2 * head, :] = dot(qkv_ref[0, 0, 0], scores_ref[...]).astype(bf16)
    packed_ref[2 * head :, :] = dot(scaled_low, raised_ref[0, 0]).astype(bf16)
    for i, d_ref in enumerate((d0, d1, d2, d3)):
        d_ref[...] = packed_ref[:, pl.ds(pl.multiple_of((rank ^ i) * rows, rows), rows)]
    total_ref[h] += dot(packed_ref[...], normed_ref[0])

    @pl.when(step_id == pl.num_programs(0) - 1)
    def _():
        weight_grad_ref[pl.ds(pl.multiple_of(h * 3 * head, head), 3 * head), :] = total_ref[
            h
        ].astype(bf16)
        span = offsets_ref.shape[2]
        folded = offsets_ref[h]
        half = 64
        while half >= 8:
            folded = folded[:half] + pltpu.roll(folded[half : 2 * half], span - half, axis=1)
            half //= 2
        bias_ref[h] = folded


def attend_back(rank, grads, saved, first, count):
    normed, qkv, raised, inverse, out = saved
    groups, length, width = normed.shape
    head = qkv.shape[3]
    rows = length // 4
    span = 2 * length
    per_head = lambda *dims: pl.BlockSpec((1, 1) + dims, lambda s, h, r: (s, first + h) + (0,) * len(dims))
    whole = lambda *dims: pl.BlockSpec(dims, lambda s, h, r: (0,) * len(dims))
    outs = pl.pallas_call(
        functools.partial(backward_kernel, rows=rows),
        grid_spec=pltpu.PrefetchScalarGridSpec(
            num_scalar_prefetch=1,
            grid=(groups, count),
            in_specs=[pl.BlockSpec((head, rows), lambda s, h, r: (first + h, s))] * 4
            + [
                per_head(3, head, length),
                per_head(length, length),
                per_head(8, length),
                per_head(head, length),
                pl.BlockSpec((1, length, width), lambda s, h, r: (s, 0, 0)),
            ],
            out_specs=[pl.BlockSpec((3 * head, rows), lambda s, h, r: (h, s))] * 4
            + [whole(3 * head * count, width), whole(count, 8, span)],
            scratch_shapes=[
                pltpu.VMEM((head, length), f32),
                pltpu.VMEM((length, 128), bf16),
                pltpu.VMEM((128, length), bf16),
                pltpu.VMEM((length, head), bf16),
                pltpu.VMEM((length, length), bf16),
                pltpu.VMEM((3 * head, length), bf16),
                pltpu.VMEM((count, 3 * head, width), f32),
                pltpu.VMEM((count, 128, span), f32),
                pltpu.VMEM((2, 256, length), f32),
            ],
        ),
        out_shape=[jax.ShapeDtypeStruct((3 * head * count, groups * rows), bf16)] * 4
        + [
            jax.ShapeDtypeStruct((3 * head * count, width), bf16),
            jax.ShapeDtypeStruct((count, 8, span), f32),
        ],
        compiler_params=pltpu.CompilerParams(vmem_limit_bytes=vmem_bytes),
        cost_estimate=pl.CostEstimate(
            flops=11_000_000_000 * count, bytes_accessed=10_000_000 * count, transcendentals=0
        ),
        name="attention_backward",
    )(rank, *grads, qkv, raised, inverse, out, normed)
    return outs[:4], outs[4], outs[5]


def out_weight_kernel(
    rank_ref, b0, b1, b2, b3, out_ref, last_ref, extra_ref, bucket_ref, *rest
):
    bias_refs, (grad_ref, whole_ref, total_ref) = rest[:-3], rest[-3:]
    rank = rank_ref[0]
    rows, width = b0.shape
    count = last_ref.shape[0]
    for i, b_ref in enumerate((b0, b1, b2, b3)):
        whole_ref[pl.ds(pl.multiple_of((rank ^ i) * rows, rows), rows), :] = b_ref[...]
    part = dot(out_ref[0].reshape(count, 4 * rows), whole_ref[...])

    @pl.when(pl.program_id(0) == 0)
    def _():
        total_ref[...] = part

    @pl.when(pl.program_id(0) > 0)
    def _():
        total_ref[...] += part

    @pl.when(pl.program_id(0) == pl.num_programs(0) - 1)
    def _():
        grad_ref[:count, :width] = last_ref[...]
        grad_ref[count:, :width] = total_ref[...].astype(bf16)
        place = extra_ref.shape[0]
        grad_ref[:place, width:] = extra_ref[...].astype(bf16)
        grad_ref[place:, width:] = jnp.zeros((2 * count - place, extra_ref.shape[1]), bf16)
        for bias_ref in bias_refs:
            for h in range(bias_ref.shape[0]):
                folded, half = bias_ref[h], 4
                while half >= 1:
                    span = folded.shape[1]
                    folded = folded[:half] + pltpu.roll(folded[half : 2 * half], span - half, axis=1)
                    half //= 2
                folded = jnp.broadcast_to(folded, (16, span))
                high = folded.astype(bf16)
                low = (folded - high.astype(f32)).astype(bf16)
                buckets = dot(high, bucket_ref[...], ((1,), (1,))) + dot(
                    low, bucket_ref[...], ((1,), (1,))
                )
                grad_ref[place : place + 16, width : width + 128] = buckets.astype(bf16)
                place += 16


def out_weight_rows(rank, blocks, out, last, extra, bucket_hot, biases):
    groups, heads, head, length = out.shape
    count, width = last.shape
    rows = length // 4
    lanes = width + extra.shape[1]
    whole = lambda v: pl.BlockSpec(v.shape, lambda s, r: (0,) * v.ndim)
    return pl.pallas_call(
        out_weight_kernel,
        grid_spec=pltpu.PrefetchScalarGridSpec(
            num_scalar_prefetch=1,
            grid=(groups,),
            in_specs=[pl.BlockSpec((rows, width), lambda s, r: (s, 0))] * 4
            + [pl.BlockSpec((1, heads, head, length), lambda s, r: (s, 0, 0, 0))]
            + [whole(v) for v in [last, extra, bucket_hot] + biases],
            out_specs=pl.BlockSpec((2 * count, lanes), lambda s, r: (0, 0)),
            scratch_shapes=[pltpu.VMEM((length, width), bf16), pltpu.VMEM((count, width), f32)],
        ),
        out_shape=jax.ShapeDtypeStruct((2 * count, lanes), bf16),
        compiler_params=pltpu.CompilerParams(vmem_limit_bytes=vmem_bytes),
        cost_estimate=pl.CostEstimate(
            flops=3_000_000_000, bytes_accessed=5_000_000, transcendentals=0
        ),
        name="out_weight_rows",
    )(rank, *blocks, out, last, extra, bucket_hot, *biases)


def head_place(rank, h, heads):
    return rank * (heads - 1) + h if h < heads - 1 else 4 * (heads - 1) + rank


def turn_kernel(rank_ref, *refs, heads, part):
    blocks, weight_refs, before_ref, rest = refs[0:4], refs[4:7], refs[7], refs[8:]
    rank = rank_ref[0]
    if part:
        q_ref, k_ref, v_ref, norm_ref, out_ref, router_ref, norm2_ref, bias_ref = rest[3:-2]
        gathered_ref, total_ref = rest[-2:]
    else:
        q_ref, k_ref, v_ref, norm_ref, gathered_ref, total_ref = rest
    count = heads - 1 if part == 0 else 1
    width = q_ref.shape[0]
    head = width // (4 * heads)

    @pl.when(pl.program_id(0) == 0)
    def _():
        total_ref[...] = jnp.zeros_like(total_ref)
        for i in range(4):
            for h in range(count):
                place = pl.multiple_of(((rank ^ i) * count + h) * head, head)
                for c in range(3):
                    gathered_ref[c, pl.ds(place, head), :] = blocks[i][
                        (3 * h + c) * head : (3 * h + c + 1) * head, :width
                    ].astype(f32)
            if part:
                for h in range(heads):
                    place = head_place(rank ^ i, h, heads)
                    start = (3 + h) * head
                    out_ref[pl.ds(pl.multiple_of(place * head, head), head), :] = blocks[i][
                        start : start + head, :width
                    ].astype(f32)
                    start = 2 * 3 * head - (heads - h) * 16
                    bias = blocks[i][start : start + 16, width : width + 128].astype(f32)
                    bias_ref[pl.ds(place, 1), :] = bias[:1, : bias_ref.shape[1]]
        if part:
            experts = router_ref.shape[0]
            spare = 2 * 3 * head - 16 * heads
            for j, (row, lane) in enumerate(extra_places(experts, width, spare)):
                here = (slice(row, row + experts + 8), slice(width + lane, width + lane + 128))
                total = blocks[0][here].astype(f32)
                for i in range(1, 4):
                    total += blocks[i][here].astype(f32)
                router_ref[:, j * 128 : (j + 1) * 128] = total[:experts]
                norm2_ref[:, j * 128 : (j + 1) * 128] = total[experts:]

    place = pl.multiple_of(pl.program_id(0) * 128, 128)
    for c, grad_ref in enumerate((q_ref, k_ref, v_ref)):
        grads = gathered_ref[c, pl.ds(place, 128), :].T
        grad_ref[...] = grads
        total_ref[...] += grads * weight_refs[c][...].astype(f32)

    @pl.when(pl.program_id(0) == pl.num_programs(0) - 1)
    def _():
        norm_ref[...] = before_ref[...] + jnp.sum(total_ref[...].T, axis=0, keepdims=True)


def turn(rank, blocks, weights, previous, heads, part, experts=0, buckets=0):
    width = weights[0].shape[0]
    head = width // (4 * heads)
    count = heads - 1 if part == 0 else 1
    first = 0 if part == 0 else 4 * (heads - 1) * head // 128
    column = pl.BlockSpec((width, 128), lambda s, r: (0, first + s))
    whole = lambda *dims: pl.BlockSpec(dims, lambda s, r: (0,) * len(dims))
    in_specs = [whole(*b.shape) for b in blocks]
    in_specs += [column] * 3 + [whole(8, width)]
    before = jnp.zeros((8, width), f32) if part == 0 else previous[3]
    args = list(blocks) + list(weights) + [before]
    out_shape = [jax.ShapeDtypeStruct((width, width), f32)] * 3
    out_shape += [jax.ShapeDtypeStruct((8, width), f32)]
    out_specs = [column] * 3 + [whole(8, width)]
    aliases = {}
    if part:
        aliases = {1 + len(args) + k: k for k in range(3)}
        in_specs += [pl.BlockSpec(memory_space=pl.ANY)] * 3
        args += list(previous[:3])
        for dims in ((width, width), (experts, width), (8, width), (4 * heads, buckets)):
            out_shape.append(jax.ShapeDtypeStruct(dims, f32))
            out_specs.append(whole(*dims))
    return pl.pallas_call(
        functools.partial(turn_kernel, heads=heads, part=part),
        grid_spec=pltpu.PrefetchScalarGridSpec(
            num_scalar_prefetch=1,
            grid=(4 * count * head // 128,),
            in_specs=in_specs,
            out_specs=out_specs,
            scratch_shapes=[
                pltpu.VMEM((3, 4 * count * head, width), f32),
                pltpu.VMEM((width, 128), f32),
            ],
        ),
        out_shape=out_shape,
        input_output_aliases=aliases,
        compiler_params=pltpu.CompilerParams(vmem_limit_bytes=vmem_bytes),
        cost_estimate=pl.CostEstimate(
            flops=3_000_000_000 * count, bytes_accessed=3_000_000 * count, transcendentals=0
        ),
        name="weight_gradient_turn",
    )(rank, *args)


def input_kernel(rank_ref, *refs, heads):
    pieces, weight_refs = refs[:8], refs[8:11]
    x_ref, grad_ref, gain_ref, out_ref, gathered_ref = refs[11:]
    rank = rank_ref[0]
    head = pieces[4].shape[0] // 3
    for i in range(4):
        for h in range(heads):
            place = pl.multiple_of(head_place(rank ^ i, h, heads) * head, head)
            source, k = (pieces[i], h) if h < heads - 1 else (pieces[4 + i], 0)
            for c in range(3):
                gathered_ref[c, pl.ds(place, head), :] = source[
                    (3 * k + c) * head : (3 * k + c + 1) * head, :
                ]
    total = dot(gathered_ref[0], weight_refs[0][...], ((0,), (1,)))
    total += dot(gathered_ref[1], weight_refs[1][...], ((0,), (1,)))
    total += dot(gathered_ref[2], weight_refs[2][...], ((0,), (1,)))
    x = x_ref[...].astype(f32)
    scale = lax.rsqrt(jnp.mean(x * x, axis=-1, keepdims=True) + epsilon)
    unit = x * scale
    scaled = total * gain_ref[...]
    inner_mean = jnp.mean(scaled * unit, axis=-1, keepdims=True)
    out_ref[...] = grad_ref[...] + scale * (scaled - unit * inner_mean)


def input_gradient(rank, pieces, weights, inputs, residual_grad, gain, heads):
    tokens, width = inputs.shape
    half = tokens // 2
    whole = lambda s, r: (0, 0)
    part = pl.BlockSpec((half, width), lambda s, r: (s, 0))
    return pl.pallas_call(
        functools.partial(input_kernel, heads=heads),
        grid_spec=pltpu.PrefetchScalarGridSpec(
            num_scalar_prefetch=1,
            grid=(2,),
            in_specs=[pl.BlockSpec((p.shape[0], half), lambda s, r: (0, s)) for p in pieces]
            + [pl.BlockSpec((width, width), whole)] * 3
            + [part, part, pl.BlockSpec((1, width), whole)],
            out_specs=part,
            scratch_shapes=[pltpu.VMEM((3, width, half), bf16)],
        ),
        out_shape=jax.ShapeDtypeStruct((tokens, width), f32),
        compiler_params=pltpu.CompilerParams(vmem_limit_bytes=vmem_bytes),
        cost_estimate=pl.CostEstimate(
            flops=6_000_000_000, bytes_accessed=9_000_000, transcendentals=0
        ),
        name="input_gradient",
    )(rank, *pieces, *weights, inputs, residual_grad, gain)


def expert_part(expert, rows, grads, into, out_of, router, experts):
    logits = dot(rows, router)
    lanes = lax.broadcasted_iota(jnp.int32, logits.shape, 1)
    logits = jnp.where(lanes < experts, logits, -1e30)
    raised = jnp.exp(logits - jnp.max(logits, axis=1, keepdims=True))
    picked = jnp.sum(jnp.where(lanes == expert, raised, 0.0), axis=1, keepdims=True)
    gate = picked / jnp.sum(raised, axis=1, keepdims=True)

    before = dot(rows, into)
    hidden = dot(grads, out_of, ((1,), (1,)))
    square = before * before
    bend = 0.5 + 0.5 * jnp.tanh(before * (0.7978845608 + (0.7978845608 * 0.044715) * square))
    active = before * bend
    slope = 2.0 * 0.7978845608 + (6.0 * 0.7978845608 * 0.044715) * square
    back = hidden * (bend + active * (1.0 - bend) * slope)
    gate_part = jnp.sum(active * hidden, axis=1, keepdims=True)
    row_part = dot(back.astype(bf16), into, ((1,), (1,))).astype(bf16)
    extra = jnp.where(
        lax.broadcasted_iota(jnp.int32, (rows.shape[0], 128), 1) == 0, gate_part, 0.0
    ).astype(bf16)
    gated = (gate * active).astype(bf16)
    produced = dot(gated, out_of).astype(bf16)
    return row_part, extra, gated, (gate * back).astype(bf16), produced


def expert_kernel(first_ref, *refs, members, experts):
    count = len(members)
    ins, outs = refs[: 6 * count + 1], refs[6 * count + 1 :]
    router_ref = ins[-1]
    for k, e in enumerate(members):
        xa, xb, ga, gb, into_ref, out_of_ref = ins[6 * k : 6 * k + 6]
        rows = jnp.concatenate([xa[...], xb[...]], axis=0)
        grads = jnp.concatenate([ga[...], gb[...]], axis=0)
        row_part, extra, gated, gated_back, produced = expert_part(
            first_ref[0] + e, rows, grads, into_ref[0], out_of_ref[0], router_ref[...], experts
        )
        half, width = xa.shape
        for p in range(2):
            part = slice(p * half, (p + 1) * half)
            d, a, b, y = outs[8 * k + p : 8 * k + 8 : 2]
            d[:, :width] = row_part[part]
            d[:, width:] = extra[part]
            y[...] = produced[part]
            a[...] = gated[part]
            b[...] = gated_back[part]


def run_experts(members, first, rows, grads, into, out_of, router, experts):
    count, width = rows[0][0].shape
    hidden = into.shape[2]
    steps = 2
    half = count // steps
    block = lambda lanes: pl.BlockSpec((half, lanes), lambda s, f: (s, 0))
    shape = lambda lanes: jax.ShapeDtypeStruct((count, lanes), bf16)
    in_specs, args, out_specs, out_shape = [], [], [], []
    for k, e in enumerate(members):
        in_specs += [block(width)] * 2
        in_specs += [block(width)] * 2
        in_specs += [
            pl.BlockSpec((1, width, hidden), functools.partial(lambda e, s, f: (e, 0, 0), e)),
            pl.BlockSpec((1, hidden, width), functools.partial(lambda e, s, f: (e, 0, 0), e)),
        ]
        args += list(rows[k]) + list(grads[k]) + [into, out_of]
        out_specs += [block(width + 128)] * 2 + [block(hidden)] * 4 + [block(width)] * 2
        out_shape += [shape(width + 128)] * 2 + [shape(hidden)] * 4 + [shape(width)] * 2
    outs = pl.pallas_call(
        functools.partial(expert_kernel, members=members, experts=experts),
        grid_spec=pltpu.PrefetchScalarGridSpec(
            num_scalar_prefetch=1,
            grid=(steps,),
            in_specs=in_specs + [pl.BlockSpec(router.shape, lambda s, f: (0, 0))],
            out_specs=out_specs,
        ),
        out_shape=out_shape,
        compiler_params=pltpu.CompilerParams(vmem_limit_bytes=vmem_bytes),
        cost_estimate=pl.CostEstimate(
            flops=8_500_000_000 * len(members), bytes_accessed=9_000_000, transcendentals=0
        ),
        name="experts",
    )(first, *args, router)
    return [[outs[8 * k + 2 * t : 8 * k + 2 * t + 2] for t in range(4)] for k in range(len(members))]


def expert_weight_kernel(*refs, owned):
    into_ref, out_of_ref = refs[-2:]
    whole = lambda parts: jnp.concatenate([p[...] for p in parts], axis=0)
    for e in range(owned):

        @pl.when(pl.program_id(0) == e)
        def _():
            rows, actives, backs, grads = [refs[16 * e + 4 * k : 16 * e + 4 * k + 4] for k in range(4)]
            into_ref[0] = dot(whole(rows), whole(backs), ((0,), (0,)))
            out_of_ref[0] = dot(whole(actives), whole(grads), ((0,), (0,)))


def expert_weight_grads(rows, actives, backs, grads):
    owned = len(rows)
    width, hidden = rows[0][0].shape[1], actives[0][0].shape[1]
    args = []
    for e in range(owned):
        args += list(rows[e]) + list(actives[e]) + list(backs[e]) + list(grads[e])
    whole = lambda v: pl.BlockSpec(v.shape, lambda s: (0, 0))
    return pl.pallas_call(
        functools.partial(expert_weight_kernel, owned=owned),
        grid=(owned,),
        in_specs=[whole(v) for v in args],
        out_specs=[
            pl.BlockSpec((1, width, hidden), lambda s: (s, 0, 0)),
            pl.BlockSpec((1, hidden, width), lambda s: (s, 0, 0)),
        ],
        out_shape=[
            jax.ShapeDtypeStruct((owned, width, hidden), f32),
            jax.ShapeDtypeStruct((owned, hidden, width), f32),
        ],
        compiler_params=pltpu.CompilerParams(vmem_limit_bytes=vmem_bytes),
        cost_estimate=pl.CostEstimate(
            flops=18_000_000_000, bytes_accessed=30_000_000, transcendentals=0
        ),
        name="expert_weight_gradients",
    )(*args)


def combine_kernel(
    rank_ref, target_ref, chosen_ref, *refs, owned, experts, spare, heads
):
    rank = rank_ref[0]
    returned = refs[:owned]
    normed_ref, residual_ref, up_ref, router_ref, gain_ref, weight_ref = refs[owned : owned + 6]
    grad_ref, branch_ref, g0, g1, g2, g3, extra_ref, turned_ref = refs[owned + 6 :]
    tokens, width = normed_ref.shape
    count = returned[0].shape[0]
    back = jnp.zeros((tokens, width + 128), f32)
    for e in range(owned):
        hot = target_ref[e : e + 1, :] == lax.broadcasted_iota(jnp.int32, (count, tokens), 0)
        back += dot(hot.astype(f32).astype(bf16), returned[e][...], ((0,), (0,)))
    residual = residual_ref[...]
    scale = lax.rsqrt(jnp.mean(residual * residual, axis=-1, keepdims=True) + epsilon)
    unit = residual * scale

    logits = dot(normed_ref[...], router_ref[...])
    lanes = lax.broadcasted_iota(jnp.int32, logits.shape, 1)
    logits = jnp.where(lanes < experts, logits, -1e30)
    raised = jnp.exp(logits - jnp.max(logits, axis=1, keepdims=True))
    probs = raised / jnp.sum(raised, axis=1, keepdims=True)
    hot = (lanes == chosen_ref[...]).astype(f32)
    gate = jnp.sum(probs * hot, axis=1, keepdims=True)
    gate_grad = back[:, width : width + 1]
    logit_grad = (probs * gate_grad * (hot - gate)).astype(bf16)
    normed_grad = dot(logit_grad, router_ref[...], ((1,), (1,))) + gate * back[:, :width]
    scaled = normed_grad * gain_ref[...]
    inner_mean = jnp.mean(scaled * unit, axis=-1, keepdims=True)
    grads = up_ref[...].astype(f32) + scale * (scaled - unit * inner_mean)
    grad_ref[...] = grads
    branch = grads.astype(bf16)
    branch_ref[...] = branch
    turned_ref[...] = dot(weight_ref[...], branch, ((1,), (1,))).astype(bf16)
    head = weight_ref.shape[0] // (4 * heads)
    for i, g_ref in enumerate((g0, g1, g2, g3)):
        for h in range(heads):
            place = pl.multiple_of(head_place(rank ^ i, h, heads) * head, head)
            g_ref[h * head : (h + 1) * head, :] = turned_ref[pl.ds(place, head), :]
    router_part = dot(logit_grad, normed_ref[...], ((0,), (0,)))
    norm_part = jnp.broadcast_to(jnp.sum(normed_grad * unit, axis=0, keepdims=True), (8, width))

    extra = jnp.concatenate([router_part[:experts], norm_part], axis=0)
    places = extra_places(experts, width, spare)

    @pl.when(pl.program_id(0) == 0)
    def _():
        extra_ref[...] = jnp.zeros_like(extra_ref)

    for j, (row, lane) in enumerate(places):
        extra_ref[row : row + experts + 8, lane : lane + 128] += extra[:, j * 128 : (j + 1) * 128]


def extra_places(experts, width, spare):
    count = spare // (experts + 8)
    return [((j % count) * (experts + 8), j // count * 128) for j in range(width // 128)]


def combine(rank, targets, chosen, returned, normed, residual, upstream, router, gain, weights, experts, spare, heads):
    tokens, width = residual.shape
    half = tokens // 2
    owned = len(returned)
    whole = lambda v: pl.BlockSpec(v.shape, lambda s, r: (0, 0))
    part = pl.BlockSpec((half, width), lambda s, r: (s, 0))
    lanes = extra_places(experts, width, spare)[-1][1] + 128
    columns = weights.shape[0] // 4
    outs = pl.pallas_call(
        functools.partial(combine_kernel, owned=owned, experts=experts, spare=spare, heads=heads),
        grid_spec=pltpu.PrefetchScalarGridSpec(
            num_scalar_prefetch=1,
            grid=(2,),
            in_specs=[
                pl.BlockSpec((targets.shape[0], half), lambda s, r: (0, s)),
                pl.BlockSpec((half, 1), lambda s, r: (s, 0)),
            ]
            + [whole(v) for v in returned]
            + [part] * 3
            + [whole(router), whole(gain), whole(weights)],
            out_specs=[part, part]
            + [pl.BlockSpec((columns, half), lambda s, r: (0, s))] * 4
            + [pl.BlockSpec((spare, lanes), lambda s, r: (0, 0))],
            scratch_shapes=[pltpu.VMEM((weights.shape[0], half), bf16)],
        ),
        out_shape=[
            jax.ShapeDtypeStruct((tokens, width), f32),
            jax.ShapeDtypeStruct((tokens, width), bf16),
        ]
        + [jax.ShapeDtypeStruct((columns, tokens), bf16)] * 4
        + [jax.ShapeDtypeStruct((spare, lanes), f32)],
        compiler_params=pltpu.CompilerParams(vmem_limit_bytes=vmem_bytes),
        cost_estimate=pl.CostEstimate(
            flops=6_000_000_000, bytes_accessed=12_000_000, transcendentals=0
        ),
        name="combine",
    )(rank, targets, chosen, *returned, normed, residual, upstream, router, gain, weights)
    return outs[0], outs[1], outs[2:6], outs[6]


def residual_kernel(rank_ref, *refs, heads, owned):
    pieces, (target_ref, x_ref, gain_ref, weight_ref) = refs[:8], refs[8:12]
    residual_ref, normed_ref = refs[12:14]
    sent_refs, (turned_ref, total_ref) = refs[14 : 14 + owned], refs[14 + owned :]
    rank = rank_ref[0]
    head = weight_ref.shape[0] // (4 * heads)
    step = pl.program_id(0)
    for k in range(2):

        @pl.when(step == k)
        def _():
            for i in range(4):
                for h in range(heads):
                    place = pl.multiple_of(head_place(rank ^ i, h, heads) * head, head)
                    turned_ref[pl.ds(place, head), :] = pieces[4 * k + i][
                        h * head : (h + 1) * head, :
                    ]

    residual = x_ref[...].astype(f32) + dot(turned_ref[...], weight_ref[...], ((0,), (0,)))
    residual_ref[...] = residual
    scale = lax.rsqrt(jnp.mean(residual * residual, axis=-1, keepdims=True) + epsilon)
    normed = (residual * scale * gain_ref[...]).astype(bf16)
    normed_ref[...] = normed
    for e in range(owned):
        count = sent_refs[e].shape[0]
        hot = target_ref[e : e + 1, :] == lax.broadcasted_iota(
            jnp.int32, (count, normed.shape[0]), 0
        )
        part = dot(hot.astype(f32).astype(bf16), normed)

        @pl.when(step == 0)
        def _():
            total_ref[e] = part

        @pl.when(step > 0)
        def _():
            sent_refs[e][...] = (total_ref[e] + part).astype(bf16)


def residual_rows(rank, pieces, targets, inputs, gain, weights, slots, owned, heads):
    tokens, width = inputs.shape
    half = tokens // 2
    whole = lambda v: pl.BlockSpec(v.shape, lambda s, r: (0, 0))
    part = pl.BlockSpec((half, width), lambda s, r: (s, 0))
    outs = pl.pallas_call(
        functools.partial(residual_kernel, heads=heads, owned=owned),
        grid_spec=pltpu.PrefetchScalarGridSpec(
            num_scalar_prefetch=1,
            grid=(2,),
            in_specs=[whole(p) for p in pieces]
            + [
                pl.BlockSpec((targets.shape[0], half), lambda s, r: (0, s)),
                part,
                whole(gain),
                whole(weights),
            ],
            out_specs=[part, part] + [pl.BlockSpec((slots, width), lambda s, r: (0, 0))] * owned,
            scratch_shapes=[
                pltpu.VMEM((weights.shape[0], half), bf16),
                pltpu.VMEM((owned, slots, width), f32),
            ],
        ),
        out_shape=[
            jax.ShapeDtypeStruct((tokens, width), f32),
            jax.ShapeDtypeStruct((tokens, width), bf16),
        ]
        + [jax.ShapeDtypeStruct((slots, width), bf16)] * owned,
        compiler_params=pltpu.CompilerParams(vmem_limit_bytes=vmem_bytes),
        cost_estimate=pl.CostEstimate(
            flops=5_000_000_000, bytes_accessed=8_000_000, transcendentals=0
        ),
        name="residual_rows",
    )(rank, *pieces, targets, inputs, gain, weights)
    return outs[0], outs[1], outs[2:]


def on_device(
    block_input, norm1_gain, query_weight, key_weight, value_weight, out_weight,
    relative_bucket_bias, norm2_gain, router_weight, expert_in, expert_out,
    expert_index, slot_index, bucket_table, out_grad,
):
    groups, rows, width = block_input.shape
    tokens = groups * rows
    wide_count = lax.axis_size("wide")
    narrow_count = lax.axis_size("narrow")
    experts = router_weight.shape[1]
    owned = expert_in.shape[0]
    capacity = max(2, (5 * tokens + 4 * experts - 1) // (4 * experts))
    buckets, head_count = relative_bucket_bias.shape
    head = width // head_count
    heads = head_count // narrow_count
    columns = heads * head
    score_scale = head ** (-0.5)
    span = bucket_table.shape[0]
    rank = lax.axis_index("narrow")
    wide_rank = lax.axis_index("wide")
    rank_arg = rank.astype(jnp.int32).reshape(1)
    gain_one = norm1_gain.astype(f32).reshape(1, width)
    gain_two = norm2_gain.astype(f32)

    first_blocks = gather_narrow(block_input[0])

    upstream_low = out_grad.reshape(tokens, width)
    chosen = expert_index.reshape(tokens)
    placed = slot_index.reshape(tokens)
    half = wide_count * capacity
    slots = owned * half
    owner_slot = (chosen // owned) * capacity + placed
    target = jnp.where(placed < capacity, chosen * capacity + placed, -1)
    dispatch = (target[None, :] == jnp.arange(slots, dtype=jnp.int32)[:, None]).astype(bf16)

    everyone = list(range(owned))
    targets = jnp.stack(
        [
            jnp.where((placed < capacity) & (chosen % owned == e), owner_slot, -1)
            for e in everyone
        ]
    )
    targets = jnp.pad(targets, ((0, -owned % 8), (0, 0)), constant_values=-1)

    grad_rows = dot(dispatch, upstream_low).astype(bf16)
    grad_rows = to_owners(grad_rows.reshape(wide_count, owned, capacity, width))

    table_turned = jnp.roll(bucket_table[::-1], -127)
    bucket_hot = (
        table_turned[None, :] == jnp.arange(128, dtype=jnp.int32)[:, None]
    ).astype(bf16)
    bias_turned = relative_bucket_bias.T
    own_bias = jnp.concatenate(
        [
            lax.dynamic_slice_in_dim(bias_turned, rank * (heads - 1), heads - 1, axis=0),
            lax.dynamic_slice_in_dim(bias_turned, narrow_count * (heads - 1) + rank, 1, axis=0),
        ],
        axis=0,
    )
    bias_rows = dot(own_bias, bucket_hot[:buckets]).reshape(heads, 1, span)

    weights = (query_weight, key_weight, value_weight)
    saved = None
    pieces = []
    blocks = first_blocks
    for s in range(groups):
        if s:
            (block,) = tie([block_input[s]], blocks[2])
            blocks = gather_narrow(block, piece[0])
        saved, piece = attend(rank_arg, blocks, gain_one, weights, bias_rows, saved, s, groups)
        pieces.append(exchange_narrow(piece))

    grad_rows = [grad_rows[:, e].reshape(half, width) for e in everyone]
    first_grads = gather_narrow(grad_rows[0])
    rest_grads = [gather_narrow(v) for v in tie(grad_rows[1:], *pieces[-1])]
    grad_rows = [first_grads] + rest_grads
    inputs = block_input.reshape(tokens, width)
    residual, normed_two, sent = residual_rows(
        rank_arg,
        tie(sum(pieces, []), first_grads[2]),
        targets,
        inputs,
        gain_two.reshape(1, width),
        out_weight,
        half,
        owned,
        heads,
    )
    own = [to_owners(v.reshape(wide_count, capacity, width)).reshape(half, width) for v in sent]
    lanes = -(-experts // 128) * 128
    router_wide = jnp.pad(router_weight, ((0, 0), (0, lanes - experts)))
    first_expert = (wide_rank * owned).astype(jnp.int32).reshape(1)

    def experts_on(e, rows_in, grads_in):
        return run_experts(
            [e], first_expert, [rows_in], [grads_in], expert_in, expert_out, router_wide, experts
        )[0]

    near, far, returned, expert_rows = [], [], [], []
    holds = [v[2] for v in grad_rows]
    whole = ()
    for e in everyone:
        near_rows = tie([own[e], swap(own[e], "narrow", 1)], *holds)
        near.append(experts_on(e, near_rows, grad_rows[e][:2]))
        (there,) = tie([swap(own[e], "narrow", 2)], near[e][0][0])
        far_rows = tie([there, swap(there, "narrow", 1)], *holds)
        far.append(experts_on(e, far_rows, grad_rows[e][2:]))
        expert_rows.append(near_rows + far_rows)
        begun = scatter_begin(tie(list(near[e][0]) + list(far[e][0]), *whole))
        holds = [far[e][0][0]]
        whole = [scatter_end(*begun)]
        returned.append(to_owners(whole[0].reshape(wide_count, capacity, -1)).reshape(half, -1))
    both = lambda k: [
        tie(list(near[e][k]) + list(far[e][k]), *whole, *returned[:-1]) for e in everyone
    ]
    in_grads, out_grads = expert_weight_grads(expert_rows, both(1), both(2), grad_rows)
    produced = [tie(list(near[e][3]) + list(far[e][3]), *whole) for e in everyone]
    produced = [scatter_begin(v) for v in produced]
    produced = [(own, one, swap(crossing, "narrow", 2)) for own, one, crossing in produced]
    returned = tie(returned, in_grads, out_grads, *[v[2] for v in produced[:-1]])

    spare = 2 * columns - 16 * heads
    residual_grad, branch_grad, own_grads, extra = combine(
        rank_arg,
        targets,
        chosen[:, None],
        returned,
        normed_two,
        residual,
        upstream_low,
        router_wide,
        gain_two.reshape(1, width),
        out_weight,
        experts,
        spare,
        heads,
    )
    grads = exchange_narrow(own_grads)
    outs_sum = [add_three(*tie(v, own_grads[0])) for v in produced]
    fetched = to_owners(
        jnp.stack([o.reshape(wide_count, capacity, width) for o in outs_sum], axis=1)
    ).reshape(slots, width)
    branch_later = tie([branch_grad], grads[2])[0]
    branch = gather_narrow(branch_later)
    low_pieces, early, low_bias = attend_back(rank_arg, grads, saved, 0, heads - 1)
    low_pieces = exchange_narrow(low_pieces)
    early = wide_parts(tie([early], branch[2], fetched)[0])
    last_pieces, late, last_bias = attend_back(rank_arg, grads, saved, heads - 1, 1)
    last_pieces = exchange_narrow(last_pieces)
    late = out_weight_rows(
        rank_arg, tie(branch, late, *low_pieces), saved[4], late, extra, bucket_hot, [low_bias, last_bias]
    )
    (early,) = tie([early], late)
    late = wide_parts(tie([late], early)[0])
    early = doubled(early)
    input_grad = input_gradient(
        rank_arg, low_pieces + last_pieces, weights, inputs, residual_grad, gain_one, heads
    )
    block_out = (residual + dot(dispatch, fetched, ((0,), (0,)))).astype(bf16)
    late = wide_whole(tie([late], input_grad, block_out)[0])
    early = gather_narrow(early, late)
    turned = turn(rank_arg, early, weights, None, heads, 0)
    late = gather_narrow(late, turned[3])
    query_grad, key_grad, value_grad, norm1_grad, out_weight_grad, router_grad, norm2_grad, biases = turn(
        rank_arg, late, weights, turned, heads, 1, experts, buckets
    )

    return (
        block_out.reshape(groups, rows, width),
        input_grad.reshape(groups, rows, width),
        norm1_grad[0] / gain_one[0],
        query_grad,
        key_grad,
        value_grad,
        out_weight_grad,
        biases.T,
        norm2_grad[0],
        router_grad.T,
        in_grads,
        out_grads,
    )


def solution(mesh):
    rows = P("wide", "narrow", None)
    into, out_of = P("wide", None, "narrow"), P("wide", "narrow", None)
    return jax.shard_map(
        on_device,
        mesh=mesh,
        in_specs=(rows,) + (P(),) * 8 + (into, out_of, P("wide", "narrow"), P("wide", "narrow"), P(), rows),
        out_specs=(rows, rows) + (P(),) * 8 + (into, out_of),
        check_vma=False,
    )
```

```python
import functools

import jax
import jax.numpy as jnp
from jax import lax
from jax.experimental import pallas as pl
from jax.experimental.pallas import tpu as pltpu
from jax.sharding import PartitionSpec as P

epsilon = 1e-06
bf16 = jnp.bfloat16
f32 = jnp.float32
vmem_bytes = 60 * 1024 * 1024
strip = 16


def swap(values, axis, bits):
    count = lax.axis_size(axis)
    return lax.ppermute(values, axis, [(j, j ^ bits) for j in range(count)])


def tie(values, *others):
    return list(lax.optimization_barrier((tuple(values), tuple(others)))[0])


def doubled(block, *holds):
    mine = lax.axis_index("wide")
    rows, width = block.shape
    bit = lax.axis_size("wide") // 2
    rounds = 0
    while bit >= 1:
        if bit == 1 and holds:
            (block,) = tie([block], *holds)
        upper = (mine & bit) > 0
        got = swap(block, "wide", bit)
        block = jnp.concatenate(
            [jnp.where(upper, got, block), jnp.where(upper, block, got)], axis=0
        )
        bit //= 2
        rounds += 1
    block = block.reshape((2,) * rounds + (rows, width))
    block = block.transpose(tuple(range(rounds))[::-1] + (rounds, rounds + 1))
    return block.reshape((1 << rounds) * rows, width)


def gather_narrow(values, *holds):
    near = swap(values, "narrow", 1)
    far = swap(values, "narrow", 2)
    held = tie([far], *holds)[0] if holds else far
    return [values, near, far, swap(held, "narrow", 1)]


def scatter_begin(pieces):
    near_one = swap(pieces[1], "narrow", 1)
    near_three = swap(pieces[3], "narrow", 1)
    crossing = (pieces[2].astype(f32) + near_three.astype(f32)).astype(bf16)
    return pieces[0], near_one, crossing


def scatter_end(own, near_one, crossing):
    far = swap(crossing, "narrow", 2)
    return add_three(own, near_one, far)


def add_three(own, near_one, far):
    return (own.astype(f32) + near_one.astype(f32) + far.astype(f32)).astype(bf16)


def exchange_narrow(pieces):
    return [pieces[0]] + [swap(pieces[i], "narrow", i) for i in (1, 2, 3)]


def to_owners(values):
    return lax.all_to_all(values, "wide", split_axis=0, concat_axis=0, tiled=True)


def wide_parts(block):
    count = lax.axis_size("wide")
    rows, width = block.shape
    parts = to_owners(block.reshape(count, rows // count, width))
    return jnp.sum(parts.astype(f32), axis=0).astype(bf16)


def wide_whole(mine):
    count = lax.axis_size("wide")
    whole = to_owners(jnp.broadcast_to(mine[None], (count,) + mine.shape))
    return whole.reshape((count * mine.shape[0],) + mine.shape[1:])


def dot(left, right, dims=((1,), (0,))):
    return lax.dot_general(left, right, (dims, ((), ())), preferred_element_type=f32)


def forward_kernel(
    rank_ref, x0, x1, x2, x3, gain_ref, wq0, wk0, wv0, wq1, wk1, wv1, bias_ref, *rest, rows, heads, first
):
    if not first:
        rest = rest[5:]
    normed_ref, qkv_ref, raised_ref, inverse_ref, out_ref, p0, p1, p2, p3 = rest[:9]
    q_ref, v_ref, base_ref, wide_ref, scores_ref, sums_ref = rest[9:]
    rank = rank_ref[0]
    length = 4 * rows
    span = bias_ref.shape[-1]

    @pl.when(pl.program_id(0) == 0)
    def _():
        for i, x_ref in enumerate((x0, x1, x2, x3)):
            x = x_ref[...].astype(f32)
            scale = lax.rsqrt(jnp.mean(x * x, axis=-1, keepdims=True) + epsilon)
            place = pl.multiple_of((rank ^ i) * rows, rows)
            normed_ref[0, pl.ds(place, rows), :] = (x * scale * gain_ref[...]).astype(bf16)
        whole = jnp.concatenate([w[...] for w in (wq0, wq1, wk0, wk1, wv0, wv1)], axis=1)
        wide_ref[...] = dot(whole, normed_ref[0], ((0,), (1,)))

    head = qkv_ref.shape[3]
    h = pl.program_id(0)
    lanes = wq0.shape[1]
    place = jnp.where(h < heads - 1, h * head, lanes + lax.rem(rank, 2) * head)
    part = lambda c: pl.ds(pl.multiple_of(c * (lanes + 128) + place, head), head)
    queries = wide_ref[part(0), :] * (head ** -0.5)
    values = wide_ref[part(2), :]
    q_ref[...] = queries.T.astype(bf16)
    v_ref[...] = values.T.astype(bf16)
    qkv_ref[0, 0, 0] = queries.astype(bf16)
    qkv_ref[0, 0, 1] = wide_ref[part(1), :].astype(bf16)
    qkv_ref[0, 0, 2] = values.astype(bf16)
    base_ref[...] = pltpu.roll(
        jnp.broadcast_to(bias_ref[0], (128, span)), 0, axis=1, stride=1, stride_axis=0
    )
    keys = qkv_ref[0, 0, 1]
    values = v_ref[...]
    top = length - 128
    step = 256
    blocks = length // step
    scores_ref[0] = dot(q_ref[0:step, :], keys)
    for b in range(blocks):
        if b + 1 < blocks:
            scores_ref[(b + 1) % 2] = dot(q_ref[(b + 1) * step : (b + 2) * step, :], keys)
        for k in range(0, step, strip):
            row = b * step + k
            place = top - row // 128 * 128
            line = row % 128
            scores = (
                scores_ref[b % 2, k : k + strip, :]
                + base_ref[line : line + strip, place : place + length]
            )
            raised = jnp.exp(scores - jnp.max(scores, axis=1, keepdims=True))
            total = jnp.sum(raised, axis=1, keepdims=True)
            sums_ref[k : k + strip, :] = jnp.broadcast_to(1.0 / total, (strip, 128))
            raised_ref[0, 0, row : row + strip, :] = raised.astype(bf16)
        inverse = sums_ref[...]
        attended = dot(raised_ref[0, 0, b * step : (b + 1) * step, :], values) * inverse[:, :head]
        out_ref[0, 0, :, b * step : (b + 1) * step] = attended.T.astype(bf16)
        inverse_ref[0, 0, :, b * step : (b + 1) * step] = inverse.T[:8]
    for i, p_ref in enumerate((p0, p1, p2, p3)):
        p_ref[...] = out_ref[0, 0, :, pl.ds(pl.multiple_of((rank ^ i) * rows, rows), rows)]


def attend(rank, blocks, gain, weights, bias_rows, previous, seq, groups):
    rows, width = blocks[0].shape
    heads, _, span = bias_rows.shape
    head = width // (4 * heads)
    length = 4 * rows
    first = previous is None
    whole = lambda h, r: (0, 0)
    low = 4 * (heads - 1) * head // 128
    lanes = (heads - 1) * head
    in_specs = [pl.BlockSpec((rows, width), whole)] * 4 + [
        pl.BlockSpec((1, width), whole),
        *[pl.BlockSpec((width, lanes), lambda h, r: (0, r[0]))] * 3,
        *[pl.BlockSpec((width, 128), lambda h, r: (0, low + lax.div(r[0], 2)))] * 3,
        pl.BlockSpec((1, 1, span), lambda h, r: (h, 0, 0)),
    ]
    args = list(blocks) + [gain] + list(weights) * 2 + [bias_rows]
    aliases = {}
    if not first:
        aliases = {1 + len(args) + k: k for k in range(5)}
        in_specs = in_specs + [pl.BlockSpec(memory_space=pl.ANY)] * 5
        args = args + list(previous)
    out_shape = [
        jax.ShapeDtypeStruct((groups, length, width), bf16),
        jax.ShapeDtypeStruct((groups, heads, 3, head, length), bf16),
        jax.ShapeDtypeStruct((groups, heads, length, length), bf16),
        jax.ShapeDtypeStruct((groups, heads, 8, length), f32),
        jax.ShapeDtypeStruct((groups, heads, head, length), bf16),
    ] + [jax.ShapeDtypeStruct((heads * head, rows), bf16)] * 4
    out_specs = [
        pl.BlockSpec((1, length, width), lambda h, r: (seq, 0, 0)),
        pl.BlockSpec((1, 1, 3, head, length), lambda h, r: (seq, h, 0, 0, 0)),
        pl.BlockSpec((1, 1, length, length), lambda h, r: (seq, h, 0, 0)),
        pl.BlockSpec((1, 1, 8, length), lambda h, r: (seq, h, 0, 0)),
        pl.BlockSpec((1, 1, head, length), lambda h, r: (seq, h, 0, 0)),
    ] + [pl.BlockSpec((head, rows), lambda h, r: (h, 0))] * 4
    outs = pl.pallas_call(
        functools.partial(forward_kernel, rows=rows, heads=heads, first=first),
        grid_spec=pltpu.PrefetchScalarGridSpec(
            num_scalar_prefetch=1,
            grid=(heads,),
            in_specs=in_specs,
            out_specs=out_specs,
            scratch_shapes=[
                pltpu.VMEM((length, head), bf16),
                pltpu.VMEM((length, head), bf16),
                pltpu.VMEM((128, span), f32),
                pltpu.VMEM((3 * (lanes + 128), length), f32),
                pltpu.VMEM((2, 256, length), f32),
                pltpu.VMEM((256, 128), f32),
            ],
        ),
        out_shape=out_shape,
        input_output_aliases=aliases,
        compiler_params=pltpu.CompilerParams(vmem_limit_bytes=vmem_bytes),
        cost_estimate=pl.CostEstimate(
            flops=(18 if first else 18) * heads * length * length * 256, bytes_accessed=8_000_000, transcendentals=0
        ),
        name="attention_forward",
    )(rank, *args)
    return outs[:5], outs[5:]


def backward_kernel(
    rank_ref, g0, g1, g2, g3, qkv_ref, raised_ref, inverse_ref, out_ref, normed_ref,
    d0, d1, d2, d3, weight_grad_ref, bias_ref,
    grad_ref, left_ref, right_ref, key_ref, scores_ref, packed_ref, total_ref, offsets_ref, inner_ref, *, rows
):
    rank = rank_ref[0]
    length = 4 * rows
    head = grad_ref.shape[0]
    step_id = pl.program_id(0)
    h = pl.program_id(1)
    for i, g_ref in enumerate((g0, g1, g2, g3)):
        grad_ref[:, pl.ds(pl.multiple_of((rank ^ i) * rows, rows), rows)] = g_ref[...].astype(f32)
    scaled = grad_ref[...] * inverse_ref[0, 0, 0:1, :]
    shift = jnp.sum(scaled * out_ref[0, 0].astype(f32), axis=0, keepdims=True)
    high = shift.astype(bf16).astype(f32)
    scaled_low = scaled.astype(bf16)
    tail = jnp.concatenate(
        [high, shift - high, jnp.zeros((128 - head - 2, length), f32)], axis=0
    )
    left_ref[...] = jnp.concatenate([scaled_low.astype(f32), tail], axis=0).T.astype(bf16)
    right_ref[0:head, :] = qkv_ref[0, 0, 2]
    right_ref[head:, :] = jnp.where(
        lax.broadcasted_iota(jnp.int32, (128 - head, length), 0) < 2, -1.0, 0.0
    ).astype(bf16)
    key_ref[...] = qkv_ref[0, 0, 1].astype(f32).T.astype(bf16)

    @pl.when(step_id == 0)
    def _():
        offsets_ref[h] = jnp.zeros(offsets_ref.shape[1:], f32)
        total_ref[h] = jnp.zeros(total_ref.shape[1:], f32)

    top = length - 128
    step = 256
    blocks = length // step
    inner_ref[0] = dot(left_ref[0:step, :], right_ref[...])
    for b in range(blocks):
        if b + 1 < blocks:
            inner_ref[(b + 1) % 2] = dot(left_ref[(b + 1) * step : (b + 2) * step, :], right_ref[...])
        for k in range(0, step, strip):
            row = b * step + k
            place = top - row // 128 * 128
            line = row % 128
            grads = raised_ref[0, 0, row : row + strip, :].astype(f32) * inner_ref[b % 2, k : k + strip, :]
            offsets_ref[h, line : line + strip, place : place + length] += grads
            scores_ref[row : row + strip, :] = grads.astype(bf16)
    packed_ref[0:head, :] = (dot(scores_ref[...], key_ref[...]) * (head ** -0.5)).T.astype(bf16)
    packed_ref[head : 2 * head, :] = dot(qkv_ref[0, 0, 0], scores_ref[...]).astype(bf16)
    packed_ref[2 * head :, :] = dot(scaled_low, raised_ref[0, 0]).astype(bf16)
    for i, d_ref in enumerate((d0, d1, d2, d3)):
        d_ref[...] = packed_ref[:, pl.ds(pl.multiple_of((rank ^ i) * rows, rows), rows)]
    total_ref[h] += dot(packed_ref[...], normed_ref[0])

    @pl.when(step_id == pl.num_programs(0) - 1)
    def _():
        weight_grad_ref[pl.ds(pl.multiple_of(h * 3 * head, head), 3 * head), :] = total_ref[
            h
        ].astype(bf16)
        span = offsets_ref.shape[2]
        folded = offsets_ref[h]
        half = 64
        while half >= 8:
            folded = folded[:half] + pltpu.roll(folded[half : 2 * half], span - half, axis=1)
            half //= 2
        bias_ref[h] = folded


def attend_back(rank, grads, saved, first, count):
    normed, qkv, raised, inverse, out = saved
    groups, length, width = normed.shape
    head = qkv.shape[3]
    rows = length // 4
    span = 2 * length
    per_head = lambda *dims: pl.BlockSpec((1, 1) + dims, lambda s, h, r: (s, first + h) + (0,) * len(dims))
    whole = lambda *dims: pl.BlockSpec(dims, lambda s, h, r: (0,) * len(dims))
    outs = pl.pallas_call(
        functools.partial(backward_kernel, rows=rows),
        grid_spec=pltpu.PrefetchScalarGridSpec(
            num_scalar_prefetch=1,
            grid=(groups, count),
            in_specs=[pl.BlockSpec((head, rows), lambda s, h, r: (h, s))] * 4
            + [
                per_head(3, head, length),
                per_head(length, length),
                per_head(8, length),
                per_head(head, length),
                pl.BlockSpec((1, length, width), lambda s, h, r: (s, 0, 0)),
            ],
            out_specs=[pl.BlockSpec((3 * head, rows), lambda s, h, r: (h, s))] * 4
            + [whole(3 * head * count, width), whole(count, 8, span)],
            scratch_shapes=[
                pltpu.VMEM((head, length), f32),
                pltpu.VMEM((length, 128), bf16),
                pltpu.VMEM((128, length), bf16),
                pltpu.VMEM((length, head), bf16),
                pltpu.VMEM((length, length), bf16),
                pltpu.VMEM((3 * head, length), bf16),
                pltpu.VMEM((count, 3 * head, width), f32),
                pltpu.VMEM((count, 128, span), f32),
                pltpu.VMEM((2, 256, length), f32),
            ],
        ),
        out_shape=[jax.ShapeDtypeStruct((3 * head * count, groups * rows), bf16)] * 4
        + [
            jax.ShapeDtypeStruct((3 * head * count, width), bf16),
            jax.ShapeDtypeStruct((count, 8, span), f32),
        ],
        compiler_params=pltpu.CompilerParams(vmem_limit_bytes=vmem_bytes),
        cost_estimate=pl.CostEstimate(
            flops=11_000_000_000 * count, bytes_accessed=10_000_000 * count, transcendentals=0
        ),
        name="attention_backward",
    )(rank, *grads, qkv, raised, inverse, out, normed)
    return outs[:4], outs[4], outs[5]


def out_weight_kernel(
    rank_ref, b0, b1, b2, b3, out_ref, last_ref, extra_ref, bucket_ref, *rest
):
    bias_refs, (grad_ref, whole_ref, total_ref) = rest[:-3], rest[-3:]
    rank = rank_ref[0]
    rows, width = b0.shape
    count = last_ref.shape[0]
    for i, b_ref in enumerate((b0, b1, b2, b3)):
        whole_ref[pl.ds(pl.multiple_of((rank ^ i) * rows, rows), rows), :] = b_ref[...]
    part = dot(out_ref[0].reshape(count, 4 * rows), whole_ref[...])

    @pl.when(pl.program_id(0) == 0)
    def _():
        total_ref[...] = part

    @pl.when(pl.program_id(0) > 0)
    def _():
        total_ref[...] += part

    @pl.when(pl.program_id(0) == pl.num_programs(0) - 1)
    def _():
        grad_ref[:count, :width] = last_ref[...]
        grad_ref[count:, :width] = total_ref[...].astype(bf16)
        place = extra_ref.shape[0]
        grad_ref[:place, width:] = extra_ref[...].astype(bf16)
        grad_ref[place:, width:] = jnp.zeros((2 * count - place, extra_ref.shape[1]), bf16)
        for bias_ref in bias_refs:
            for h in range(bias_ref.shape[0]):
                folded, half = bias_ref[h], 4
                while half >= 1:
                    span = folded.shape[1]
                    folded = folded[:half] + pltpu.roll(folded[half : 2 * half], span - half, axis=1)
                    half //= 2
                folded = jnp.broadcast_to(folded, (16, span))
                high = folded.astype(bf16)
                low = (folded - high.astype(f32)).astype(bf16)
                buckets = dot(high, bucket_ref[...], ((1,), (1,))) + dot(
                    low, bucket_ref[...], ((1,), (1,))
                )
                grad_ref[place : place + 16, width : width + 128] = buckets.astype(bf16)
                place += 16


def out_weight_rows(rank, blocks, out, last, extra, bucket_hot, biases):
    groups, heads, head, length = out.shape
    count, width = last.shape
    rows = length // 4
    lanes = width + extra.shape[1]
    whole = lambda v: pl.BlockSpec(v.shape, lambda s, r: (0,) * v.ndim)
    return pl.pallas_call(
        out_weight_kernel,
        grid_spec=pltpu.PrefetchScalarGridSpec(
            num_scalar_prefetch=1,
            grid=(groups,),
            in_specs=[pl.BlockSpec((rows, width), lambda s, r: (s, 0))] * 4
            + [pl.BlockSpec((1, heads, head, length), lambda s, r: (s, 0, 0, 0))]
            + [whole(v) for v in [last, extra, bucket_hot] + biases],
            out_specs=pl.BlockSpec((2 * count, lanes), lambda s, r: (0, 0)),
            scratch_shapes=[pltpu.VMEM((length, width), bf16), pltpu.VMEM((count, width), f32)],
        ),
        out_shape=jax.ShapeDtypeStruct((2 * count, lanes), bf16),
        compiler_params=pltpu.CompilerParams(vmem_limit_bytes=vmem_bytes),
        cost_estimate=pl.CostEstimate(
            flops=3_000_000_000, bytes_accessed=5_000_000, transcendentals=0
        ),
        name="out_weight_rows",
    )(rank, *blocks, out, last, extra, bucket_hot, *biases)


def head_place(rank, h, heads):
    return rank * (heads - 1) + h if h < heads - 1 else 4 * (heads - 1) + rank


def turn_kernel(rank_ref, *refs, heads, part):
    blocks, weight_refs, before_ref, rest = refs[0:4], refs[4:7], refs[7], refs[8:]
    rank = rank_ref[0]
    if part:
        q_ref, k_ref, v_ref, norm_ref, out_ref, router_ref, norm2_ref, bias_ref = rest[3:-2]
        gathered_ref, total_ref = rest[-2:]
    else:
        q_ref, k_ref, v_ref, norm_ref, gathered_ref, total_ref = rest
    count = heads - 1 if part == 0 else 1
    width = q_ref.shape[0]
    head = width // (4 * heads)

    @pl.when(pl.program_id(0) == 0)
    def _():
        total_ref[...] = jnp.zeros_like(total_ref)
        for i in range(4):
            for h in range(count):
                place = pl.multiple_of(((rank ^ i) * count + h) * head, head)
                for c in range(3):
                    gathered_ref[c, pl.ds(place, head), :] = blocks[i][
                        (3 * h + c) * head : (3 * h + c + 1) * head, :width
                    ].astype(f32)
            if part:
                for h in range(heads):
                    place = head_place(rank ^ i, h, heads)
                    start = (3 + h) * head
                    out_ref[pl.ds(pl.multiple_of(place * head, head), head), :] = blocks[i][
                        start : start + head, :width
                    ].astype(f32)
                    start = 2 * 3 * head - (heads - h) * 16
                    bias = blocks[i][start : start + 16, width : width + 128].astype(f32)
                    bias_ref[pl.ds(place, 1), :] = bias[:1, : bias_ref.shape[1]]
        if part:
            experts = router_ref.shape[0]
            spare = 2 * 3 * head - 16 * heads
            for j, (row, lane) in enumerate(extra_places(experts, width, spare)):
                here = (slice(row, row + experts + 8), slice(width + lane, width + lane + 128))
                total = blocks[0][here].astype(f32)
                for i in range(1, 4):
                    total += blocks[i][here].astype(f32)
                router_ref[:, j * 128 : (j + 1) * 128] = total[:experts]
                norm2_ref[:, j * 128 : (j + 1) * 128] = total[experts:]

    place = pl.multiple_of(pl.program_id(0) * 128, 128)
    for c, grad_ref in enumerate((q_ref, k_ref, v_ref)):
        grads = gathered_ref[c, pl.ds(place, 128), :].T
        grad_ref[...] = grads
        total_ref[...] += grads * weight_refs[c][...].astype(f32)

    @pl.when(pl.program_id(0) == pl.num_programs(0) - 1)
    def _():
        norm_ref[...] = before_ref[...] + jnp.sum(total_ref[...].T, axis=0, keepdims=True)


def turn(rank, blocks, weights, previous, heads, part, experts=0, buckets=0):
    width = weights[0].shape[0]
    head = width // (4 * heads)
    count = heads - 1 if part == 0 else 1
    first = 0 if part == 0 else 4 * (heads - 1) * head // 128
    column = pl.BlockSpec((width, 128), lambda s, r: (0, first + s))
    whole = lambda *dims: pl.BlockSpec(dims, lambda s, r: (0,) * len(dims))
    in_specs = [whole(*b.shape) for b in blocks]
    in_specs += [column] * 3 + [whole(8, width)]
    before = jnp.zeros((8, width), f32) if part == 0 else previous[3]
    args = list(blocks) + list(weights) + [before]
    out_shape = [jax.ShapeDtypeStruct((width, width), f32)] * 3
    out_shape += [jax.ShapeDtypeStruct((8, width), f32)]
    out_specs = [column] * 3 + [whole(8, width)]
    aliases = {}
    if part:
        aliases = {1 + len(args) + k: k for k in range(3)}
        in_specs += [pl.BlockSpec(memory_space=pl.ANY)] * 3
        args += list(previous[:3])
        for dims in ((width, width), (experts, width), (8, width), (4 * heads, buckets)):
            out_shape.append(jax.ShapeDtypeStruct(dims, f32))
            out_specs.append(whole(*dims))
    return pl.pallas_call(
        functools.partial(turn_kernel, heads=heads, part=part),
        grid_spec=pltpu.PrefetchScalarGridSpec(
            num_scalar_prefetch=1,
            grid=(4 * count * head // 128,),
            in_specs=in_specs,
            out_specs=out_specs,
            scratch_shapes=[
                pltpu.VMEM((3, 4 * count * head, width), f32),
                pltpu.VMEM((width, 128), f32),
            ],
        ),
        out_shape=out_shape,
        input_output_aliases=aliases,
        compiler_params=pltpu.CompilerParams(vmem_limit_bytes=vmem_bytes),
        cost_estimate=pl.CostEstimate(
            flops=3_000_000_000 * count, bytes_accessed=3_000_000 * count, transcendentals=0
        ),
        name="weight_gradient_turn",
    )(rank, *args)


def input_kernel(rank_ref, *refs, heads):
    pieces, weight_refs = refs[:8], refs[8:11]
    x_ref, grad_ref, gain_ref, out_ref, gathered_ref = refs[11:]
    rank = rank_ref[0]
    head = pieces[4].shape[0] // 3
    for i in range(4):
        for h in range(heads):
            place = pl.multiple_of(head_place(rank ^ i, h, heads) * head, head)
            source, k = (pieces[i], h) if h < heads - 1 else (pieces[4 + i], 0)
            for c in range(3):
                gathered_ref[c, pl.ds(place, head), :] = source[
                    (3 * k + c) * head : (3 * k + c + 1) * head, :
                ]
    total = dot(gathered_ref[0], weight_refs[0][...], ((0,), (1,)))
    total += dot(gathered_ref[1], weight_refs[1][...], ((0,), (1,)))
    total += dot(gathered_ref[2], weight_refs[2][...], ((0,), (1,)))
    x = x_ref[...].astype(f32)
    scale = lax.rsqrt(jnp.mean(x * x, axis=-1, keepdims=True) + epsilon)
    unit = x * scale
    scaled = total * gain_ref[...]
    inner_mean = jnp.mean(scaled * unit, axis=-1, keepdims=True)
    out_ref[...] = grad_ref[...] + scale * (scaled - unit * inner_mean)


def input_gradient(rank, pieces, weights, inputs, residual_grad, gain, heads):
    tokens, width = inputs.shape
    half = tokens // 2
    whole = lambda s, r: (0, 0)
    part = pl.BlockSpec((half, width), lambda s, r: (s, 0))
    return pl.pallas_call(
        functools.partial(input_kernel, heads=heads),
        grid_spec=pltpu.PrefetchScalarGridSpec(
            num_scalar_prefetch=1,
            grid=(2,),
            in_specs=[pl.BlockSpec((p.shape[0], half), lambda s, r: (0, s)) for p in pieces]
            + [pl.BlockSpec((width, width), whole)] * 3
            + [part, part, pl.BlockSpec((1, width), whole)],
            out_specs=part,
            scratch_shapes=[pltpu.VMEM((3, width, half), bf16)],
        ),
        out_shape=jax.ShapeDtypeStruct((tokens, width), f32),
        compiler_params=pltpu.CompilerParams(vmem_limit_bytes=vmem_bytes),
        cost_estimate=pl.CostEstimate(
            flops=6_000_000_000, bytes_accessed=9_000_000, transcendentals=0
        ),
        name="input_gradient",
    )(rank, *pieces, *weights, inputs, residual_grad, gain)


def expert_part(expert, rows, grads, into, out_of, router, experts):
    logits = dot(rows, router)
    lanes = lax.broadcasted_iota(jnp.int32, logits.shape, 1)
    logits = jnp.where(lanes < experts, logits, -1e30)
    raised = jnp.exp(logits - jnp.max(logits, axis=1, keepdims=True))
    picked = jnp.sum(jnp.where(lanes == expert, raised, 0.0), axis=1, keepdims=True)
    gate = picked / jnp.sum(raised, axis=1, keepdims=True)

    before = dot(rows, into)
    hidden = dot(grads, out_of, ((1,), (1,)))
    square = before * before
    bend = 0.5 + 0.5 * jnp.tanh(before * (0.7978845608 + (0.7978845608 * 0.044715) * square))
    active = before * bend
    slope = 2.0 * 0.7978845608 + (6.0 * 0.7978845608 * 0.044715) * square
    back = hidden * (bend + active * (1.0 - bend) * slope)
    gate_part = jnp.sum(active * hidden, axis=1, keepdims=True)
    row_part = dot(back.astype(bf16), into, ((1,), (1,))).astype(bf16)
    extra = jnp.where(
        lax.broadcasted_iota(jnp.int32, (rows.shape[0], 128), 1) == 0, gate_part, 0.0
    ).astype(bf16)
    gated = (gate * active).astype(bf16)
    produced = dot(gated, out_of).astype(bf16)
    return row_part, extra, gated, (gate * back).astype(bf16), produced


def expert_kernel(first_ref, *refs, members, experts):
    count = len(members)
    ins, outs = refs[: 6 * count + 1], refs[6 * count + 1 :]
    router_ref = ins[-1]
    for k, e in enumerate(members):
        xa, xb, ga, gb, into_ref, out_of_ref = ins[6 * k : 6 * k + 6]
        rows = jnp.concatenate([xa[...], xb[...]], axis=0)
        grads = jnp.concatenate([ga[...], gb[...]], axis=0)
        row_part, extra, gated, gated_back, produced = expert_part(
            first_ref[0] + e, rows, grads, into_ref[0], out_of_ref[0], router_ref[...], experts
        )
        half, width = xa.shape
        for p in range(2):
            part = slice(p * half, (p + 1) * half)
            d, a, b, y = outs[8 * k + p : 8 * k + 8 : 2]
            d[:, :width] = row_part[part]
            d[:, width:] = extra[part]
            y[...] = produced[part]
            a[...] = gated[part]
            b[...] = gated_back[part]


def run_experts(members, first, rows, grads, into, out_of, router, experts):
    count, width = rows[0][0].shape
    hidden = into.shape[2]
    steps = 2
    half = count // steps
    block = lambda lanes: pl.BlockSpec((half, lanes), lambda s, f: (s, 0))
    shape = lambda lanes: jax.ShapeDtypeStruct((count, lanes), bf16)
    in_specs, args, out_specs, out_shape = [], [], [], []
    for k, e in enumerate(members):
        in_specs += [block(width)] * 2
        in_specs += [block(width)] * 2
        in_specs += [
            pl.BlockSpec((1, width, hidden), functools.partial(lambda e, s, f: (e, 0, 0), e)),
            pl.BlockSpec((1, hidden, width), functools.partial(lambda e, s, f: (e, 0, 0), e)),
        ]
        args += list(rows[k]) + list(grads[k]) + [into, out_of]
        out_specs += [block(width + 128)] * 2 + [block(hidden)] * 4 + [block(width)] * 2
        out_shape += [shape(width + 128)] * 2 + [shape(hidden)] * 4 + [shape(width)] * 2
    outs = pl.pallas_call(
        functools.partial(expert_kernel, members=members, experts=experts),
        grid_spec=pltpu.PrefetchScalarGridSpec(
            num_scalar_prefetch=1,
            grid=(steps,),
            in_specs=in_specs + [pl.BlockSpec(router.shape, lambda s, f: (0, 0))],
            out_specs=out_specs,
        ),
        out_shape=out_shape,
        compiler_params=pltpu.CompilerParams(vmem_limit_bytes=vmem_bytes),
        cost_estimate=pl.CostEstimate(
            flops=8_500_000_000 * len(members), bytes_accessed=9_000_000, transcendentals=0
        ),
        name="experts",
    )(first, *args, router)
    return [[outs[8 * k + 2 * t : 8 * k + 2 * t + 2] for t in range(4)] for k in range(len(members))]


def expert_weight_kernel(*refs, owned):
    into_ref, out_of_ref = refs[-2:]
    whole = lambda parts: jnp.concatenate([p[...] for p in parts], axis=0)
    for e in range(owned):

        @pl.when(pl.program_id(0) == e)
        def _():
            rows, actives, backs, grads = [refs[16 * e + 4 * k : 16 * e + 4 * k + 4] for k in range(4)]
            into_ref[0] = dot(whole(rows), whole(backs), ((0,), (0,)))
            out_of_ref[0] = dot(whole(actives), whole(grads), ((0,), (0,)))


def expert_weight_grads(rows, actives, backs, grads):
    owned = len(rows)
    width, hidden = rows[0][0].shape[1], actives[0][0].shape[1]
    args = []
    for e in range(owned):
        args += list(rows[e]) + list(actives[e]) + list(backs[e]) + list(grads[e])
    whole = lambda v: pl.BlockSpec(v.shape, lambda s: (0, 0))
    return pl.pallas_call(
        functools.partial(expert_weight_kernel, owned=owned),
        grid=(owned,),
        in_specs=[whole(v) for v in args],
        out_specs=[
            pl.BlockSpec((1, width, hidden), lambda s: (s, 0, 0)),
            pl.BlockSpec((1, hidden, width), lambda s: (s, 0, 0)),
        ],
        out_shape=[
            jax.ShapeDtypeStruct((owned, width, hidden), f32),
            jax.ShapeDtypeStruct((owned, hidden, width), f32),
        ],
        compiler_params=pltpu.CompilerParams(vmem_limit_bytes=vmem_bytes),
        cost_estimate=pl.CostEstimate(
            flops=500_000_000, bytes_accessed=500_000, transcendentals=0
        ),
        name="expert_weight_gradients",
    )(*args)


def combine_kernel(
    rank_ref, target_ref, chosen_ref, *refs, owned, experts, spare, heads
):
    rank = rank_ref[0]
    returned = refs[:owned]
    normed_ref, residual_ref, up_ref, router_ref, gain_ref, weight_ref = refs[owned : owned + 6]
    grad_ref, branch_ref = refs[owned + 6 : owned + 8]
    low_refs, last_refs = refs[owned + 8 : owned + 12], refs[owned + 12 : owned + 16]
    extra_ref, turned_ref = refs[owned + 16 :]
    tokens, width = normed_ref.shape
    count = returned[0].shape[0]
    back = jnp.zeros((tokens, width + 128), f32)
    for e in range(owned):
        hot = target_ref[e : e + 1, :] == lax.broadcasted_iota(jnp.int32, (count, tokens), 0)
        back += dot(hot.astype(f32).astype(bf16), returned[e][...], ((0,), (0,)))
    residual = residual_ref[...]
    scale = lax.rsqrt(jnp.mean(residual * residual, axis=-1, keepdims=True) + epsilon)
    unit = residual * scale

    logits = dot(normed_ref[...], router_ref[...])
    lanes = lax.broadcasted_iota(jnp.int32, logits.shape, 1)
    logits = jnp.where(lanes < experts, logits, -1e30)
    raised = jnp.exp(logits - jnp.max(logits, axis=1, keepdims=True))
    probs = raised / jnp.sum(raised, axis=1, keepdims=True)
    hot = (lanes == chosen_ref[...]).astype(f32)
    gate = jnp.sum(probs * hot, axis=1, keepdims=True)
    gate_grad = back[:, width : width + 1]
    logit_grad = (probs * gate_grad * (hot - gate)).astype(bf16)
    normed_grad = dot(logit_grad, router_ref[...], ((1,), (1,))) + gate * back[:, :width]
    scaled = normed_grad * gain_ref[...]
    inner_mean = jnp.mean(scaled * unit, axis=-1, keepdims=True)
    grads = up_ref[...].astype(f32) + scale * (scaled - unit * inner_mean)
    grad_ref[...] = grads
    branch = grads.astype(bf16)
    branch_ref[...] = branch
    turned_ref[...] = dot(weight_ref[...], branch, ((1,), (1,))).astype(bf16)
    head = weight_ref.shape[0] // (4 * heads)
    for i in range(4):
        for h in range(heads):
            place = pl.multiple_of(head_place(rank ^ i, h, heads) * head, head)
            g_ref, k = (low_refs[i], h) if h < heads - 1 else (last_refs[i], 0)
            g_ref[k * head : (k + 1) * head, :] = turned_ref[pl.ds(place, head), :]
    router_part = dot(logit_grad, normed_ref[...], ((0,), (0,)))
    norm_part = jnp.broadcast_to(jnp.sum(normed_grad * unit, axis=0, keepdims=True), (8, width))

    extra = jnp.concatenate([router_part[:experts], norm_part], axis=0)
    places = extra_places(experts, width, spare)

    @pl.when(pl.program_id(0) == 0)
    def _():
        extra_ref[...] = jnp.zeros_like(extra_ref)

    for j, (row, lane) in enumerate(places):
        extra_ref[row : row + experts + 8, lane : lane + 128] += extra[:, j * 128 : (j + 1) * 128]


def extra_places(experts, width, spare):
    count = spare // (experts + 8)
    return [((j % count) * (experts + 8), j // count * 128) for j in range(width // 128)]


def combine(rank, targets, chosen, returned, normed, residual, upstream, router, gain, weights, experts, spare, heads):
    tokens, width = residual.shape
    half = tokens // 2
    owned = len(returned)
    whole = lambda v: pl.BlockSpec(v.shape, lambda s, r: (0, 0))
    part = pl.BlockSpec((half, width), lambda s, r: (s, 0))
    lanes = extra_places(experts, width, spare)[-1][1] + 128
    columns = weights.shape[0] // 4
    head = columns // heads
    outs = pl.pallas_call(
        functools.partial(combine_kernel, owned=owned, experts=experts, spare=spare, heads=heads),
        grid_spec=pltpu.PrefetchScalarGridSpec(
            num_scalar_prefetch=1,
            grid=(2,),
            in_specs=[
                pl.BlockSpec((targets.shape[0], half), lambda s, r: (0, s)),
                pl.BlockSpec((half, 1), lambda s, r: (s, 0)),
            ]
            + [whole(v) for v in returned]
            + [part] * 3
            + [whole(router), whole(gain), whole(weights)],
            out_specs=[part, part]
            + [pl.BlockSpec((columns - head, half), lambda s, r: (0, s))] * 4
            + [pl.BlockSpec((head, half), lambda s, r: (0, s))] * 4
            + [pl.BlockSpec((spare, lanes), lambda s, r: (0, 0))],
            scratch_shapes=[pltpu.VMEM((weights.shape[0], half), bf16)],
        ),
        out_shape=[
            jax.ShapeDtypeStruct((tokens, width), f32),
            jax.ShapeDtypeStruct((tokens, width), bf16),
        ]
        + [jax.ShapeDtypeStruct((columns - head, tokens), bf16)] * 4
        + [jax.ShapeDtypeStruct((head, tokens), bf16)] * 4
        + [jax.ShapeDtypeStruct((spare, lanes), f32)],
        compiler_params=pltpu.CompilerParams(vmem_limit_bytes=vmem_bytes),
        cost_estimate=pl.CostEstimate(
            flops=6_000_000_000, bytes_accessed=12_000_000, transcendentals=0
        ),
        name="combine",
    )(rank, targets, chosen, *returned, normed, residual, upstream, router, gain, weights)
    return outs[0], outs[1], outs[2:6], outs[6:10], outs[10]


def residual_kernel(rank_ref, *refs, heads, owned, first):
    pieces, (target_ref, x_ref, gain_ref, weight_ref) = refs[:4], refs[4:8]
    before, rest = ((), refs[8:]) if first else (refs[8 : 8 + owned], refs[10 + owned :])
    residual_ref, normed_ref = rest[:2]
    sent_refs, turned_ref = rest[2 : 2 + owned], rest[2 + owned]
    rank = rank_ref[0]
    head = weight_ref.shape[0] // (4 * heads)
    for i in range(4):
        for h in range(heads):
            place = pl.multiple_of(head_place(rank ^ i, h, heads) * head, head)
            turned_ref[pl.ds(place, head), :] = pieces[i][h * head : (h + 1) * head, :]

    residual = x_ref[...].astype(f32) + dot(turned_ref[...], weight_ref[...], ((0,), (0,)))
    residual_ref[...] = residual
    scale = lax.rsqrt(jnp.mean(residual * residual, axis=-1, keepdims=True) + epsilon)
    normed = (residual * scale * gain_ref[...]).astype(bf16)
    normed_ref[...] = normed
    for e in range(owned):
        count = sent_refs[e].shape[0]
        hot = target_ref[e : e + 1, :] == lax.broadcasted_iota(
            jnp.int32, (count, normed.shape[0]), 0
        )
        part = dot(hot.astype(f32).astype(bf16), normed)
        if not first:
            part = part + before[e][...].astype(f32)
        sent_refs[e][...] = part.astype(bf16)


def residual_rows(rank, pieces, targets, inputs, gain, weights, slots, owned, heads, seq, previous):
    tokens, width = inputs.shape
    half = tokens // 2
    whole = lambda v: pl.BlockSpec(v.shape, lambda s, r: (0, 0))
    part = pl.BlockSpec((half, width), lambda s, r: (seq, 0))
    args = list(pieces) + [targets, inputs, gain, weights]
    in_specs = [whole(p) for p in pieces] + [
        pl.BlockSpec((targets.shape[0], half), lambda s, r: (0, seq)),
        part,
        whole(gain),
        whole(weights),
    ]
    aliases = {}
    if previous is not None:
        residual, normed, sent = previous
        in_specs += [whole(v) for v in sent] + [pl.BlockSpec(memory_space=pl.ANY)] * 2
        args += list(sent) + [residual, normed]
        aliases = {len(args) - 1: 0, len(args): 1}
    outs = pl.pallas_call(
        functools.partial(residual_kernel, heads=heads, owned=owned, first=previous is None),
        grid_spec=pltpu.PrefetchScalarGridSpec(
            num_scalar_prefetch=1,
            grid=(1,),
            in_specs=in_specs,
            out_specs=[part, part] + [pl.BlockSpec((slots, width), lambda s, r: (0, 0))] * owned,
            scratch_shapes=[pltpu.VMEM((weights.shape[0], half), bf16)],
        ),
        out_shape=[
            jax.ShapeDtypeStruct((tokens, width), f32),
            jax.ShapeDtypeStruct((tokens, width), bf16),
        ]
        + [jax.ShapeDtypeStruct((slots, width), bf16)] * owned,
        input_output_aliases=aliases,
        compiler_params=pltpu.CompilerParams(vmem_limit_bytes=vmem_bytes),
        cost_estimate=pl.CostEstimate(
            flops=4_000_000_000, bytes_accessed=6_000_000, transcendentals=0
        ),
        name="residual_rows",
    )(rank, *args)
    return outs[0], outs[1], outs[2:]


def on_device(
    block_input, norm1_gain, query_weight, key_weight, value_weight, out_weight,
    relative_bucket_bias, norm2_gain, router_weight, expert_in, expert_out,
    expert_index, slot_index, bucket_table, out_grad,
):
    groups, rows, width = block_input.shape
    tokens = groups * rows
    wide_count = lax.axis_size("wide")
    narrow_count = lax.axis_size("narrow")
    experts = router_weight.shape[1]
    owned = expert_in.shape[0]
    capacity = max(2, (5 * tokens + 4 * experts - 1) // (4 * experts))
    buckets, head_count = relative_bucket_bias.shape
    head = width // head_count
    heads = head_count // narrow_count
    columns = heads * head
    score_scale = head ** (-0.5)
    span = bucket_table.shape[0]
    rank = lax.axis_index("narrow")
    wide_rank = lax.axis_index("wide")
    rank_arg = rank.astype(jnp.int32).reshape(1)
    gain_one = norm1_gain.astype(f32).reshape(1, width)
    gain_two = norm2_gain.astype(f32)

    first_blocks = gather_narrow(block_input[0])

    upstream_low = out_grad.reshape(tokens, width)
    chosen = expert_index.reshape(tokens)
    placed = slot_index.reshape(tokens)
    half = wide_count * capacity
    slots = owned * half
    owner_slot = (chosen // owned) * capacity + placed
    target = jnp.where(placed < capacity, chosen * capacity + placed, -1)
    dispatch = (target[None, :] == jnp.arange(slots, dtype=jnp.int32)[:, None]).astype(bf16)

    everyone = list(range(owned))
    targets = jnp.stack(
        [
            jnp.where((placed < capacity) & (chosen % owned == e), owner_slot, -1)
            for e in everyone
        ]
    )
    targets = jnp.pad(targets, ((0, -owned % 8), (0, 0)), constant_values=-1)

    grad_rows = dot(dispatch, upstream_low).astype(bf16)
    grad_rows = to_owners(grad_rows.reshape(wide_count, owned, capacity, width))

    table_turned = jnp.roll(bucket_table[::-1], -127)
    bucket_hot = (
        table_turned[None, :] == jnp.arange(128, dtype=jnp.int32)[:, None]
    ).astype(bf16)
    bias_turned = relative_bucket_bias.T
    own_bias = jnp.concatenate(
        [
            lax.dynamic_slice_in_dim(bias_turned, rank * (heads - 1), heads - 1, axis=0),
            lax.dynamic_slice_in_dim(bias_turned, narrow_count * (heads - 1) + rank, 1, axis=0),
        ],
        axis=0,
    )
    bias_rows = dot(own_bias, bucket_hot[:buckets]).reshape(heads, 1, span)

    weights = (query_weight, key_weight, value_weight)
    saved = None
    pieces = []
    blocks = first_blocks
    for s in range(groups):
        if s:
            (block,) = tie([block_input[s]], blocks[2])
            blocks = gather_narrow(block, piece[0])
        saved, piece = attend(rank_arg, blocks, gain_one, weights, bias_rows, saved, s, groups)
        pieces.append(exchange_narrow(piece))

    grad_rows = [grad_rows[:, e].reshape(half, width) for e in everyone]
    first_grads = gather_narrow(grad_rows[0])
    rest_grads = [gather_narrow(v) for v in tie(grad_rows[1:], *pieces[-1])]
    grad_rows = [first_grads] + rest_grads
    inputs = block_input.reshape(tokens, width)
    after_rows = None
    for s in range(groups):
        after_rows = residual_rows(
            rank_arg,
            tie(pieces[s], saved[3], *([first_grads[2]] if s else [])),
            targets,
            inputs,
            gain_two.reshape(1, width),
            out_weight,
            half,
            owned,
            heads,
            s,
            after_rows,
        )
    residual, normed_two, sent = after_rows
    sent = list(sent[:1]) + tie(sent[1:], *[v[2] for v in rest_grads])
    own = [to_owners(v.reshape(wide_count, capacity, width)).reshape(half, width) for v in sent]
    lanes = -(-experts // 128) * 128
    router_wide = jnp.pad(router_weight, ((0, 0), (0, lanes - experts)))
    first_expert = (wide_rank * owned).astype(jnp.int32).reshape(1)

    def experts_on(e, rows_in, grads_in):
        return run_experts(
            [e], first_expert, [rows_in], [grads_in], expert_in, expert_out, router_wide, experts
        )[0]

    near, far, near_rows, across = [], [], [], []
    holds = [first_grads[2]]
    for e in everyone:
        if e:
            own[e:] = tie(own[e:], near[-1][0][0])
        near_rows.append(tie([own[e], swap(own[e], "narrow", 1)], *holds))
        across.append(swap(own[e], "narrow", 2))
        near.append(experts_on(e, near_rows[e], grad_rows[e][:2]))
        holds = [near[e][0][0]]
    returned, expert_rows = [], []
    whole = ()
    for e in everyone:
        (there,) = tie([across[e]], far[-1][0][0] if e else near[0][0][0])
        far_rows = tie([there, swap(there, "narrow", 1)], *holds)
        far.append(experts_on(e, far_rows, grad_rows[e][2:]))
        expert_rows.append(near_rows[e] + far_rows)
        begun = scatter_begin(tie(list(near[e][0]) + list(far[e][0]), *whole))
        holds = [begun[2]]
        whole = [scatter_end(*begun)]
        returned.append(to_owners(whole[0].reshape(wide_count, capacity, -1)).reshape(half, -1))
    both = lambda k: [
        tie(list(near[e][k]) + list(far[e][k]), *whole, *returned[:-1]) for e in everyone
    ]
    in_grads, out_grads = expert_weight_grads(expert_rows, both(1), both(2), grad_rows)
    produced = [tie(list(near[e][3]) + list(far[e][3]), *whole) for e in everyone]
    produced = [scatter_begin(v) for v in produced]
    produced = [(own, one, swap(crossing, "narrow", 2)) for own, one, crossing in produced]
    returned = tie(returned, in_grads, out_grads, *[v[2] for v in produced])

    spare = 2 * columns - 16 * heads
    residual_grad, branch_grad, own_grads, last_grads, extra = combine(
        rank_arg,
        targets,
        chosen[:, None],
        returned,
        normed_two,
        residual,
        upstream_low,
        router_wide,
        gain_two.reshape(1, width),
        out_weight,
        experts,
        spare,
        heads,
    )
    grads = exchange_narrow(own_grads)
    last_grads = exchange_narrow(tie(last_grads, grads[2]))
    outs_sum = [add_three(*v) for v in produced]
    fetched = to_owners(
        jnp.stack([o.reshape(wide_count, capacity, width) for o in outs_sum], axis=1)
    ).reshape(slots, width)
    branch_later = tie([branch_grad], grads[2])[0]
    branch = gather_narrow(branch_later)
    low_pieces, early, low_bias = attend_back(rank_arg, grads, saved, 0, heads - 1)
    low_pieces = exchange_narrow(low_pieces)
    early = wide_parts(tie([early], branch[2], fetched)[0])
    last_pieces, late, last_bias = attend_back(rank_arg, last_grads, saved, heads - 1, 1)
    last_pieces = exchange_narrow(last_pieces)
    late = out_weight_rows(
        rank_arg, tie(branch, late, low_pieces[1], low_pieces[2]), saved[4], late, extra, bucket_hot, [low_bias, last_bias]
    )
    (early,) = tie([early], late)
    late = wide_parts(tie([late], early)[0])
    early = doubled(early, *last_pieces)
    late = wide_whole(late)

    near_rows, far_rows = [swap(early, "narrow", i) for i in (1, 2)]
    input_grad = input_gradient(
        rank_arg,
        tie(low_pieces + last_pieces, near_rows),
        weights,
        inputs,
        residual_grad,
        gain_one,
        heads,
    )
    (far_rows,) = tie([far_rows], input_grad)
    early = [early, near_rows, far_rows, swap(far_rows, "narrow", 1)]
    turned = turn(rank_arg, early, weights, None, heads, 0)
    near_rows, far_rows = [swap(late, "narrow", i) for i in (1, 2)]
    fetched = tie([fetched], near_rows)[0]
    block_out = (residual + dot(dispatch, fetched, ((0,), (0,)))).astype(bf16)
    (far_rows,) = tie([far_rows], turned[3], block_out)
    late = [late, near_rows, far_rows, swap(far_rows, "narrow", 1)]
    query_grad, key_grad, value_grad, norm1_grad, out_weight_grad, router_grad, norm2_grad, biases = turn(
        rank_arg, late, weights, turned, heads, 1, experts, buckets
    )

    return (
        block_out.reshape(groups, rows, width),
        input_grad.reshape(groups, rows, width),
        norm1_grad[0] / gain_one[0],
        query_grad,
        key_grad,
        value_grad,
        out_weight_grad,
        biases.T,
        norm2_grad[0],
        router_grad.T,
        in_grads,
        out_grads,
    )


def solution(mesh):
    rows = P("wide", "narrow", None)
    into, out_of = P("wide", None, "narrow"), P("wide", "narrow", None)
    return jax.shard_map(
        on_device,
        mesh=mesh,
        in_specs=(rows,) + (P(),) * 8 + (into, out_of, P("wide", "narrow"), P("wide", "narrow"), P(), rows),
        out_specs=(rows, rows) + (P(),) * 8 + (into, out_of),
        check_vma=False,
    )
```

```python
import functools

import jax
import jax.numpy as jnp
from jax import lax
from jax.experimental import pallas as pl
from jax.experimental.pallas import tpu as pltpu
from jax.sharding import PartitionSpec as P

epsilon = 1e-06
bf16 = jnp.bfloat16
f32 = jnp.float32
vmem_bytes = 60 * 1024 * 1024
strip = 16


def swap(values, axis, bits):
    count = lax.axis_size(axis)
    return lax.ppermute(values, axis, [(j, j ^ bits) for j in range(count)])


def tie(values, *others):
    return list(lax.optimization_barrier((tuple(values), tuple(others)))[0])


def doubled(block, *holds):
    mine = lax.axis_index("wide")
    rows, width = block.shape
    bit = lax.axis_size("wide") // 2
    rounds = 0
    while bit >= 1:
        if bit == 1 and holds:
            (block,) = tie([block], *holds)
        upper = (mine & bit) > 0
        got = swap(block, "wide", bit)
        block = jnp.concatenate(
            [jnp.where(upper, got, block), jnp.where(upper, block, got)], axis=0
        )
        bit //= 2
        rounds += 1
    block = block.reshape((2,) * rounds + (rows, width))
    block = block.transpose(tuple(range(rounds))[::-1] + (rounds, rounds + 1))
    return block.reshape((1 << rounds) * rows, width)


def gather_narrow(values, *holds):
    near = swap(values, "narrow", 1)
    far = swap(values, "narrow", 2)
    held = tie([far], *holds)[0] if holds else far
    return [values, near, far, swap(held, "narrow", 1)]


def scatter_begin(pieces):
    near_one = swap(pieces[1], "narrow", 1)
    near_three = swap(pieces[3], "narrow", 1)
    crossing = (pieces[2].astype(f32) + near_three.astype(f32)).astype(bf16)
    return pieces[0], near_one, crossing


def scatter_end(own, near_one, crossing):
    far = swap(crossing, "narrow", 2)
    return add_three(own, near_one, far)


def add_three(own, near_one, far):
    return (own.astype(f32) + near_one.astype(f32) + far.astype(f32)).astype(bf16)


def exchange_narrow(pieces):
    return [pieces[0]] + [swap(pieces[i], "narrow", i) for i in (1, 2, 3)]


def to_owners(values):
    return lax.all_to_all(values, "wide", split_axis=0, concat_axis=0, tiled=True)


def wide_parts(block):
    count = lax.axis_size("wide")
    rows, width = block.shape
    parts = to_owners(block.reshape(count, rows // count, width))
    return jnp.sum(parts.astype(f32), axis=0).astype(bf16)


def wide_whole(mine):
    count = lax.axis_size("wide")
    whole = to_owners(jnp.broadcast_to(mine[None], (count,) + mine.shape))
    return whole.reshape((count * mine.shape[0],) + mine.shape[1:])


def dot(left, right, dims=((1,), (0,))):
    return lax.dot_general(left, right, (dims, ((), ())), preferred_element_type=f32)


def forward_kernel(
    rank_ref, x0, x1, x2, x3, gain_ref, wq0, wk0, wv0, wq1, wk1, wv1, bias_ref, *rest, rows, heads, first
):
    if not first:
        rest = rest[5:]
    normed_ref, qkv_ref, raised_ref, inverse_ref, out_ref, p0, p1, p2, p3 = rest[:9]
    q_ref, v_ref, base_ref, wide_ref, scores_ref, sums_ref = rest[9:]
    rank = rank_ref[0]
    length = 4 * rows
    span = bias_ref.shape[-1]

    @pl.when(pl.program_id(0) == 0)
    def _():
        for i, x_ref in enumerate((x0, x1, x2, x3)):
            x = x_ref[...].astype(f32)
            scale = lax.rsqrt(jnp.mean(x * x, axis=-1, keepdims=True) + epsilon)
            place = pl.multiple_of((rank ^ i) * rows, rows)
            normed_ref[0, pl.ds(place, rows), :] = (x * scale * gain_ref[...]).astype(bf16)
        whole = jnp.concatenate([w[...] for w in (wq0, wq1, wk0, wk1, wv0, wv1)], axis=1)
        wide_ref[...] = dot(whole, normed_ref[0], ((0,), (1,)))

    head = qkv_ref.shape[3]
    h = pl.program_id(0)
    lanes = wq0.shape[1]
    place = jnp.where(h < heads - 1, h * head, lanes + lax.rem(rank, 2) * head)
    part = lambda c: pl.ds(pl.multiple_of(c * (lanes + 128) + place, head), head)
    queries = wide_ref[part(0), :] * (head ** -0.5)
    values = wide_ref[part(2), :]
    q_ref[...] = queries.T.astype(bf16)
    v_ref[...] = values.T.astype(bf16)
    qkv_ref[0, 0, 0] = queries.astype(bf16)
    qkv_ref[0, 0, 1] = wide_ref[part(1), :].astype(bf16)
    qkv_ref[0, 0, 2] = values.astype(bf16)
    base_ref[...] = pltpu.roll(
        jnp.broadcast_to(bias_ref[0], (128, span)), 0, axis=1, stride=1, stride_axis=0
    )
    keys = qkv_ref[0, 0, 1]
    values = v_ref[...]
    top = length - 128
    step = 256
    blocks = length // step
    scores_ref[0] = dot(q_ref[0:step, :], keys)
    for b in range(blocks):
        if b + 1 < blocks:
            scores_ref[(b + 1) % 2] = dot(q_ref[(b + 1) * step : (b + 2) * step, :], keys)
        for k in range(0, step, strip):
            row = b * step + k
            place = top - row // 128 * 128
            line = row % 128
            scores = (
                scores_ref[b % 2, k : k + strip, :]
                + base_ref[line : line + strip, place : place + length]
            )
            raised = jnp.exp(scores - jnp.max(scores, axis=1, keepdims=True))
            total = jnp.sum(raised, axis=1, keepdims=True)
            sums_ref[k : k + strip, :] = jnp.broadcast_to(1.0 / total, (strip, 128))
            raised_ref[0, 0, row : row + strip, :] = raised.astype(bf16)
        inverse = sums_ref[...]
        attended = dot(raised_ref[0, 0, b * step : (b + 1) * step, :], values) * inverse[:, :head]
        out_ref[0, 0, :, b * step : (b + 1) * step] = attended.T.astype(bf16)
        inverse_ref[0, 0, :, b * step : (b + 1) * step] = inverse.T[:8]
    for i, p_ref in enumerate((p0, p1, p2, p3)):
        p_ref[...] = out_ref[0, 0, :, pl.ds(pl.multiple_of((rank ^ i) * rows, rows), rows)]


def attend(rank, blocks, gain, weights, bias_rows, previous, seq, groups):
    rows, width = blocks[0].shape
    heads, _, span = bias_rows.shape
    head = width // (4 * heads)
    length = 4 * rows
    first = previous is None
    whole = lambda h, r: (0, 0)
    low = 4 * (heads - 1) * head // 128
    lanes = (heads - 1) * head
    in_specs = [pl.BlockSpec((rows, width), whole)] * 4 + [
        pl.BlockSpec((1, width), whole),
        *[pl.BlockSpec((width, lanes), lambda h, r: (0, r[0]))] * 3,
        *[pl.BlockSpec((width, 128), lambda h, r: (0, low + lax.div(r[0], 2)))] * 3,
        pl.BlockSpec((1, 1, span), lambda h, r: (h, 0, 0)),
    ]
    args = list(blocks) + [gain] + list(weights) * 2 + [bias_rows]
    aliases = {}
    if not first:
        aliases = {1 + len(args) + k: k for k in range(5)}
        in_specs = in_specs + [pl.BlockSpec(memory_space=pl.ANY)] * 5
        args = args + list(previous)
    out_shape = [
        jax.ShapeDtypeStruct((groups, length, width), bf16),
        jax.ShapeDtypeStruct((groups, heads, 3, head, length), bf16),
        jax.ShapeDtypeStruct((groups, heads, length, length), bf16),
        jax.ShapeDtypeStruct((groups, heads, 8, length), f32),
        jax.ShapeDtypeStruct((groups, heads, head, length), bf16),
    ] + [jax.ShapeDtypeStruct((heads * head, rows), bf16)] * 4
    out_specs = [
        pl.BlockSpec((1, length, width), lambda h, r: (seq, 0, 0)),
        pl.BlockSpec((1, 1, 3, head, length), lambda h, r: (seq, h, 0, 0, 0)),
        pl.BlockSpec((1, 1, length, length), lambda h, r: (seq, h, 0, 0)),
        pl.BlockSpec((1, 1, 8, length), lambda h, r: (seq, h, 0, 0)),
        pl.BlockSpec((1, 1, head, length), lambda h, r: (seq, h, 0, 0)),
    ] + [pl.BlockSpec((head, rows), lambda h, r: (h, 0))] * 4
    outs = pl.pallas_call(
        functools.partial(forward_kernel, rows=rows, heads=heads, first=first),
        grid_spec=pltpu.PrefetchScalarGridSpec(
            num_scalar_prefetch=1,
            grid=(heads,),
            in_specs=in_specs,
            out_specs=out_specs,
            scratch_shapes=[
                pltpu.VMEM((length, head), bf16),
                pltpu.VMEM((length, head), bf16),
                pltpu.VMEM((128, span), f32),
                pltpu.VMEM((3 * (lanes + 128), length), f32),
                pltpu.VMEM((2, 256, length), f32),
                pltpu.VMEM((256, 128), f32),
            ],
        ),
        out_shape=out_shape,
        input_output_aliases=aliases,
        compiler_params=pltpu.CompilerParams(vmem_limit_bytes=vmem_bytes),
        cost_estimate=pl.CostEstimate(
            flops=(18 if first else 18) * heads * length * length * 256, bytes_accessed=8_000_000, transcendentals=0
        ),
        name="attention_forward",
    )(rank, *args)
    return outs[:5], outs[5:]


def backward_kernel(
    rank_ref, g0, g1, g2, g3, qkv_ref, raised_ref, inverse_ref, out_ref, normed_ref,
    d0, d1, d2, d3, weight_grad_ref, bias_ref,
    grad_ref, left_ref, right_ref, key_ref, scores_ref, packed_ref, total_ref, offsets_ref, inner_ref, *, rows
):
    rank = rank_ref[0]
    length = 4 * rows
    head = grad_ref.shape[0]
    step_id = pl.program_id(0)
    h = pl.program_id(1)
    for i, g_ref in enumerate((g0, g1, g2, g3)):
        grad_ref[:, pl.ds(pl.multiple_of((rank ^ i) * rows, rows), rows)] = g_ref[...].astype(f32)
    scaled = grad_ref[...] * inverse_ref[0, 0, 0:1, :]
    shift = jnp.sum(scaled * out_ref[0, 0].astype(f32), axis=0, keepdims=True)
    high = shift.astype(bf16).astype(f32)
    scaled_low = scaled.astype(bf16)
    tail = jnp.concatenate(
        [high, shift - high, jnp.zeros((128 - head - 2, length), f32)], axis=0
    )
    left_ref[...] = jnp.concatenate([scaled_low.astype(f32), tail], axis=0).T.astype(bf16)
    right_ref[0:head, :] = qkv_ref[0, 0, 2]
    right_ref[head:, :] = jnp.where(
        lax.broadcasted_iota(jnp.int32, (128 - head, length), 0) < 2, -1.0, 0.0
    ).astype(bf16)
    key_ref[...] = qkv_ref[0, 0, 1].astype(f32).T.astype(bf16)

    @pl.when(step_id == 0)
    def _():
        offsets_ref[h] = jnp.zeros(offsets_ref.shape[1:], f32)
        total_ref[h] = jnp.zeros(total_ref.shape[1:], f32)

    top = length - 128
    step = 256
    blocks = length // step
    inner_ref[0] = dot(left_ref[0:step, :], right_ref[...])
    for b in range(blocks):
        if b + 1 < blocks:
            inner_ref[(b + 1) % 2] = dot(left_ref[(b + 1) * step : (b + 2) * step, :], right_ref[...])
        for k in range(0, step, strip):
            row = b * step + k
            place = top - row // 128 * 128
            line = row % 128
            grads = raised_ref[0, 0, row : row + strip, :].astype(f32) * inner_ref[b % 2, k : k + strip, :]
            offsets_ref[h, line : line + strip, place : place + length] += grads
            scores_ref[row : row + strip, :] = grads.astype(bf16)
    packed_ref[0:head, :] = (dot(scores_ref[...], key_ref[...]) * (head ** -0.5)).T.astype(bf16)
    packed_ref[head : 2 * head, :] = dot(qkv_ref[0, 0, 0], scores_ref[...]).astype(bf16)
    packed_ref[2 * head :, :] = dot(scaled_low, raised_ref[0, 0]).astype(bf16)
    for i, d_ref in enumerate((d0, d1, d2, d3)):
        d_ref[...] = packed_ref[:, pl.ds(pl.multiple_of((rank ^ i) * rows, rows), rows)]
    total_ref[h] += dot(packed_ref[...], normed_ref[0])

    @pl.when(step_id == pl.num_programs(0) - 1)
    def _():
        weight_grad_ref[pl.ds(pl.multiple_of(h * 3 * head, head), 3 * head), :] = total_ref[
            h
        ].astype(bf16)
        span = offsets_ref.shape[2]
        folded = offsets_ref[h]
        half = 64
        while half >= 8:
            folded = folded[:half] + pltpu.roll(folded[half : 2 * half], span - half, axis=1)
            half //= 2
        bias_ref[h] = folded


def attend_back(rank, grads, saved, first, count):
    normed, qkv, raised, inverse, out = saved
    groups, length, width = normed.shape
    head = qkv.shape[3]
    rows = length // 4
    span = 2 * length
    per_head = lambda *dims: pl.BlockSpec((1, 1) + dims, lambda s, h, r: (s, first + h) + (0,) * len(dims))
    whole = lambda *dims: pl.BlockSpec(dims, lambda s, h, r: (0,) * len(dims))
    outs = pl.pallas_call(
        functools.partial(backward_kernel, rows=rows),
        grid_spec=pltpu.PrefetchScalarGridSpec(
            num_scalar_prefetch=1,
            grid=(groups, count),
            in_specs=[pl.BlockSpec((head, rows), lambda s, h, r: (h, s))] * 4
            + [
                per_head(3, head, length),
                per_head(length, length),
                per_head(8, length),
                per_head(head, length),
                pl.BlockSpec((1, length, width), lambda s, h, r: (s, 0, 0)),
            ],
            out_specs=[pl.BlockSpec((3 * head, rows), lambda s, h, r: (h, s))] * 4
            + [whole(3 * head * count, width), whole(count, 8, span)],
            scratch_shapes=[
                pltpu.VMEM((head, length), f32),
                pltpu.VMEM((length, 128), bf16),
                pltpu.VMEM((128, length), bf16),
                pltpu.VMEM((length, head), bf16),
                pltpu.VMEM((length, length), bf16),
                pltpu.VMEM((3 * head, length), bf16),
                pltpu.VMEM((count, 3 * head, width), f32),
                pltpu.VMEM((count, 128, span), f32),
                pltpu.VMEM((2, 256, length), f32),
            ],
        ),
        out_shape=[jax.ShapeDtypeStruct((3 * head * count, groups * rows), bf16)] * 4
        + [
            jax.ShapeDtypeStruct((3 * head * count, width), bf16),
            jax.ShapeDtypeStruct((count, 8, span), f32),
        ],
        compiler_params=pltpu.CompilerParams(vmem_limit_bytes=vmem_bytes),
        cost_estimate=pl.CostEstimate(
            flops=11_000_000_000 * count, bytes_accessed=10_000_000 * count, transcendentals=0
        ),
        name="attention_backward",
    )(rank, *grads, qkv, raised, inverse, out, normed)
    return outs[:4], outs[4], outs[5]


def out_weight_kernel(
    rank_ref, b0, b1, b2, b3, out_ref, last_ref, extra_ref, bucket_ref, *rest
):
    bias_refs, (grad_ref, whole_ref, total_ref) = rest[:-3], rest[-3:]
    rank = rank_ref[0]
    rows, width = b0.shape
    count = last_ref.shape[0]
    for i, b_ref in enumerate((b0, b1, b2, b3)):
        whole_ref[pl.ds(pl.multiple_of((rank ^ i) * rows, rows), rows), :] = b_ref[...]
    part = dot(out_ref[0].reshape(count, 4 * rows), whole_ref[...])

    @pl.when(pl.program_id(0) == 0)
    def _():
        total_ref[...] = part

    @pl.when(pl.program_id(0) > 0)
    def _():
        total_ref[...] += part

    @pl.when(pl.program_id(0) == pl.num_programs(0) - 1)
    def _():
        grad_ref[:count, :width] = last_ref[...]
        grad_ref[count:, :width] = total_ref[...].astype(bf16)
        place = extra_ref.shape[0]
        grad_ref[:place, width:] = extra_ref[...].astype(bf16)
        grad_ref[place:, width:] = jnp.zeros((2 * count - place, extra_ref.shape[1]), bf16)
        for bias_ref in bias_refs:
            for h in range(bias_ref.shape[0]):
                folded, half = bias_ref[h], 4
                while half >= 1:
                    span = folded.shape[1]
                    folded = folded[:half] + pltpu.roll(folded[half : 2 * half], span - half, axis=1)
                    half //= 2
                folded = jnp.broadcast_to(folded, (16, span))
                high = folded.astype(bf16)
                low = (folded - high.astype(f32)).astype(bf16)
                buckets = dot(high, bucket_ref[...], ((1,), (1,))) + dot(
                    low, bucket_ref[...], ((1,), (1,))
                )
                grad_ref[place : place + 16, width : width + 128] = buckets.astype(bf16)
                place += 16


def out_weight_rows(rank, blocks, out, last, extra, bucket_hot, biases):
    groups, heads, head, length = out.shape
    count, width = last.shape
    rows = length // 4
    lanes = width + extra.shape[1]
    whole = lambda v: pl.BlockSpec(v.shape, lambda s, r: (0,) * v.ndim)
    return pl.pallas_call(
        out_weight_kernel,
        grid_spec=pltpu.PrefetchScalarGridSpec(
            num_scalar_prefetch=1,
            grid=(groups,),
            in_specs=[pl.BlockSpec((rows, width), lambda s, r: (s, 0))] * 4
            + [pl.BlockSpec((1, heads, head, length), lambda s, r: (s, 0, 0, 0))]
            + [whole(v) for v in [last, extra, bucket_hot] + biases],
            out_specs=pl.BlockSpec((2 * count, lanes), lambda s, r: (0, 0)),
            scratch_shapes=[pltpu.VMEM((length, width), bf16), pltpu.VMEM((count, width), f32)],
        ),
        out_shape=jax.ShapeDtypeStruct((2 * count, lanes), bf16),
        compiler_params=pltpu.CompilerParams(vmem_limit_bytes=vmem_bytes),
        cost_estimate=pl.CostEstimate(
            flops=300_000_000, bytes_accessed=300_000, transcendentals=0
        ),
        name="out_weight_rows",
    )(rank, *blocks, out, last, extra, bucket_hot, *biases)


def head_place(rank, h, heads):
    return rank * (heads - 1) + h if h < heads - 1 else 4 * (heads - 1) + rank


def turn_kernel(rank_ref, *refs, heads, part):
    blocks, weight_refs, before_ref, gain_ref, rest = refs[0:4], refs[4:7], refs[7], refs[8], refs[9:]
    rank = rank_ref[0]
    if part:
        q_ref, k_ref, v_ref, norm_ref, out_ref, router_ref, norm2_ref, bias_ref = rest[3:-2]
        gathered_ref, total_ref = rest[-2:]
    else:
        q_ref, k_ref, v_ref, norm_ref, gathered_ref, total_ref = rest
    count = heads - 1 if part == 0 else 1
    width = q_ref.shape[0]
    head = width // (4 * heads)

    @pl.when(pl.program_id(0) == 0)
    def _():
        total_ref[...] = jnp.zeros_like(total_ref)
        for i in range(4):
            for h in range(count):
                place = pl.multiple_of(((rank ^ i) * count + h) * head, head)
                for c in range(3):
                    gathered_ref[c, pl.ds(place, head), :] = blocks[i][
                        (3 * h + c) * head : (3 * h + c + 1) * head, :width
                    ].astype(f32)
            if part:
                for h in range(heads):
                    place = head_place(rank ^ i, h, heads)
                    start = (3 + h) * head
                    out_ref[pl.ds(pl.multiple_of(place * head, head), head), :] = blocks[i][
                        start : start + head, :width
                    ].astype(f32)
                    start = 2 * 3 * head - (heads - h) * 16
                    bias = blocks[i][start : start + 16, width : width + 128].astype(f32)
                    bias_ref[pl.ds(place, 1), :] = bias[:1, : bias_ref.shape[1]]
        if part:
            experts = router_ref.shape[0]
            spare = 2 * 3 * head - 16 * heads
            for j, (row, lane) in enumerate(extra_places(experts, width, spare)):
                here = (slice(row, row + experts + 8), slice(width + lane, width + lane + 128))
                total = blocks[0][here].astype(f32)
                for i in range(1, 4):
                    total += blocks[i][here].astype(f32)
                router_ref[:, j * 128 : (j + 1) * 128] = total[:experts]
                norm2_ref[j * 128 : (j + 1) * 128] = total[experts : experts + 1].reshape(128)

    place = pl.multiple_of(pl.program_id(0) * 128, 128)
    for c, grad_ref in enumerate((q_ref, k_ref, v_ref)):
        grads = gathered_ref[c, pl.ds(place, 128), :].T
        grad_ref[...] = grads
        total_ref[...] += grads * weight_refs[c][...].astype(f32)

    @pl.when(pl.program_id(0) == pl.num_programs(0) - 1)
    def _():
        total = jnp.sum(total_ref[...].T, axis=0, keepdims=True) / gain_ref[...]
        norm_ref[...] = (before_ref[...] + total).reshape(norm_ref.shape)


def turn(rank, blocks, weights, gain, previous, heads, part, experts=0, buckets=0):
    width = weights[0].shape[0]
    head = width // (4 * heads)
    count = heads - 1 if part == 0 else 1
    first = 0 if part == 0 else 4 * (heads - 1) * head // 128
    column = pl.BlockSpec((width, 128), lambda s, r: (0, first + s))
    whole = lambda *dims: pl.BlockSpec(dims, lambda s, r: (0,) * len(dims))
    in_specs = [whole(*b.shape) for b in blocks]
    in_specs += [column] * 3 + [whole(1, width)] * 2
    before = jnp.zeros((1, width), f32) if part == 0 else previous[3]
    args = list(blocks) + list(weights) + [before, gain]
    norm = (1, width) if part == 0 else (width,)
    out_shape = [jax.ShapeDtypeStruct((width, width), f32)] * 3
    out_shape += [jax.ShapeDtypeStruct(norm, f32)]
    out_specs = [column] * 3 + [whole(*norm)]
    aliases = {}
    if part:
        aliases = {1 + len(args) + k: k for k in range(3)}
        in_specs += [pl.BlockSpec(memory_space=pl.ANY)] * 3
        args += list(previous[:3])
        for dims in ((width, width), (experts, width), (width,), (4 * heads, buckets)):
            out_shape.append(jax.ShapeDtypeStruct(dims, f32))
            out_specs.append(whole(*dims))
    return pl.pallas_call(
        functools.partial(turn_kernel, heads=heads, part=part),
        grid_spec=pltpu.PrefetchScalarGridSpec(
            num_scalar_prefetch=1,
            grid=(4 * count * head // 128,),
            in_specs=in_specs,
            out_specs=out_specs,
            scratch_shapes=[
                pltpu.VMEM((3, 4 * count * head, width), f32),
                pltpu.VMEM((width, 128), f32),
            ],
        ),
        out_shape=out_shape,
        input_output_aliases=aliases,
        compiler_params=pltpu.CompilerParams(vmem_limit_bytes=vmem_bytes),
        cost_estimate=pl.CostEstimate(
            flops=3_000_000_000 * count, bytes_accessed=3_000_000 * count, transcendentals=0
        ),
        name="weight_gradient_turn",
    )(rank, *args)


def input_kernel(rank_ref, *refs, heads):
    pieces, weight_refs = refs[:8], refs[8:11]
    x_ref, grad_ref, gain_ref, out_ref, gathered_ref = refs[11:]
    rank = rank_ref[0]
    head = pieces[4].shape[0] // 3
    for i in range(4):
        for h in range(heads):
            place = pl.multiple_of(head_place(rank ^ i, h, heads) * head, head)
            source, k = (pieces[i], h) if h < heads - 1 else (pieces[4 + i], 0)
            for c in range(3):
                gathered_ref[c, pl.ds(place, head), :] = source[
                    (3 * k + c) * head : (3 * k + c + 1) * head, :
                ]
    total = dot(gathered_ref[0], weight_refs[0][...], ((0,), (1,)))
    total += dot(gathered_ref[1], weight_refs[1][...], ((0,), (1,)))
    total += dot(gathered_ref[2], weight_refs[2][...], ((0,), (1,)))
    x = x_ref[...].astype(f32)
    scale = lax.rsqrt(jnp.mean(x * x, axis=-1, keepdims=True) + epsilon)
    unit = x * scale
    scaled = total * gain_ref[...]
    inner_mean = jnp.mean(scaled * unit, axis=-1, keepdims=True)
    out_ref[...] = grad_ref[...] + scale * (scaled - unit * inner_mean)


def input_gradient(rank, pieces, weights, inputs, residual_grad, gain, heads):
    tokens, width = inputs.shape
    half = tokens // 2
    whole = lambda s, r: (0, 0)
    part = pl.BlockSpec((half, width), lambda s, r: (s, 0))
    return pl.pallas_call(
        functools.partial(input_kernel, heads=heads),
        grid_spec=pltpu.PrefetchScalarGridSpec(
            num_scalar_prefetch=1,
            grid=(2,),
            in_specs=[pl.BlockSpec((p.shape[0], half), lambda s, r: (0, s)) for p in pieces]
            + [pl.BlockSpec((width, width), whole)] * 3
            + [part, part, pl.BlockSpec((1, width), whole)],
            out_specs=part,
            scratch_shapes=[pltpu.VMEM((3, width, half), bf16)],
        ),
        out_shape=jax.ShapeDtypeStruct((tokens, width), f32),
        compiler_params=pltpu.CompilerParams(vmem_limit_bytes=vmem_bytes),
        cost_estimate=pl.CostEstimate(
            flops=6_000_000_000, bytes_accessed=9_000_000, transcendentals=0
        ),
        name="input_gradient",
    )(rank, *pieces, *weights, inputs, residual_grad, gain)


def expert_part(expert, rows, grads, into, out_of, router, experts):
    logits = dot(rows, router)
    lanes = lax.broadcasted_iota(jnp.int32, logits.shape, 1)
    logits = jnp.where(lanes < experts, logits, -1e30)
    raised = jnp.exp(logits - jnp.max(logits, axis=1, keepdims=True))
    picked = jnp.sum(jnp.where(lanes == expert, raised, 0.0), axis=1, keepdims=True)
    gate = picked / jnp.sum(raised, axis=1, keepdims=True)

    before = dot(rows, into)
    hidden = dot(grads, out_of, ((1,), (1,)))
    square = before * before
    bend = 0.5 + 0.5 * jnp.tanh(before * (0.7978845608 + (0.7978845608 * 0.044715) * square))
    active = before * bend
    slope = 2.0 * 0.7978845608 + (6.0 * 0.7978845608 * 0.044715) * square
    back = hidden * (bend + active * (1.0 - bend) * slope)
    gate_part = jnp.sum(active * hidden, axis=1, keepdims=True)
    row_part = dot(back.astype(bf16), into, ((1,), (1,))).astype(bf16)
    extra = jnp.where(
        lax.broadcasted_iota(jnp.int32, (rows.shape[0], 128), 1) == 0, gate_part, 0.0
    ).astype(bf16)
    gated = (gate * active).astype(bf16)
    produced = dot(gated, out_of).astype(bf16)
    return row_part, extra, gated, (gate * back).astype(bf16), produced


def expert_kernel(first_ref, *refs, members, experts):
    count = len(members)
    ins, outs = refs[: 6 * count + 1], refs[6 * count + 1 :]
    router_ref = ins[-1]
    for k, e in enumerate(members):
        xa, xb, ga, gb, into_ref, out_of_ref = ins[6 * k : 6 * k + 6]
        rows = jnp.concatenate([xa[...], xb[...]], axis=0)
        grads = jnp.concatenate([ga[...], gb[...]], axis=0)
        row_part, extra, gated, gated_back, produced = expert_part(
            first_ref[0] + e, rows, grads, into_ref[0], out_of_ref[0], router_ref[...], experts
        )
        half, width = xa.shape
        for p in range(2):
            part = slice(p * half, (p + 1) * half)
            d, a, b, y = outs[8 * k + p : 8 * k + 8 : 2]
            d[:, :width] = row_part[part]
            d[:, width:] = extra[part]
            y[...] = produced[part]
            a[...] = gated[part]
            b[...] = gated_back[part]


def run_experts(members, first, rows, grads, into, out_of, router, experts, cost):
    count, width = rows[0][0].shape
    hidden = into.shape[2]
    steps = 2
    half = count // steps
    block = lambda lanes: pl.BlockSpec((half, lanes), lambda s, f: (s, 0))
    shape = lambda lanes: jax.ShapeDtypeStruct((count, lanes), bf16)
    in_specs, args, out_specs, out_shape = [], [], [], []
    for k, e in enumerate(members):
        in_specs += [block(width)] * 2
        in_specs += [block(width)] * 2
        in_specs += [
            pl.BlockSpec((1, width, hidden), functools.partial(lambda e, s, f: (e, 0, 0), e)),
            pl.BlockSpec((1, hidden, width), functools.partial(lambda e, s, f: (e, 0, 0), e)),
        ]
        args += list(rows[k]) + list(grads[k]) + [into, out_of]
        out_specs += [block(width + 128)] * 2 + [block(hidden)] * 4 + [block(width)] * 2
        out_shape += [shape(width + 128)] * 2 + [shape(hidden)] * 4 + [shape(width)] * 2
    outs = pl.pallas_call(
        functools.partial(expert_kernel, members=members, experts=experts),
        grid_spec=pltpu.PrefetchScalarGridSpec(
            num_scalar_prefetch=1,
            grid=(steps,),
            in_specs=in_specs + [pl.BlockSpec(router.shape, lambda s, f: (0, 0))],
            out_specs=out_specs,
        ),
        out_shape=out_shape,
        compiler_params=pltpu.CompilerParams(vmem_limit_bytes=vmem_bytes),
        cost_estimate=pl.CostEstimate(
            flops=cost, bytes_accessed=cost // 1000, transcendentals=0
        ),
        name="experts",
    )(first, *args, router)
    return [[outs[8 * k + 2 * t : 8 * k + 2 * t + 2] for t in range(4)] for k in range(len(members))]


def expert_weight_kernel(*refs, owned):
    into_ref, out_of_ref = refs[-2:]
    whole = lambda parts: jnp.concatenate([p[...] for p in parts], axis=0)
    for e in range(owned):

        @pl.when(pl.program_id(0) == e)
        def _():
            rows, actives, backs, grads = [refs[16 * e + 4 * k : 16 * e + 4 * k + 4] for k in range(4)]
            into_ref[0] = dot(whole(rows), whole(backs), ((0,), (0,)))
            out_of_ref[0] = dot(whole(actives), whole(grads), ((0,), (0,)))


def expert_weight_grads(rows, actives, backs, grads):
    owned = len(rows)
    width, hidden = rows[0][0].shape[1], actives[0][0].shape[1]
    args = []
    for e in range(owned):
        args += list(rows[e]) + list(actives[e]) + list(backs[e]) + list(grads[e])
    whole = lambda v: pl.BlockSpec(v.shape, lambda s: (0, 0))
    return pl.pallas_call(
        functools.partial(expert_weight_kernel, owned=owned),
        grid=(owned,),
        in_specs=[whole(v) for v in args],
        out_specs=[
            pl.BlockSpec((1, width, hidden), lambda s: (s, 0, 0)),
            pl.BlockSpec((1, hidden, width), lambda s: (s, 0, 0)),
        ],
        out_shape=[
            jax.ShapeDtypeStruct((owned, width, hidden), f32),
            jax.ShapeDtypeStruct((owned, hidden, width), f32),
        ],
        compiler_params=pltpu.CompilerParams(vmem_limit_bytes=vmem_bytes),
        cost_estimate=pl.CostEstimate(
            flops=500_000_000, bytes_accessed=500_000, transcendentals=0
        ),
        name="expert_weight_gradients",
    )(*args)


def combine_kernel(
    rank_ref, target_ref, chosen_ref, *refs, owned, experts, spare, heads
):
    rank = rank_ref[0]
    returned = refs[:owned]
    normed_ref, residual_ref, up_ref, router_ref, gain_ref, weight_ref = refs[owned : owned + 6]
    grad_ref, branch_ref = refs[owned + 6 : owned + 8]
    low_refs, last_refs = refs[owned + 8 : owned + 12], refs[owned + 12 : owned + 16]
    extra_ref, turned_ref = refs[owned + 16 :]
    tokens, width = normed_ref.shape
    count = returned[0].shape[0]
    back = jnp.zeros((tokens, width + 128), f32)
    for e in range(owned):
        hot = target_ref[e : e + 1, :] == lax.broadcasted_iota(jnp.int32, (count, tokens), 0)
        back += dot(hot.astype(f32).astype(bf16), returned[e][...], ((0,), (0,)))
    residual = residual_ref[...]
    scale = lax.rsqrt(jnp.mean(residual * residual, axis=-1, keepdims=True) + epsilon)
    unit = residual * scale

    logits = dot(normed_ref[...], router_ref[...])
    lanes = lax.broadcasted_iota(jnp.int32, logits.shape, 1)
    logits = jnp.where(lanes < experts, logits, -1e30)
    raised = jnp.exp(logits - jnp.max(logits, axis=1, keepdims=True))
    probs = raised / jnp.sum(raised, axis=1, keepdims=True)
    hot = (lanes == chosen_ref[...]).astype(f32)
    gate = jnp.sum(probs * hot, axis=1, keepdims=True)
    gate_grad = back[:, width : width + 1]
    logit_grad = (probs * gate_grad * (hot - gate)).astype(bf16)
    normed_grad = dot(logit_grad, router_ref[...], ((1,), (1,))) + gate * back[:, :width]
    scaled = normed_grad * gain_ref[...]
    inner_mean = jnp.mean(scaled * unit, axis=-1, keepdims=True)
    grads = up_ref[...].astype(f32) + scale * (scaled - unit * inner_mean)
    grad_ref[...] = grads
    branch = grads.astype(bf16)
    branch_ref[...] = branch
    turned_ref[...] = dot(weight_ref[...], branch, ((1,), (1,))).astype(bf16)
    head = weight_ref.shape[0] // (4 * heads)
    for i in range(4):
        for h in range(heads):
            place = pl.multiple_of(head_place(rank ^ i, h, heads) * head, head)
            g_ref, k = (low_refs[i], h) if h < heads - 1 else (last_refs[i], 0)
            g_ref[k * head : (k + 1) * head, :] = turned_ref[pl.ds(place, head), :]
    router_part = dot(logit_grad, normed_ref[...], ((0,), (0,)))
    norm_part = jnp.broadcast_to(jnp.sum(normed_grad * unit, axis=0, keepdims=True), (8, width))

    extra = jnp.concatenate([router_part[:experts], norm_part], axis=0)
    places = extra_places(experts, width, spare)

    @pl.when(pl.program_id(0) == 0)
    def _():
        extra_ref[...] = jnp.zeros_like(extra_ref)

    for j, (row, lane) in enumerate(places):
        extra_ref[row : row + experts + 8, lane : lane + 128] += extra[:, j * 128 : (j + 1) * 128]


def extra_places(experts, width, spare):
    count = spare // (experts + 8)
    return [((j % count) * (experts + 8), j // count * 128) for j in range(width // 128)]


def combine(rank, targets, chosen, returned, normed, residual, upstream, router, gain, weights, experts, spare, heads):
    tokens, width = residual.shape
    half = tokens // 2
    owned = len(returned)
    whole = lambda v: pl.BlockSpec(v.shape, lambda s, r: (0, 0))
    part = pl.BlockSpec((half, width), lambda s, r: (s, 0))
    lanes = extra_places(experts, width, spare)[-1][1] + 128
    columns = weights.shape[0] // 4
    head = columns // heads
    outs = pl.pallas_call(
        functools.partial(combine_kernel, owned=owned, experts=experts, spare=spare, heads=heads),
        grid_spec=pltpu.PrefetchScalarGridSpec(
            num_scalar_prefetch=1,
            grid=(2,),
            in_specs=[
                pl.BlockSpec((targets.shape[0], half), lambda s, r: (0, s)),
                pl.BlockSpec((half, 1), lambda s, r: (s, 0)),
            ]
            + [whole(v) for v in returned]
            + [part] * 3
            + [whole(router), whole(gain), whole(weights)],
            out_specs=[part, part]
            + [pl.BlockSpec((columns - head, half), lambda s, r: (0, s))] * 4
            + [pl.BlockSpec((head, half), lambda s, r: (0, s))] * 4
            + [pl.BlockSpec((spare, lanes), lambda s, r: (0, 0))],
            scratch_shapes=[pltpu.VMEM((weights.shape[0], half), bf16)],
        ),
        out_shape=[
            jax.ShapeDtypeStruct((tokens, width), f32),
            jax.ShapeDtypeStruct((tokens, width), bf16),
        ]
        + [jax.ShapeDtypeStruct((columns - head, tokens), bf16)] * 4
        + [jax.ShapeDtypeStruct((head, tokens), bf16)] * 4
        + [jax.ShapeDtypeStruct((spare, lanes), f32)],
        compiler_params=pltpu.CompilerParams(vmem_limit_bytes=vmem_bytes),
        cost_estimate=pl.CostEstimate(
            flops=6_000_000_000, bytes_accessed=12_000_000, transcendentals=0
        ),
        name="combine",
    )(rank, targets, chosen, *returned, normed, residual, upstream, router, gain, weights)
    return outs[0], outs[1], outs[2:6], outs[6:10], outs[10]


def residual_kernel(rank_ref, *refs, heads, owned, first):
    pieces, (target_ref, x_ref, gain_ref, weight_ref) = refs[:4], refs[4:8]
    before, rest = ((), refs[8:]) if first else (refs[8 : 8 + owned], refs[10 + owned :])
    residual_ref, normed_ref = rest[:2]
    sent_refs, turned_ref = rest[2 : 2 + owned], rest[2 + owned]
    rank = rank_ref[0]
    head = weight_ref.shape[0] // (4 * heads)
    for i in range(4):
        for h in range(heads):
            place = pl.multiple_of(head_place(rank ^ i, h, heads) * head, head)
            turned_ref[pl.ds(place, head), :] = pieces[i][h * head : (h + 1) * head, :]

    residual = x_ref[...].astype(f32) + dot(turned_ref[...], weight_ref[...], ((0,), (0,)))
    residual_ref[...] = residual
    scale = lax.rsqrt(jnp.mean(residual * residual, axis=-1, keepdims=True) + epsilon)
    normed = (residual * scale * gain_ref[...]).astype(bf16)
    normed_ref[...] = normed
    for e in range(owned):
        count = sent_refs[e].shape[0]
        hot = target_ref[e : e + 1, :] == lax.broadcasted_iota(
            jnp.int32, (count, normed.shape[0]), 0
        )
        part = dot(hot.astype(f32).astype(bf16), normed)
        if not first:
            part = part + before[e][...].astype(f32)
        sent_refs[e][...] = part.astype(bf16)


def residual_rows(rank, pieces, targets, inputs, gain, weights, slots, owned, heads, seq, previous):
    tokens, width = inputs.shape
    half = tokens // 2
    whole = lambda v: pl.BlockSpec(v.shape, lambda s, r: (0, 0))
    part = pl.BlockSpec((half, width), lambda s, r: (seq, 0))
    args = list(pieces) + [targets, inputs, gain, weights]
    in_specs = [whole(p) for p in pieces] + [
        pl.BlockSpec((targets.shape[0], half), lambda s, r: (0, seq)),
        part,
        whole(gain),
        whole(weights),
    ]
    aliases = {}
    if previous is not None:
        residual, normed, sent = previous
        in_specs += [whole(v) for v in sent] + [pl.BlockSpec(memory_space=pl.ANY)] * 2
        args += list(sent) + [residual, normed]
        aliases = {len(args) - 1: 0, len(args): 1}
    outs = pl.pallas_call(
        functools.partial(residual_kernel, heads=heads, owned=owned, first=previous is None),
        grid_spec=pltpu.PrefetchScalarGridSpec(
            num_scalar_prefetch=1,
            grid=(1,),
            in_specs=in_specs,
            out_specs=[part, part] + [pl.BlockSpec((slots, width), lambda s, r: (0, 0))] * owned,
            scratch_shapes=[pltpu.VMEM((weights.shape[0], half), bf16)],
        ),
        out_shape=[
            jax.ShapeDtypeStruct((tokens, width), f32),
            jax.ShapeDtypeStruct((tokens, width), bf16),
        ]
        + [jax.ShapeDtypeStruct((slots, width), bf16)] * owned,
        input_output_aliases=aliases,
        compiler_params=pltpu.CompilerParams(vmem_limit_bytes=vmem_bytes),
        cost_estimate=pl.CostEstimate(
            flops=4_000_000_000, bytes_accessed=6_000_000, transcendentals=0
        ),
        name="residual_rows",
    )(rank, *args)
    return outs[0], outs[1], outs[2:]


def on_device(
    block_input, norm1_gain, query_weight, key_weight, value_weight, out_weight,
    relative_bucket_bias, norm2_gain, router_weight, expert_in, expert_out,
    expert_index, slot_index, bucket_table, out_grad,
):
    groups, rows, width = block_input.shape
    tokens = groups * rows
    wide_count = lax.axis_size("wide")
    narrow_count = lax.axis_size("narrow")
    experts = router_weight.shape[1]
    owned = expert_in.shape[0]
    capacity = max(2, (5 * tokens + 4 * experts - 1) // (4 * experts))
    buckets, head_count = relative_bucket_bias.shape
    head = width // head_count
    heads = head_count // narrow_count
    columns = heads * head
    score_scale = head ** (-0.5)
    span = bucket_table.shape[0]
    rank = lax.axis_index("narrow")
    wide_rank = lax.axis_index("wide")
    rank_arg = rank.astype(jnp.int32).reshape(1)
    gain_one = norm1_gain.astype(f32).reshape(1, width)
    gain_two = norm2_gain.astype(f32)

    first_blocks = gather_narrow(block_input[0])

    upstream_low = out_grad.reshape(tokens, width)
    chosen = expert_index.reshape(tokens)
    placed = slot_index.reshape(tokens)
    half = wide_count * capacity
    slots = owned * half
    owner_slot = (chosen // owned) * capacity + placed
    target = jnp.where(placed < capacity, chosen * capacity + placed, -1)
    dispatch = (target[None, :] == jnp.arange(slots, dtype=jnp.int32)[:, None]).astype(bf16)

    everyone = list(range(owned))
    targets = jnp.stack(
        [
            jnp.where((placed < capacity) & (chosen % owned == e), owner_slot, -1)
            for e in everyone
        ]
    )
    targets = jnp.pad(targets, ((0, -owned % 8), (0, 0)), constant_values=-1)

    grad_rows = dot(dispatch, upstream_low).astype(bf16)
    grad_rows = to_owners(grad_rows.reshape(wide_count, owned, capacity, width))

    table_turned = jnp.roll(bucket_table[::-1], -127)
    bucket_hot = (
        table_turned[None, :] == jnp.arange(128, dtype=jnp.int32)[:, None]
    ).astype(bf16)
    bias_turned = relative_bucket_bias.T
    own_bias = jnp.concatenate(
        [
            lax.dynamic_slice_in_dim(bias_turned, rank * (heads - 1), heads - 1, axis=0),
            lax.dynamic_slice_in_dim(bias_turned, narrow_count * (heads - 1) + rank, 1, axis=0),
        ],
        axis=0,
    )
    bias_rows = dot(own_bias, bucket_hot[:buckets]).reshape(heads, 1, span)

    weights = (query_weight, key_weight, value_weight)
    saved = None
    pieces = []
    blocks = first_blocks
    for s in range(groups):
        if s:
            (block,) = tie([block_input[s]], blocks[2])
            blocks = gather_narrow(block, piece[0])
        saved, piece = attend(rank_arg, blocks, gain_one, weights, bias_rows, saved, s, groups)
        pieces.append(exchange_narrow(piece))

    grad_rows = [grad_rows[:, e].reshape(half, width) for e in everyone]
    first_grads = gather_narrow(grad_rows[0])
    rest_grads = [gather_narrow(v) for v in tie(grad_rows[1:], *pieces[-1])]
    grad_rows = [first_grads] + rest_grads
    lanes = -(-experts // 128) * 128
    router_wide = jnp.pad(router_weight, ((0, 0), (0, lanes - experts)))
    inputs = block_input.reshape(tokens, width)
    after_rows = None
    for s in range(groups):
        after_rows = residual_rows(
            rank_arg,
            tie(pieces[s], saved[3], *([first_grads[2], router_wide] if s else [])),
            targets,
            inputs,
            gain_two.reshape(1, width),
            out_weight,
            half,
            owned,
            heads,
            s,
            after_rows,
        )
    residual, normed_two, sent = after_rows
    sent = list(sent[:1]) + tie(sent[1:], *[v[2] for v in rest_grads])
    own = [to_owners(v.reshape(wide_count, capacity, width)).reshape(half, width) for v in sent]
    first_expert = (wide_rank * owned).astype(jnp.int32).reshape(1)

    def experts_on(e, rows_in, grads_in, cost=8_500_000_000):
        return run_experts(
            [e], first_expert, [rows_in], [grads_in], expert_in, expert_out, router_wide, experts, cost
        )[0]

    near, far, returned, expert_rows = [], [], [], []
    holds = [first_grads[2]] + [v[2] for v in rest_grads]
    whole = ()
    for e in everyone:
        if e:
            own[e:] = tie(own[e:], near[-1][0][0])
        near_rows = tie([own[e], swap(own[e], "narrow", 1)], *holds)
        across = swap(own[e], "narrow", 2)
        near.append(experts_on(e, near_rows, grad_rows[e][:2], 3_000_000_000))
        (there,) = tie([across], near[e][0][0])
        far_rows = tie([there, swap(there, "narrow", 1)], *([crossing] if e else []))
        far.append(experts_on(e, far_rows, grad_rows[e][2:], 500_000_000))
        expert_rows.append(near_rows + far_rows)
        begun = scatter_begin(tie(list(near[e][0]) + list(far[e][0]), *whole))
        crossing = begun[2]
        holds = [far[e][0][0]]
        whole = [scatter_end(*begun)]
        returned.append(to_owners(whole[0].reshape(wide_count, capacity, -1)).reshape(half, -1))
    both = lambda k: [
        tie(list(near[e][k]) + list(far[e][k]), *whole, *returned[:-1]) for e in everyone
    ]
    in_grads, out_grads = expert_weight_grads(expert_rows, both(1), both(2), grad_rows)
    produced = [tie(list(near[e][3]) + list(far[e][3]), *whole) for e in everyone]
    produced = [scatter_begin(v) for v in produced]
    produced = [(own, one, swap(crossing, "narrow", 2)) for own, one, crossing in produced]
    returned = tie(returned, in_grads, out_grads, *[v[2] for v in produced])

    spare = 2 * columns - 16 * heads
    residual_grad, branch_grad, own_grads, last_grads, extra = combine(
        rank_arg,
        targets,
        chosen[:, None],
        returned,
        normed_two,
        residual,
        upstream_low,
        router_wide,
        gain_two.reshape(1, width),
        out_weight,
        experts,
        spare,
        heads,
    )
    grads = exchange_narrow(own_grads)
    last_grads = exchange_narrow(tie(last_grads, grads[2]))
    outs_sum = [add_three(*v) for v in produced]
    fetched = to_owners(
        jnp.stack([o.reshape(wide_count, capacity, width) for o in outs_sum], axis=1)
    ).reshape(slots, width)
    branch_later = tie([branch_grad], grads[2])[0]
    branch = gather_narrow(branch_later)
    low_pieces, early, low_bias = attend_back(rank_arg, grads, saved, 0, heads - 1)
    low_pieces = exchange_narrow(low_pieces)
    early = wide_parts(tie([early], branch[2], fetched)[0])
    last_pieces, late, last_bias = attend_back(rank_arg, last_grads, saved, heads - 1, 1)
    last_pieces = exchange_narrow(last_pieces)
    late = out_weight_rows(
        rank_arg, tie(branch, late, low_pieces[1], low_pieces[2]), saved[4], late, extra, bucket_hot, [low_bias, last_bias]
    )
    (early,) = tie([early], late)
    late = wide_parts(tie([late], early)[0])
    early = doubled(early, *last_pieces)
    late = wide_whole(late)

    near_rows, far_rows = [swap(early, "narrow", i) for i in (1, 2)]
    input_grad = input_gradient(
        rank_arg,
        tie(low_pieces + last_pieces, near_rows),
        weights,
        inputs,
        residual_grad,
        gain_one,
        heads,
    )
    (far_rows,) = tie([far_rows], input_grad)
    early = [early, near_rows, far_rows, swap(far_rows, "narrow", 1)]
    turned = turn(rank_arg, early, weights, gain_one, None, heads, 0)
    near_rows, far_rows = [swap(late, "narrow", i) for i in (1, 2)]
    fetched = tie([fetched], near_rows)[0]
    block_out = (residual + dot(dispatch, fetched, ((0,), (0,)))).astype(bf16)
    (far_rows,) = tie([far_rows], turned[3], block_out)
    late = [late, near_rows, far_rows, swap(far_rows, "narrow", 1)]
    query_grad, key_grad, value_grad, norm1_grad, out_weight_grad, router_grad, norm2_grad, biases = turn(
        rank_arg, late, weights, gain_one, turned, heads, 1, experts, buckets
    )

    return (
        block_out.reshape(groups, rows, width),
        input_grad.reshape(groups, rows, width),
        norm1_grad,
        query_grad,
        key_grad,
        value_grad,
        out_weight_grad,
        biases.T,
        norm2_grad,
        router_grad.T,
        in_grads,
        out_grads,
    )


def solution(mesh):
    rows = P("wide", "narrow", None)
    into, out_of = P("wide", None, "narrow"), P("wide", "narrow", None)
    return jax.shard_map(
        on_device,
        mesh=mesh,
        in_specs=(rows,) + (P(),) * 8 + (into, out_of, P("wide", "narrow"), P("wide", "narrow"), P(), rows),
        out_specs=(rows, rows) + (P(),) * 8 + (into, out_of),
        check_vma=False,
    )
```

```python
import functools

import jax
import jax.numpy as jnp
from jax import lax
from jax.experimental import pallas as pl
from jax.experimental.pallas import tpu as pltpu
from jax.sharding import PartitionSpec as P

epsilon = 1e-06
bf16 = jnp.bfloat16
f32 = jnp.float32
vmem_bytes = 60 * 1024 * 1024
strip = 16


def swap(values, axis, bits):
    count = lax.axis_size(axis)
    return lax.ppermute(values, axis, [(j, j ^ bits) for j in range(count)])


def tie(values, *others):
    return list(lax.optimization_barrier((tuple(values), tuple(others)))[0])


def doubled(block, *holds):
    mine = lax.axis_index("wide")
    rows, width = block.shape
    bit = lax.axis_size("wide") // 2
    rounds = 0
    while bit >= 1:
        if bit == 1 and holds:
            (block,) = tie([block], *holds)
        upper = (mine & bit) > 0
        got = swap(block, "wide", bit)
        block = jnp.concatenate(
            [jnp.where(upper, got, block), jnp.where(upper, block, got)], axis=0
        )
        bit //= 2
        rounds += 1
    block = block.reshape((2,) * rounds + (rows, width))
    block = block.transpose(tuple(range(rounds))[::-1] + (rounds, rounds + 1))
    return block.reshape((1 << rounds) * rows, width)


def gather_narrow(values, *holds):
    near = swap(values, "narrow", 1)
    far = swap(values, "narrow", 2)
    held = tie([far], *holds)[0] if holds else far
    return [values, near, far, swap(held, "narrow", 1)]


def scatter_begin(pieces):
    near_one = swap(pieces[1], "narrow", 1)
    near_three = swap(pieces[3], "narrow", 1)
    crossing = (pieces[2].astype(f32) + near_three.astype(f32)).astype(bf16)
    return pieces[0], near_one, crossing


def scatter_end(own, near_one, crossing):
    far = swap(crossing, "narrow", 2)
    return add_three(own, near_one, far)


def add_three(own, near_one, far):
    return (own.astype(f32) + near_one.astype(f32) + far.astype(f32)).astype(bf16)


def exchange_narrow(pieces):
    return [pieces[0]] + [swap(pieces[i], "narrow", i) for i in (1, 2, 3)]


def to_owners(values):
    return lax.all_to_all(values, "wide", split_axis=0, concat_axis=0, tiled=True)


def wide_parts(block):
    count = lax.axis_size("wide")
    rows, width = block.shape
    parts = to_owners(block.reshape(count, rows // count, width))
    return jnp.sum(parts.astype(f32), axis=0).astype(bf16)


def wide_whole(mine):
    count = lax.axis_size("wide")
    whole = to_owners(jnp.broadcast_to(mine[None], (count,) + mine.shape))
    return whole.reshape((count * mine.shape[0],) + mine.shape[1:])


def dot(left, right, dims=((1,), (0,))):
    return lax.dot_general(left, right, (dims, ((), ())), preferred_element_type=f32)


def forward_kernel(
    rank_ref, x0, x1, x2, x3, gain_ref, wq0, wk0, wv0, wq1, wk1, wv1, bias_ref, *rest, rows, heads, first
):
    if not first:
        rest = rest[6:]
    normed_ref, qkv_ref, raised_ref, inverse_ref, out_ref, exact_ref, p0, p1, p2, p3 = rest[:10]
    q_ref, v_ref, base_ref, wide_ref, scores_ref, sums_ref = rest[10:]
    rank = rank_ref[0]
    length = 4 * rows
    span = bias_ref.shape[-1]

    @pl.when(pl.program_id(0) == 0)
    def _():
        for i, x_ref in enumerate((x0, x1, x2, x3)):
            x = x_ref[...].astype(f32)
            scale = lax.rsqrt(jnp.mean(x * x, axis=-1, keepdims=True) + epsilon)
            place = pl.multiple_of((rank ^ i) * rows, rows)
            normed_ref[0, pl.ds(place, rows), :] = (x * scale * gain_ref[...]).astype(bf16)
        whole = jnp.concatenate([w[...] for w in (wq0, wq1, wk0, wk1, wv0, wv1)], axis=1)
        wide_ref[...] = dot(whole, normed_ref[0], ((0,), (1,)))

    head = qkv_ref.shape[3]
    h = pl.program_id(0)
    lanes = wq0.shape[1]
    place = jnp.where(h < heads - 1, h * head, lanes + lax.rem(rank, 2) * head)
    part = lambda c: pl.ds(pl.multiple_of(c * (lanes + 128) + place, head), head)
    queries = wide_ref[part(0), :] * (head ** -0.5)
    values = wide_ref[part(2), :]
    q_ref[...] = queries.T.astype(bf16)
    v_ref[...] = values.T.astype(bf16)
    qkv_ref[0, 0, 0] = queries.astype(bf16)
    qkv_ref[0, 0, 1] = wide_ref[part(1), :].astype(bf16)
    qkv_ref[0, 0, 2] = values.astype(bf16)
    base_ref[...] = pltpu.roll(
        jnp.broadcast_to(bias_ref[0], (128, span)), 0, axis=1, stride=1, stride_axis=0
    )
    keys = qkv_ref[0, 0, 1]
    values = v_ref[...]
    top = length - 128
    step = 256
    blocks = length // step
    scores_ref[0] = dot(q_ref[0:step, :], keys)
    for b in range(blocks):
        if b + 1 < blocks:
            scores_ref[(b + 1) % 2] = dot(q_ref[(b + 1) * step : (b + 2) * step, :], keys)
        for k in range(0, step, strip):
            row = b * step + k
            place = top - row // 128 * 128
            line = row % 128
            scores = (
                scores_ref[b % 2, k : k + strip, :]
                + base_ref[line : line + strip, place : place + length]
            )
            raised = jnp.exp(scores - jnp.max(scores, axis=1, keepdims=True))
            total = jnp.sum(raised, axis=1, keepdims=True)
            sums_ref[k : k + strip, :] = jnp.broadcast_to(1.0 / total, (strip, 128))
            raised_ref[0, 0, row : row + strip, :] = raised.astype(bf16)
        inverse = sums_ref[...]
        attended = dot(raised_ref[0, 0, b * step : (b + 1) * step, :], values) * inverse[:, :head]
        attended = attended.T
        exact_ref[0, 0, :, b * step : (b + 1) * step] = attended
        out_ref[0, 0, :, b * step : (b + 1) * step] = attended.astype(bf16)
        inverse_ref[0, 0, :, b * step : (b + 1) * step] = inverse.T[:8]
    for i, p_ref in enumerate((p0, p1, p2, p3)):
        p_ref[...] = out_ref[0, 0, :, pl.ds(pl.multiple_of((rank ^ i) * rows, rows), rows)]


def attend(rank, blocks, gain, weights, bias_rows, previous, seq, groups):
    rows, width = blocks[0].shape
    heads, _, span = bias_rows.shape
    head = width // (4 * heads)
    length = 4 * rows
    first = previous is None
    whole = lambda h, r: (0, 0)
    low = 4 * (heads - 1) * head // 128
    lanes = (heads - 1) * head
    in_specs = [pl.BlockSpec((rows, width), whole)] * 4 + [
        pl.BlockSpec((1, width), whole),
        *[pl.BlockSpec((width, lanes), lambda h, r: (0, r[0]))] * 3,
        *[pl.BlockSpec((width, 128), lambda h, r: (0, low + lax.div(r[0], 2)))] * 3,
        pl.BlockSpec((1, 1, span), lambda h, r: (h, 0, 0)),
    ]
    args = list(blocks) + [gain] + list(weights) * 2 + [bias_rows]
    aliases = {}
    if not first:
        aliases = {1 + len(args) + k: k for k in range(6)}
        in_specs = in_specs + [pl.BlockSpec(memory_space=pl.ANY)] * 6
        args = args + list(previous)
    out_shape = [
        jax.ShapeDtypeStruct((groups, length, width), bf16),
        jax.ShapeDtypeStruct((groups, heads, 3, head, length), bf16),
        jax.ShapeDtypeStruct((groups, heads, length, length), bf16),
        jax.ShapeDtypeStruct((groups, heads, 8, length), f32),
        jax.ShapeDtypeStruct((groups, heads, head, length), bf16),
        jax.ShapeDtypeStruct((groups, heads, head, length), f32),
    ] + [jax.ShapeDtypeStruct((heads * head, rows), bf16)] * 4
    out_specs = [
        pl.BlockSpec((1, length, width), lambda h, r: (seq, 0, 0)),
        pl.BlockSpec((1, 1, 3, head, length), lambda h, r: (seq, h, 0, 0, 0)),
        pl.BlockSpec((1, 1, length, length), lambda h, r: (seq, h, 0, 0)),
        pl.BlockSpec((1, 1, 8, length), lambda h, r: (seq, h, 0, 0)),
        pl.BlockSpec((1, 1, head, length), lambda h, r: (seq, h, 0, 0)),
        pl.BlockSpec((1, 1, head, length), lambda h, r: (seq, h, 0, 0)),
    ] + [pl.BlockSpec((head, rows), lambda h, r: (h, 0))] * 4
    outs = pl.pallas_call(
        functools.partial(forward_kernel, rows=rows, heads=heads, first=first),
        grid_spec=pltpu.PrefetchScalarGridSpec(
            num_scalar_prefetch=1,
            grid=(heads,),
            in_specs=in_specs,
            out_specs=out_specs,
            scratch_shapes=[
                pltpu.VMEM((length, head), bf16),
                pltpu.VMEM((length, head), bf16),
                pltpu.VMEM((128, span), f32),
                pltpu.VMEM((3 * (lanes + 128), length), f32),
                pltpu.VMEM((2, 256, length), f32),
                pltpu.VMEM((256, 128), f32),
            ],
        ),
        out_shape=out_shape,
        input_output_aliases=aliases,
        compiler_params=pltpu.CompilerParams(vmem_limit_bytes=vmem_bytes),
        cost_estimate=pl.CostEstimate(
            flops=(18 if first else 18) * heads * length * length * 256, bytes_accessed=8_000_000, transcendentals=0
        ),
        name="attention_forward",
    )(rank, *args)
    return outs[:6], outs[6:]


def backward_kernel(
    rank_ref, g0, g1, g2, g3, qkv_ref, raised_ref, inverse_ref, out_ref, normed_ref,
    d0, d1, d2, d3, weight_grad_ref, bias_ref,
    grad_ref, left_ref, right_ref, key_ref, scores_ref, packed_ref, total_ref, offsets_ref, inner_ref, *, rows
):
    rank = rank_ref[0]
    length = 4 * rows
    head = grad_ref.shape[0]
    step_id = pl.program_id(0)
    h = pl.program_id(1)
    for i, g_ref in enumerate((g0, g1, g2, g3)):
        grad_ref[:, pl.ds(pl.multiple_of((rank ^ i) * rows, rows), rows)] = g_ref[...].astype(f32)
    scaled = grad_ref[...] * inverse_ref[0, 0, 0:1, :]
    scaled_low = scaled.astype(bf16)
    shift = jnp.sum(scaled_low.astype(f32) * out_ref[0, 0], axis=0, keepdims=True)
    high = shift.astype(bf16).astype(f32)
    tail = jnp.concatenate(
        [high, shift - high, jnp.zeros((128 - head - 2, length), f32)], axis=0
    )
    left_ref[...] = jnp.concatenate([scaled_low.astype(f32), tail], axis=0).T.astype(bf16)
    right_ref[0:head, :] = qkv_ref[0, 0, 2]
    right_ref[head:, :] = jnp.where(
        lax.broadcasted_iota(jnp.int32, (128 - head, length), 0) < 2, -1.0, 0.0
    ).astype(bf16)
    key_ref[...] = qkv_ref[0, 0, 1].astype(f32).T.astype(bf16)

    @pl.when(step_id == 0)
    def _():
        offsets_ref[h] = jnp.zeros(offsets_ref.shape[1:], f32)
        total_ref[h] = jnp.zeros(total_ref.shape[1:], f32)

    top = length - 128
    step = 256
    blocks = length // step
    inner_ref[0] = dot(left_ref[0:step, :], right_ref[...])
    for b in range(blocks):
        if b + 1 < blocks:
            inner_ref[(b + 1) % 2] = dot(left_ref[(b + 1) * step : (b + 2) * step, :], right_ref[...])
        for k in range(0, step, strip):
            row = b * step + k
            place = top - row // 128 * 128
            line = row % 128
            grads = raised_ref[0, 0, row : row + strip, :].astype(f32) * inner_ref[b % 2, k : k + strip, :]
            offsets_ref[h, line : line + strip, place : place + length] += grads
            scores_ref[row : row + strip, :] = grads.astype(bf16)
    packed_ref[0:head, :] = (dot(scores_ref[...], key_ref[...]) * (head ** -0.5)).T.astype(bf16)
    packed_ref[head : 2 * head, :] = dot(qkv_ref[0, 0, 0], scores_ref[...]).astype(bf16)
    packed_ref[2 * head :, :] = dot(scaled_low, raised_ref[0, 0]).astype(bf16)
    for i, d_ref in enumerate((d0, d1, d2, d3)):
        d_ref[...] = packed_ref[:, pl.ds(pl.multiple_of((rank ^ i) * rows, rows), rows)]
    total_ref[h] += dot(packed_ref[...], normed_ref[0])

    @pl.when(step_id == pl.num_programs(0) - 1)
    def _():
        weight_grad_ref[pl.ds(pl.multiple_of(h * 3 * head, head), 3 * head), :] = total_ref[
            h
        ].astype(bf16)
        span = offsets_ref.shape[2]
        folded = offsets_ref[h]
        half = 64
        while half >= 8:
            folded = folded[:half] + pltpu.roll(folded[half : 2 * half], span - half, axis=1)
            half //= 2
        bias_ref[h] = folded


def attend_back(rank, grads, saved, first, count):
    normed, qkv, raised, inverse, _, out = saved
    groups, length, width = normed.shape
    head = qkv.shape[3]
    rows = length // 4
    span = 2 * length
    per_head = lambda *dims: pl.BlockSpec((1, 1) + dims, lambda s, h, r: (s, first + h) + (0,) * len(dims))
    whole = lambda *dims: pl.BlockSpec(dims, lambda s, h, r: (0,) * len(dims))
    outs = pl.pallas_call(
        functools.partial(backward_kernel, rows=rows),
        grid_spec=pltpu.PrefetchScalarGridSpec(
            num_scalar_prefetch=1,
            grid=(groups, count),
            in_specs=[pl.BlockSpec((head, rows), lambda s, h, r: (h, s))] * 4
            + [
                per_head(3, head, length),
                per_head(length, length),
                per_head(8, length),
                per_head(head, length),
                pl.BlockSpec((1, length, width), lambda s, h, r: (s, 0, 0)),
            ],
            out_specs=[pl.BlockSpec((3 * head, rows), lambda s, h, r: (h, s))] * 4
            + [whole(3 * head * count, width), whole(count, 8, span)],
            scratch_shapes=[
                pltpu.VMEM((head, length), f32),
                pltpu.VMEM((length, 128), bf16),
                pltpu.VMEM((128, length), bf16),
                pltpu.VMEM((length, head), bf16),
                pltpu.VMEM((length, length), bf16),
                pltpu.VMEM((3 * head, length), bf16),
                pltpu.VMEM((count, 3 * head, width), f32),
                pltpu.VMEM((count, 128, span), f32),
                pltpu.VMEM((2, 256, length), f32),
            ],
        ),
        out_shape=[jax.ShapeDtypeStruct((3 * head * count, groups * rows), bf16)] * 4
        + [
            jax.ShapeDtypeStruct((3 * head * count, width), bf16),
            jax.ShapeDtypeStruct((count, 8, span), f32),
        ],
        compiler_params=pltpu.CompilerParams(vmem_limit_bytes=vmem_bytes),
        cost_estimate=pl.CostEstimate(
            flops=11_000_000_000 * count, bytes_accessed=10_000_000 * count, transcendentals=0
        ),
        name="attention_backward",
    )(rank, *grads, qkv, raised, inverse, out, normed)
    return outs[:4], outs[4], outs[5]


def out_weight_kernel(
    rank_ref, b0, b1, b2, b3, out_ref, last_ref, extra_ref, bucket_ref, *rest
):
    bias_refs, (grad_ref, whole_ref, total_ref) = rest[:-3], rest[-3:]
    rank = rank_ref[0]
    rows, width = b0.shape
    count = last_ref.shape[0]
    for i, b_ref in enumerate((b0, b1, b2, b3)):
        whole_ref[pl.ds(pl.multiple_of((rank ^ i) * rows, rows), rows), :] = b_ref[...]
    part = dot(out_ref[0].reshape(count, 4 * rows), whole_ref[...])

    @pl.when(pl.program_id(0) == 0)
    def _():
        total_ref[...] = part

    @pl.when(pl.program_id(0) > 0)
    def _():
        total_ref[...] += part

    @pl.when(pl.program_id(0) == pl.num_programs(0) - 1)
    def _():
        grad_ref[:count, :width] = last_ref[...]
        grad_ref[count:, :width] = total_ref[...].astype(bf16)
        place = extra_ref.shape[0]
        grad_ref[:place, width:] = extra_ref[...].astype(bf16)
        grad_ref[place:, width:] = jnp.zeros((2 * count - place, extra_ref.shape[1]), bf16)
        for bias_ref in bias_refs:
            for h in range(bias_ref.shape[0]):
                folded, half = bias_ref[h], 4
                while half >= 1:
                    span = folded.shape[1]
                    folded = folded[:half] + pltpu.roll(folded[half : 2 * half], span - half, axis=1)
                    half //= 2
                folded = jnp.broadcast_to(folded, (16, span))
                high = folded.astype(bf16)
                low = (folded - high.astype(f32)).astype(bf16)
                buckets = dot(high, bucket_ref[...], ((1,), (1,))) + dot(
                    low, bucket_ref[...], ((1,), (1,))
                )
                grad_ref[place : place + 16, width : width + 128] = buckets.astype(bf16)
                place += 16


def out_weight_rows(rank, blocks, out, last, extra, bucket_hot, biases):
    groups, heads, head, length = out.shape
    count, width = last.shape
    rows = length // 4
    lanes = width + extra.shape[1]
    whole = lambda v: pl.BlockSpec(v.shape, lambda s, r: (0,) * v.ndim)
    return pl.pallas_call(
        out_weight_kernel,
        grid_spec=pltpu.PrefetchScalarGridSpec(
            num_scalar_prefetch=1,
            grid=(groups,),
            in_specs=[pl.BlockSpec((rows, width), lambda s, r: (s, 0))] * 4
            + [pl.BlockSpec((1, heads, head, length), lambda s, r: (s, 0, 0, 0))]
            + [whole(v) for v in [last, extra, bucket_hot] + biases],
            out_specs=pl.BlockSpec((2 * count, lanes), lambda s, r: (0, 0)),
            scratch_shapes=[pltpu.VMEM((length, width), bf16), pltpu.VMEM((count, width), f32)],
        ),
        out_shape=jax.ShapeDtypeStruct((2 * count, lanes), bf16),
        compiler_params=pltpu.CompilerParams(vmem_limit_bytes=vmem_bytes),
        cost_estimate=pl.CostEstimate(
            flops=300_000_000, bytes_accessed=300_000, transcendentals=0
        ),
        name="out_weight_rows",
    )(rank, *blocks, out, last, extra, bucket_hot, *biases)


def head_place(rank, h, heads):
    return rank * (heads - 1) + h if h < heads - 1 else 4 * (heads - 1) + rank


def turn_kernel(rank_ref, *refs, heads, part):
    blocks, weight_refs, before_ref, gain_ref, rest = refs[0:4], refs[4:7], refs[7], refs[8], refs[9:]
    rank = rank_ref[0]
    if part:
        q_ref, k_ref, v_ref, norm_ref, out_ref, router_ref, norm2_ref, bias_ref = rest[3:-2]
        gathered_ref, total_ref = rest[-2:]
    else:
        q_ref, k_ref, v_ref, norm_ref, gathered_ref, total_ref = rest
    count = heads - 1 if part == 0 else 1
    width = q_ref.shape[0]
    head = width // (4 * heads)

    @pl.when(pl.program_id(0) == 0)
    def _():
        total_ref[...] = jnp.zeros_like(total_ref)
        for i in range(4):
            for h in range(count):
                place = pl.multiple_of(((rank ^ i) * count + h) * head, head)
                for c in range(3):
                    gathered_ref[c, pl.ds(place, head), :] = blocks[i][
                        (3 * h + c) * head : (3 * h + c + 1) * head, :width
                    ].astype(f32)
            if part:
                for h in range(heads):
                    place = head_place(rank ^ i, h, heads)
                    start = (3 + h) * head
                    out_ref[pl.ds(pl.multiple_of(place * head, head), head), :] = blocks[i][
                        start : start + head, :width
                    ].astype(f32)
                    start = 2 * 3 * head - (heads - h) * 16
                    bias = blocks[i][start : start + 16, width : width + 128].astype(f32)
                    bias_ref[pl.ds(place, 1), :] = bias[:1, : bias_ref.shape[1]]
        if part:
            experts = router_ref.shape[0]
            spare = 2 * 3 * head - 16 * heads
            total = blocks[0][:, width:].astype(f32)
            for i in range(1, 4):
                total += blocks[i][:, width:].astype(f32)
            for j, (row, lane) in enumerate(extra_places(experts, width, spare)):
                here = total[row : row + experts + 8, lane : lane + 128]
                router_ref[:, j * 128 : (j + 1) * 128] = here[:experts]
                norm2_ref[j * 128 : (j + 1) * 128] = here[experts : experts + 1].reshape(128)

    place = pl.multiple_of(pl.program_id(0) * 128, 128)
    for c, grad_ref in enumerate((q_ref, k_ref, v_ref)):
        grads = gathered_ref[c, pl.ds(place, 128), :].T
        grad_ref[...] = grads
        total_ref[...] += grads * weight_refs[c][...].astype(f32)

    @pl.when(pl.program_id(0) == pl.num_programs(0) - 1)
    def _():
        total = jnp.sum(total_ref[...].T, axis=0, keepdims=True) / gain_ref[...]
        norm_ref[...] = (before_ref[...] + total).reshape(norm_ref.shape)


def turn(rank, blocks, weights, gain, previous, heads, part, experts=0, buckets=0):
    width = weights[0].shape[0]
    head = width // (4 * heads)
    count = heads - 1 if part == 0 else 1
    first = 0 if part == 0 else 4 * (heads - 1) * head // 128
    column = pl.BlockSpec((width, 128), lambda s, r: (0, first + s))
    whole = lambda *dims: pl.BlockSpec(dims, lambda s, r: (0,) * len(dims))
    in_specs = [whole(*b.shape) for b in blocks]
    in_specs += [column] * 3 + [whole(1, width)] * 2
    before = jnp.zeros((1, width), f32) if part == 0 else previous[3]
    args = list(blocks) + list(weights) + [before, gain]
    norm = (1, width) if part == 0 else (width,)
    out_shape = [jax.ShapeDtypeStruct((width, width), f32)] * 3
    out_shape += [jax.ShapeDtypeStruct(norm, f32)]
    out_specs = [column] * 3 + [whole(*norm)]
    aliases = {}
    if part:
        aliases = {1 + len(args) + k: k for k in range(3)}
        in_specs += [pl.BlockSpec(memory_space=pl.ANY)] * 3
        args += list(previous[:3])
        for dims in ((width, width), (experts, width), (width,), (4 * heads, buckets)):
            out_shape.append(jax.ShapeDtypeStruct(dims, f32))
            out_specs.append(whole(*dims))
    return pl.pallas_call(
        functools.partial(turn_kernel, heads=heads, part=part),
        grid_spec=pltpu.PrefetchScalarGridSpec(
            num_scalar_prefetch=1,
            grid=(4 * count * head // 128,),
            in_specs=in_specs,
            out_specs=out_specs,
            scratch_shapes=[
                pltpu.VMEM((3, 4 * count * head, width), f32),
                pltpu.VMEM((width, 128), f32),
            ],
        ),
        out_shape=out_shape,
        input_output_aliases=aliases,
        compiler_params=pltpu.CompilerParams(vmem_limit_bytes=vmem_bytes),
        cost_estimate=pl.CostEstimate(
            flops=3_000_000_000 * count, bytes_accessed=3_000_000 * count, transcendentals=0
        ),
        name="weight_gradient_turn",
    )(rank, *args)


def input_kernel(rank_ref, *refs, heads):
    pieces, weight_refs = refs[:8], refs[8:11]
    x_ref, grad_ref, gain_ref, out_ref, gathered_ref = refs[11:]
    rank = rank_ref[0]
    head = pieces[4].shape[0] // 3
    for i in range(4):
        for h in range(heads):
            place = pl.multiple_of(head_place(rank ^ i, h, heads) * head, head)
            source, k = (pieces[i], h) if h < heads - 1 else (pieces[4 + i], 0)
            for c in range(3):
                gathered_ref[c, pl.ds(place, head), :] = source[
                    (3 * k + c) * head : (3 * k + c + 1) * head, :
                ]
    total = dot(gathered_ref[0], weight_refs[0][...], ((0,), (1,)))
    total += dot(gathered_ref[1], weight_refs[1][...], ((0,), (1,)))
    total += dot(gathered_ref[2], weight_refs[2][...], ((0,), (1,)))
    x = x_ref[...].astype(f32)
    scale = lax.rsqrt(jnp.mean(x * x, axis=-1, keepdims=True) + epsilon)
    unit = x * scale
    scaled = total * gain_ref[...]
    inner_mean = jnp.mean(scaled * unit, axis=-1, keepdims=True)
    out_ref[...] = grad_ref[...] + scale * (scaled - unit * inner_mean)


def input_gradient(rank, pieces, weights, inputs, residual_grad, gain, heads):
    tokens, width = inputs.shape
    half = tokens // 2
    whole = lambda s, r: (0, 0)
    part = pl.BlockSpec((half, width), lambda s, r: (s, 0))
    return pl.pallas_call(
        functools.partial(input_kernel, heads=heads),
        grid_spec=pltpu.PrefetchScalarGridSpec(
            num_scalar_prefetch=1,
            grid=(2,),
            in_specs=[pl.BlockSpec((p.shape[0], half), lambda s, r: (0, s)) for p in pieces]
            + [pl.BlockSpec((width, width), whole)] * 3
            + [part, part, pl.BlockSpec((1, width), whole)],
            out_specs=part,
            scratch_shapes=[pltpu.VMEM((3, width, half), bf16)],
        ),
        out_shape=jax.ShapeDtypeStruct((tokens, width), f32),
        compiler_params=pltpu.CompilerParams(vmem_limit_bytes=vmem_bytes),
        cost_estimate=pl.CostEstimate(
            flops=6_000_000_000, bytes_accessed=9_000_000, transcendentals=0
        ),
        name="input_gradient",
    )(rank, *pieces, *weights, inputs, residual_grad, gain)


def expert_part(expert, rows, grads, into, out_of, router, experts):
    logits = dot(rows, router)
    lanes = lax.broadcasted_iota(jnp.int32, logits.shape, 1)
    logits = jnp.where(lanes < experts, logits, -1e30)
    raised = jnp.exp(logits - jnp.max(logits, axis=1, keepdims=True))
    picked = jnp.sum(jnp.where(lanes == expert, raised, 0.0), axis=1, keepdims=True)
    gate = picked / jnp.sum(raised, axis=1, keepdims=True)

    before = dot(rows, into)
    hidden = dot(grads, out_of, ((1,), (1,)))
    square = before * before
    bend = 0.5 + 0.5 * jnp.tanh(before * (0.7978845608 + (0.7978845608 * 0.044715) * square))
    active = before * bend
    slope = 2.0 * 0.7978845608 + (6.0 * 0.7978845608 * 0.044715) * square
    back = hidden * (bend + active * (1.0 - bend) * slope)
    gate_part = jnp.sum(active * hidden, axis=1, keepdims=True)
    row_part = dot(back.astype(bf16), into, ((1,), (1,))).astype(bf16)
    extra = jnp.where(
        lax.broadcasted_iota(jnp.int32, (rows.shape[0], 128), 1) == 0, gate_part, 0.0
    ).astype(bf16)
    gated = (gate * active).astype(bf16)
    produced = dot(gated, out_of).astype(bf16)
    return row_part, extra, gated, (gate * back).astype(bf16), produced


def expert_kernel(first_ref, *refs, members, experts):
    count = len(members)
    ins, outs = refs[: 6 * count + 1], refs[6 * count + 1 :]
    router_ref = ins[-1]
    for k, e in enumerate(members):
        xa, xb, ga, gb, into_ref, out_of_ref = ins[6 * k : 6 * k + 6]
        rows = jnp.concatenate([xa[...], xb[...]], axis=0)
        grads = jnp.concatenate([ga[...], gb[...]], axis=0)
        row_part, extra, gated, gated_back, produced = expert_part(
            first_ref[0] + e, rows, grads, into_ref[0], out_of_ref[0], router_ref[...], experts
        )
        half, width = xa.shape
        for p in range(2):
            part = slice(p * half, (p + 1) * half)
            d, a, b, y = outs[8 * k + p : 8 * k + 8 : 2]
            d[:, :width] = row_part[part]
            d[:, width:] = extra[part]
            y[...] = produced[part]
            a[...] = gated[part]
            b[...] = gated_back[part]


def run_experts(members, first, rows, grads, into, out_of, router, experts, cost):
    count, width = rows[0][0].shape
    hidden = into.shape[2]
    steps = 2
    half = count // steps
    block = lambda lanes: pl.BlockSpec((half, lanes), lambda s, f: (s, 0))
    shape = lambda lanes: jax.ShapeDtypeStruct((count, lanes), bf16)
    in_specs, args, out_specs, out_shape = [], [], [], []
    for k, e in enumerate(members):
        in_specs += [block(width)] * 2
        in_specs += [block(width)] * 2
        in_specs += [
            pl.BlockSpec((1, width, hidden), functools.partial(lambda e, s, f: (e, 0, 0), e)),
            pl.BlockSpec((1, hidden, width), functools.partial(lambda e, s, f: (e, 0, 0), e)),
        ]
        args += list(rows[k]) + list(grads[k]) + [into, out_of]
        out_specs += [block(width + 128)] * 2 + [block(hidden)] * 4 + [block(width)] * 2
        out_shape += [shape(width + 128)] * 2 + [shape(hidden)] * 4 + [shape(width)] * 2
    outs = pl.pallas_call(
        functools.partial(expert_kernel, members=members, experts=experts),
        grid_spec=pltpu.PrefetchScalarGridSpec(
            num_scalar_prefetch=1,
            grid=(steps,),
            in_specs=in_specs + [pl.BlockSpec(router.shape, lambda s, f: (0, 0))],
            out_specs=out_specs,
        ),
        out_shape=out_shape,
        compiler_params=pltpu.CompilerParams(vmem_limit_bytes=vmem_bytes),
        cost_estimate=pl.CostEstimate(
            flops=cost, bytes_accessed=cost // 1000, transcendentals=0
        ),
        name="experts",
    )(first, *args, router)
    return [[outs[8 * k + 2 * t : 8 * k + 2 * t + 2] for t in range(4)] for k in range(len(members))]


def expert_weight_kernel(*refs, owned):
    into_ref, out_of_ref = refs[-2:]
    whole = lambda parts: jnp.concatenate([p[...] for p in parts], axis=0)
    for e in range(owned):

        @pl.when(pl.program_id(0) == e)
        def _():
            rows, actives, backs, grads = [refs[16 * e + 4 * k : 16 * e + 4 * k + 4] for k in range(4)]
            into_ref[0] = dot(whole(rows), whole(backs), ((0,), (0,)))
            out_of_ref[0] = dot(whole(actives), whole(grads), ((0,), (0,)))


def expert_weight_grads(rows, actives, backs, grads):
    owned = len(rows)
    width, hidden = rows[0][0].shape[1], actives[0][0].shape[1]
    args = []
    for e in range(owned):
        args += list(rows[e]) + list(actives[e]) + list(backs[e]) + list(grads[e])
    whole = lambda v: pl.BlockSpec(v.shape, lambda s: (0, 0))
    return pl.pallas_call(
        functools.partial(expert_weight_kernel, owned=owned),
        grid=(owned,),
        in_specs=[whole(v) for v in args],
        out_specs=[
            pl.BlockSpec((1, width, hidden), lambda s: (s, 0, 0)),
            pl.BlockSpec((1, hidden, width), lambda s: (s, 0, 0)),
        ],
        out_shape=[
            jax.ShapeDtypeStruct((owned, width, hidden), f32),
            jax.ShapeDtypeStruct((owned, hidden, width), f32),
        ],
        compiler_params=pltpu.CompilerParams(vmem_limit_bytes=vmem_bytes),
        cost_estimate=pl.CostEstimate(
            flops=500_000_000, bytes_accessed=500_000, transcendentals=0
        ),
        name="expert_weight_gradients",
    )(*args)


def combine_kernel(
    rank_ref, target_ref, chosen_ref, *refs, owned, experts, spare, heads
):
    rank = rank_ref[0]
    returned = refs[:owned]
    normed_ref, residual_ref, up_ref, router_ref, gain_ref, weight_ref = refs[owned : owned + 6]
    grad_ref, branch_ref = refs[owned + 6 : owned + 8]
    low_refs, last_refs = refs[owned + 8 : owned + 12], refs[owned + 12 : owned + 16]
    extra_ref, turned_ref = refs[owned + 16 :]
    tokens, width = normed_ref.shape
    count = returned[0].shape[0]
    back = jnp.zeros((tokens, width + 128), f32)
    for e in range(owned):
        hot = target_ref[e : e + 1, :] == lax.broadcasted_iota(jnp.int32, (count, tokens), 0)
        back += dot(hot.astype(f32).astype(bf16), returned[e][...], ((0,), (0,)))
    residual = residual_ref[...]
    scale = lax.rsqrt(jnp.mean(residual * residual, axis=-1, keepdims=True) + epsilon)
    unit = residual * scale

    logits = dot(normed_ref[...], router_ref[...])
    lanes = lax.broadcasted_iota(jnp.int32, logits.shape, 1)
    logits = jnp.where(lanes < experts, logits, -1e30)
    raised = jnp.exp(logits - jnp.max(logits, axis=1, keepdims=True))
    probs = raised / jnp.sum(raised, axis=1, keepdims=True)
    hot = (lanes == chosen_ref[...]).astype(f32)
    gate = jnp.sum(probs * hot, axis=1, keepdims=True)
    gate_grad = back[:, width : width + 1]
    logit_grad = (probs * gate_grad * (hot - gate)).astype(bf16)
    normed_grad = dot(logit_grad, router_ref[...], ((1,), (1,))) + gate * back[:, :width]
    scaled = normed_grad * gain_ref[...]
    inner_mean = jnp.mean(scaled * unit, axis=-1, keepdims=True)
    grads = up_ref[...].astype(f32) + scale * (scaled - unit * inner_mean)
    grad_ref[...] = grads
    branch = grads.astype(bf16)
    branch_ref[...] = branch
    turned_ref[...] = dot(weight_ref[...], branch, ((1,), (1,))).astype(bf16)
    head = weight_ref.shape[0] // (4 * heads)
    for i in range(4):
        for h in range(heads):
            place = pl.multiple_of(head_place(rank ^ i, h, heads) * head, head)
            g_ref, k = (low_refs[i], h) if h < heads - 1 else (last_refs[i], 0)
            g_ref[k * head : (k + 1) * head, :] = turned_ref[pl.ds(place, head), :]
    router_part = dot(logit_grad, normed_ref[...], ((0,), (0,)))
    norm_part = jnp.broadcast_to(jnp.sum(normed_grad * unit, axis=0, keepdims=True), (8, width))

    extra = jnp.concatenate([router_part[:experts], norm_part], axis=0)
    places = extra_places(experts, width, spare)

    @pl.when(pl.program_id(0) == 0)
    def _():
        extra_ref[...] = jnp.zeros_like(extra_ref)

    for j, (row, lane) in enumerate(places):
        extra_ref[row : row + experts + 8, lane : lane + 128] += extra[:, j * 128 : (j + 1) * 128]


def extra_places(experts, width, spare):
    count = spare // (experts + 8)
    return [((j % count) * (experts + 8), j // count * 128) for j in range(width // 128)]


def combine(rank, targets, chosen, returned, normed, residual, upstream, router, gain, weights, experts, spare, heads):
    tokens, width = residual.shape
    half = tokens // 2
    owned = len(returned)
    whole = lambda v: pl.BlockSpec(v.shape, lambda s, r: (0, 0))
    part = pl.BlockSpec((half, width), lambda s, r: (s, 0))
    lanes = extra_places(experts, width, spare)[-1][1] + 128
    columns = weights.shape[0] // 4
    head = columns // heads
    outs = pl.pallas_call(
        functools.partial(combine_kernel, owned=owned, experts=experts, spare=spare, heads=heads),
        grid_spec=pltpu.PrefetchScalarGridSpec(
            num_scalar_prefetch=1,
            grid=(2,),
            in_specs=[
                pl.BlockSpec((targets.shape[0], half), lambda s, r: (0, s)),
                pl.BlockSpec((half, 1), lambda s, r: (s, 0)),
            ]
            + [whole(v) for v in returned]
            + [part] * 3
            + [whole(router), whole(gain), whole(weights)],
            out_specs=[part, part]
            + [pl.BlockSpec((columns - head, half), lambda s, r: (0, s))] * 4
            + [pl.BlockSpec((head, half), lambda s, r: (0, s))] * 4
            + [pl.BlockSpec((spare, lanes), lambda s, r: (0, 0))],
            scratch_shapes=[pltpu.VMEM((weights.shape[0], half), bf16)],
        ),
        out_shape=[
            jax.ShapeDtypeStruct((tokens, width), f32),
            jax.ShapeDtypeStruct((tokens, width), bf16),
        ]
        + [jax.ShapeDtypeStruct((columns - head, tokens), bf16)] * 4
        + [jax.ShapeDtypeStruct((head, tokens), bf16)] * 4
        + [jax.ShapeDtypeStruct((spare, lanes), f32)],
        compiler_params=pltpu.CompilerParams(vmem_limit_bytes=vmem_bytes),
        cost_estimate=pl.CostEstimate(
            flops=6_000_000_000, bytes_accessed=12_000_000, transcendentals=0
        ),
        name="combine",
    )(rank, targets, chosen, *returned, normed, residual, upstream, router, gain, weights)
    return outs[0], outs[1], outs[2:6], outs[6:10], outs[10]


def residual_kernel(rank_ref, *refs, heads, owned, first):
    pieces, (target_ref, x_ref, gain_ref, weight_ref) = refs[:4], refs[4:8]
    before, rest = ((), refs[8:]) if first else (refs[8 : 8 + owned], refs[10 + owned :])
    residual_ref, normed_ref = rest[:2]
    sent_refs, turned_ref = rest[2 : 2 + owned], rest[2 + owned]
    rank = rank_ref[0]
    head = weight_ref.shape[0] // (4 * heads)
    for i in range(4):
        for h in range(heads):
            place = pl.multiple_of(head_place(rank ^ i, h, heads) * head, head)
            turned_ref[pl.ds(place, head), :] = pieces[i][h * head : (h + 1) * head, :]

    residual = x_ref[...].astype(f32) + dot(turned_ref[...], weight_ref[...], ((0,), (0,)))
    residual_ref[...] = residual
    scale = lax.rsqrt(jnp.mean(residual * residual, axis=-1, keepdims=True) + epsilon)
    normed = (residual * scale * gain_ref[...]).astype(bf16)
    normed_ref[...] = normed
    for e in range(owned):
        count = sent_refs[e].shape[0]
        hot = target_ref[e : e + 1, :] == lax.broadcasted_iota(
            jnp.int32, (count, normed.shape[0]), 0
        )
        part = dot(hot.astype(f32).astype(bf16), normed)
        if not first:
            part = part + before[e][...].astype(f32)
        sent_refs[e][...] = part.astype(bf16)


def residual_rows(rank, pieces, targets, inputs, gain, weights, slots, owned, heads, seq, previous):
    tokens, width = inputs.shape
    half = tokens // 2
    whole = lambda v: pl.BlockSpec(v.shape, lambda s, r: (0, 0))
    part = pl.BlockSpec((half, width), lambda s, r: (seq, 0))
    args = list(pieces) + [targets, inputs, gain, weights]
    in_specs = [whole(p) for p in pieces] + [
        pl.BlockSpec((targets.shape[0], half), lambda s, r: (0, seq)),
        part,
        whole(gain),
        whole(weights),
    ]
    aliases = {}
    if previous is not None:
        residual, normed, sent = previous
        in_specs += [whole(v) for v in sent] + [pl.BlockSpec(memory_space=pl.ANY)] * 2
        args += list(sent) + [residual, normed]
        aliases = {len(args) - 1: 0, len(args): 1}
    outs = pl.pallas_call(
        functools.partial(residual_kernel, heads=heads, owned=owned, first=previous is None),
        grid_spec=pltpu.PrefetchScalarGridSpec(
            num_scalar_prefetch=1,
            grid=(1,),
            in_specs=in_specs,
            out_specs=[part, part] + [pl.BlockSpec((slots, width), lambda s, r: (0, 0))] * owned,
            scratch_shapes=[pltpu.VMEM((weights.shape[0], half), bf16)],
        ),
        out_shape=[
            jax.ShapeDtypeStruct((tokens, width), f32),
            jax.ShapeDtypeStruct((tokens, width), bf16),
        ]
        + [jax.ShapeDtypeStruct((slots, width), bf16)] * owned,
        input_output_aliases=aliases,
        compiler_params=pltpu.CompilerParams(vmem_limit_bytes=vmem_bytes),
        cost_estimate=pl.CostEstimate(
            flops=4_000_000_000, bytes_accessed=6_000_000, transcendentals=0
        ),
        name="residual_rows",
    )(rank, *args)
    return outs[0], outs[1], outs[2:]


def on_device(
    block_input, norm1_gain, query_weight, key_weight, value_weight, out_weight,
    relative_bucket_bias, norm2_gain, router_weight, expert_in, expert_out,
    expert_index, slot_index, bucket_table, out_grad,
):
    groups, rows, width = block_input.shape
    tokens = groups * rows
    wide_count = lax.axis_size("wide")
    narrow_count = lax.axis_size("narrow")
    experts = router_weight.shape[1]
    owned = expert_in.shape[0]
    capacity = max(2, (5 * tokens + 4 * experts - 1) // (4 * experts))
    buckets, head_count = relative_bucket_bias.shape
    head = width // head_count
    heads = head_count // narrow_count
    columns = heads * head
    score_scale = head ** (-0.5)
    span = bucket_table.shape[0]
    rank = lax.axis_index("narrow")
    wide_rank = lax.axis_index("wide")
    rank_arg = rank.astype(jnp.int32).reshape(1)
    gain_one = norm1_gain.astype(f32).reshape(1, width)
    gain_two = norm2_gain.astype(f32)

    first_blocks = gather_narrow(block_input[0])

    upstream_low = out_grad.reshape(tokens, width)
    chosen = expert_index.reshape(tokens)
    placed = slot_index.reshape(tokens)
    half = wide_count * capacity
    slots = owned * half
    owner_slot = (chosen // owned) * capacity + placed
    target = jnp.where(placed < capacity, chosen * capacity + placed, -1)
    dispatch = (target[None, :] == jnp.arange(slots, dtype=jnp.int32)[:, None]).astype(bf16)

    everyone = list(range(owned))
    targets = jnp.stack(
        [
            jnp.where((placed < capacity) & (chosen % owned == e), owner_slot, -1)
            for e in everyone
        ]
    )
    targets = jnp.pad(targets, ((0, -owned % 8), (0, 0)), constant_values=-1)

    grad_rows = dot(dispatch, upstream_low).astype(bf16)
    grad_rows = to_owners(grad_rows.reshape(wide_count, owned, capacity, width))

    table_turned = jnp.roll(bucket_table[::-1], -127)
    bucket_hot = (
        table_turned[None, :] == jnp.arange(128, dtype=jnp.int32)[:, None]
    ).astype(bf16)
    bias_turned = relative_bucket_bias.T
    own_bias = jnp.concatenate(
        [
            lax.dynamic_slice_in_dim(bias_turned, rank * (heads - 1), heads - 1, axis=0),
            lax.dynamic_slice_in_dim(bias_turned, narrow_count * (heads - 1) + rank, 1, axis=0),
        ],
        axis=0,
    )
    bias_rows = dot(own_bias, bucket_hot[:buckets]).reshape(heads, 1, span)

    weights = (query_weight, key_weight, value_weight)
    saved = None
    pieces = []
    blocks = first_blocks
    for s in range(groups):
        if s:
            (block,) = tie([block_input[s]], blocks[2])
            blocks = gather_narrow(block, piece[0])
        saved, piece = attend(rank_arg, blocks, gain_one, weights, bias_rows, saved, s, groups)
        pieces.append(exchange_narrow(piece))

    grad_rows = [grad_rows[:, e].reshape(half, width) for e in everyone]
    first_grads = gather_narrow(grad_rows[0])
    rest_grads = [gather_narrow(v) for v in tie(grad_rows[1:], *pieces[-1])]
    grad_rows = [first_grads] + rest_grads
    lanes = -(-experts // 128) * 128
    router_wide = jnp.pad(router_weight, ((0, 0), (0, lanes - experts)))
    inputs = block_input.reshape(tokens, width)
    after_rows = None
    for s in range(groups):
        after_rows = residual_rows(
            rank_arg,
            tie(pieces[s], saved[3], *([first_grads[2], router_wide] if s else [])),
            targets,
            inputs,
            gain_two.reshape(1, width),
            out_weight,
            half,
            owned,
            heads,
            s,
            after_rows,
        )
    residual, normed_two, sent = after_rows
    sent = list(sent[:1]) + tie(sent[1:], *[v[2] for v in rest_grads])
    own = [to_owners(v.reshape(wide_count, capacity, width)).reshape(half, width) for v in sent]
    first_expert = (wide_rank * owned).astype(jnp.int32).reshape(1)

    def experts_on(e, rows_in, grads_in, cost=8_500_000_000):
        return run_experts(
            [e], first_expert, [rows_in], [grads_in], expert_in, expert_out, router_wide, experts, cost
        )[0]

    near, far, returned, expert_rows = [], [], [], []
    holds = [first_grads[2]] + [v[2] for v in rest_grads]
    whole = ()
    for e in everyone:
        if e:
            own[e:] = tie(own[e:], near[-1][0][0])
        near_rows = tie([own[e], swap(own[e], "narrow", 1)], *holds)
        across = swap(own[e], "narrow", 2)
        near.append(experts_on(e, near_rows, grad_rows[e][:2], 3_000_000_000))
        (there,) = tie([across], near[e][0][0])
        far_rows = tie([there, swap(there, "narrow", 1)], *([crossing] if e else []))
        far.append(experts_on(e, far_rows, grad_rows[e][2:], 500_000_000))
        expert_rows.append(near_rows + far_rows)
        begun = scatter_begin(tie(list(near[e][0]) + list(far[e][0]), *whole))
        crossing = begun[2]
        holds = [far[e][0][0]]
        whole = [scatter_end(*begun)]
        returned.append(to_owners(whole[0].reshape(wide_count, capacity, -1)).reshape(half, -1))
    both = lambda k: [
        tie(list(near[e][k]) + list(far[e][k]), *whole, *returned[:-1]) for e in everyone
    ]
    in_grads, out_grads = expert_weight_grads(expert_rows, both(1), both(2), grad_rows)
    produced = [tie(list(near[e][3]) + list(far[e][3]), *whole) for e in everyone]
    produced = [scatter_begin(v) for v in produced]
    produced = [(own, one, swap(crossing, "narrow", 2)) for own, one, crossing in produced]
    returned = tie(returned, in_grads, out_grads, *[v[2] for v in produced])

    spare = 2 * columns - 16 * heads
    residual_grad, branch_grad, own_grads, last_grads, extra = combine(
        rank_arg,
        targets,
        chosen[:, None],
        returned,
        normed_two,
        residual,
        upstream_low,
        router_wide,
        gain_two.reshape(1, width),
        out_weight,
        experts,
        spare,
        heads,
    )
    grads = exchange_narrow(own_grads)
    last_grads = exchange_narrow(tie(last_grads, grads[2]))
    outs_sum = [add_three(*v) for v in produced]
    fetched = to_owners(
        jnp.stack([o.reshape(wide_count, capacity, width) for o in outs_sum], axis=1)
    ).reshape(slots, width)
    branch_later = tie([branch_grad], grads[2])[0]
    branch = gather_narrow(branch_later)
    low_pieces, early, low_bias = attend_back(rank_arg, grads, saved, 0, heads - 1)
    low_pieces = exchange_narrow(low_pieces)
    early = wide_parts(tie([early], branch[2], fetched)[0])
    last_pieces, late, last_bias = attend_back(rank_arg, last_grads, saved, heads - 1, 1)
    last_pieces = exchange_narrow(last_pieces)
    late = out_weight_rows(
        rank_arg, tie(branch, late, low_pieces[1], low_pieces[2]), saved[4], late, extra, bucket_hot, [low_bias, last_bias]
    )
    (early,) = tie([early], late)
    late = wide_parts(tie([late], early)[0])
    early = doubled(early, *last_pieces)
    late = wide_whole(late)

    near_rows, far_rows = [swap(early, "narrow", i) for i in (1, 2)]
    input_grad = input_gradient(
        rank_arg,
        tie(low_pieces + last_pieces, near_rows),
        weights,
        inputs,
        residual_grad,
        gain_one,
        heads,
    )
    (far_rows,) = tie([far_rows], input_grad)
    early = [early, near_rows, far_rows, swap(far_rows, "narrow", 1)]
    turned = turn(rank_arg, early, weights, gain_one, None, heads, 0)
    near_rows, far_rows = [swap(late, "narrow", i) for i in (1, 2)]
    fetched = tie([fetched], near_rows)[0]
    block_out = (residual + dot(dispatch, fetched, ((0,), (0,)))).astype(bf16)
    (far_rows,) = tie([far_rows], turned[3], block_out)
    late = [late, near_rows, far_rows, swap(far_rows, "narrow", 1)]
    query_grad, key_grad, value_grad, norm1_grad, out_weight_grad, router_grad, norm2_grad, biases = turn(
        rank_arg, late, weights, gain_one, turned, heads, 1, experts, buckets
    )

    return (
        block_out.reshape(groups, rows, width),
        input_grad.reshape(groups, rows, width),
        norm1_grad,
        query_grad,
        key_grad,
        value_grad,
        out_weight_grad,
        biases.T,
        norm2_grad,
        router_grad.T,
        in_grads,
        out_grads,
    )


def solution(mesh):
    rows = P("wide", "narrow", None)
    into, out_of = P("wide", None, "narrow"), P("wide", "narrow", None)
    return jax.shard_map(
        on_device,
        mesh=mesh,
        in_specs=(rows,) + (P(),) * 8 + (into, out_of, P("wide", "narrow"), P("wide", "narrow"), P(), rows),
        out_specs=(rows, rows) + (P(),) * 8 + (into, out_of),
        check_vma=False,
    )
```
